256 devices in a mesh: dp: 8 (over y, core), mp: 32 (over x, z).
Axes of the slice: x: 4, y: 4, z: 8, core: 2. Of those that a mesh axis runs over, the one named last changes fastest.
Arguments:
- acts: bfloat16 [8192, 4096], P('dp', 'mp'), may hold values from -6 to 6
- grad_out: bfloat16 [8192, 14336], P('dp', 'mp'), may hold values from -0.29882812 to 0.29882812
- error_buffer: bfloat16 [32768, 14336], P('dp', 'mp'), may hold values from -6 to 6
- q_prev: float32 [32, 14336], P(None, 'mp'), may hold values from -0.046875 to 0.046875
- weight: float32 [4096, 14336], P('dp', 'mp'), may hold values from -0.12 to 0.12
- moment1: float32 [4096, 14336], P('dp', 'mp'), may hold values from -0.3 to 0.3
- moment2: float32 [4096, 14336], P('dp', 'mp'), may hold values from 1e-05 to 0.001
Outputs:
- new_weight: float32 [4096, 14336], P('dp', 'mp')
- new_moment1: float32 [4096, 14336], P('dp', 'mp')
- new_moment2: float32 [4096, 14336], P('dp', 'mp')
- new_error: bfloat16 [32768, 14336], P('dp', 'mp')
- q_new: float32 [32, 14336], P(None, 'mp')
The draws below stay inside these ranges and needn't reach their ends.
All inputs are finite; a program needn't handle non-finite values.
Results may differ from the reference program's by a relative error of at most 0.001.
Values may be sent and summed in bfloat16 or wider, within the bound.
No kernel may reach another device: no remote copies, remote signals or barrier semaphores. Data moves between devices by JAX's collectives and lax.ppermute only.
A program may use at most 64 MiB of HBM per device.

```python
import math
import jax
import jax.numpy as jnp
from jax import lax

D = 4096
FF = 14336
R = 32
TOKENS = 8192
ROWS_ALL = 32768
N_DP = 8


def block_levels(rng, extent, pieces, low, largest):
    factor_of, own = 1.0, jax.random.fold_in(rng, 6)
    for dim, blocks in pieces:
        steps = jnp.exp(jax.random.uniform(jax.random.fold_in(own, dim), (blocks,), jnp.float32, low / len(pieces), largest / len(pieces)))
        factor_of = factor_of * jnp.repeat(steps, extent[dim] // blocks).reshape([-1 if axis == dim else 1 for axis in range(len(extent))])
    return factor_of


def noise(key, shape, deviation, most, split=(), held_as=jnp.bfloat16):
    gain = block_levels(key, shape, split, -0.22, 0.18) if split else 1.0
    array = jax.random.normal(key, shape, jnp.float32) * deviation * gain
    return jnp.minimum(jnp.maximum(array, -most), most).astype(held_as)


def setup_inputs(seed: int = 0) -> dict:
    streams_of = jax.random.split(jax.random.key(seed), 8)
    return {
        "acts": noise(streams_of[0], (TOKENS, D), 1.0, 6.0, ((0, 8), (1, 32))),
        "grad_out": noise(streams_of[1], (TOKENS, FF), 0.05, 0.29882812, ((0, 8), (1, 32))),
        "error_buffer": noise(streams_of[2], (ROWS_ALL, FF), 1.0, 6.0, ((0, 8), (1, 32))),
        "q_prev": noise(streams_of[3], (R, FF), FF ** -0.5, 0.046875, ((1, 32),), jnp.float32),
        "weight": noise(streams_of[4], (D, FF), 0.02, 0.12, ((0, 8), (1, 32)), jnp.float32),
        "moment1": noise(streams_of[5], (D, FF), 0.05, 0.3, ((0, 8), (1, 32)), jnp.float32),
        "moment2": jnp.clip(jnp.exp(math.log(0.001) - 4.6051703 * jax.random.uniform(streams_of[6], (D, FF), jnp.float32) ** block_levels(streams_of[6], (D, FF), ((0, 8), (1, 32)), -0.2, 0.2)), 9.999999747378752e-06, 0.001),
    }


ortho_eps = 1e-08
adam_eps = 1e-08
beta_one = 0.9
beta_two = 0.95
learn_rate = 0.01
corr_one = 1.0 - 0.9 ** 10
corr_two = 1.0 - 0.95 ** 10

def orthonormal_rows(panel):
    count = panel.shape[0]
    order = jnp.arange(count, dtype=jnp.int32)

    def visit(index, panel):
        row = lax.dynamic_slice_in_dim(panel, index, 1, 0)
        row = row / (jnp.sqrt(jnp.sum(row * row)) + ortho_eps)
        panel = lax.dynamic_update_slice_in_dim(panel, row, index, 0)
        inner = jnp.dot(panel, row[0], precision=lax.Precision.HIGHEST)
        later = (order > index).astype(panel.dtype)
        return panel - (inner * later)[:, None] * row
    return lax.fori_loop(0, count, visit, panel)

def reference(acts, grad_out, error_buffer, q_prev, weight, moment1, moment2):
    tok = acts.shape[0] // N_DP
    fields = []
    panel = jnp.zeros((R, D), jnp.float32)
    for replica in range(N_DP):
        inputs = acts[replica * tok:(replica + 1) * tok]
        outgrad = grad_out[replica * tok:(replica + 1) * tok]
        grad = lax.dot_general(inputs, outgrad, (((0,), (0,)), ((), ())), preferred_element_type=jnp.float32)
        field = grad + error_buffer[replica * D:(replica + 1) * D].astype(jnp.float32)
        fields.append(field)
        panel = panel + lax.dot_general(q_prev, field, (((1,), (1,)), ((), ())), precision=lax.Precision.HIGHEST)
    basis = orthonormal_rows(panel / N_DP)
    q_new = jnp.zeros((R, FF), jnp.float32)
    for field in fields:
        q_new = q_new + jnp.dot(basis, field, precision=lax.Precision.HIGHEST)
    q_new = q_new / N_DP
    approx = lax.dot_general(basis, q_new, (((0,), (0,)), ((), ())), precision=lax.Precision.HIGHEST)
    new_error = jnp.concatenate([(field - approx).astype(jnp.bfloat16) for field in fields], axis=0)
    new_moment1 = beta_one * moment1 + (1.0 - beta_one) * approx
    new_moment2 = beta_two * moment2 + (1.0 - beta_two) * approx * approx
    new_weight = weight - learn_rate * (new_moment1 / corr_one) / (jnp.sqrt(new_moment2 / corr_two) + adam_eps)
    return (new_weight, new_moment1, new_moment2, new_error, q_new)
```

```python
import functools

import jax
import jax.numpy as jnp
from jax import lax
from jax.experimental import pallas as pl
from jax.experimental.pallas import tpu as pltpu
from jax.sharding import PartitionSpec as P

ortho_eps = 1e-08
adam_eps = 1e-08
beta_one = 0.9
beta_two = 0.95
learn_rate = 0.01
corr_one = 1.0 - 0.9**10
corr_two = 1.0 - 0.95**10

NX, NZ, NDP = 4, 8, 8
F32, BF16 = jnp.float32, jnp.bfloat16
MIB = 1 << 20
SMEM = pl.BlockSpec(memory_space=pltpu.SMEM)
VMEM = pl.BlockSpec(memory_space=pltpu.VMEM)


def split3(value):
    hi = value.astype(BF16)
    rest = value - hi.astype(F32)
    mid = rest.astype(BF16)
    lo = (rest - mid.astype(F32)).astype(BF16)
    return jnp.concatenate([hi, mid, lo], axis=0)


def fold3(stacked):
    rows = stacked.shape[0] // 3
    return stacked[:rows] + (stacked[rows : 2 * rows] + stacked[2 * rows :])


def dot_nn(a, b):
    return lax.dot_general(a, b, (((1,), (0,)), ((), ())), preferred_element_type=F32)


def dot_nt(a, b):
    return lax.dot_general(a, b, (((1,), (1,)), ((), ())), preferred_element_type=F32)


def dot_tn(a, b):
    return lax.dot_general(a, b, (((0,), (0,)), ((), ())), preferred_element_type=F32)


def token_kernel(z_ref, q_ref, gt_ref, *refs):
    outs, parts = refs[:NZ], refs[NZ]
    total = fold3(dot_nn(split3(q_ref[...]), gt_ref[...]))
    width = total.shape[1] // NZ
    for block in range(NZ):
        parts[block] = total[:, block * width : (block + 1) * width]
    for shift in range(NZ):
        outs[shift][...] = parts[lax.rem(z_ref[0] + shift, NZ)]


def error_kernel(x_ref, q_ref, et_ref, *refs):
    outs, parts = refs[:NX], refs[NX]
    split = split3(q_ref[...])
    width = et_ref.shape[1] // NX
    for block in range(NX):
        parts[block] = fold3(dot_nn(split, et_ref[:, block * width : (block + 1) * width]))
    for shift in range(NX):
        outs[shift][...] = parts[lax.rem(x_ref[0] + shift, NX)]


def split_sum_kernel(z_ref, *refs):
    ins, outs, parts = refs[:NX], refs[NX : NX + NZ], refs[NX + NZ]
    total = (ins[0][...] + ins[1][...]) + (ins[2][...] + ins[3][...])
    width = total.shape[1] // NZ
    for block in range(NZ):
        parts[block] = total[:, block * width : (block + 1) * width]
    for shift in range(NZ):
        outs[shift][...] = parts[lax.rem(z_ref[0] + shift, NZ)]


def add_all(values):
    while len(values) > 1:
        values = [a + b for a, b in zip(values[::2], values[1::2])]
    return values[0]


def sum_kernel(*refs):
    refs[-1][...] = add_all([ref[...] for ref in refs[:-1]])


def piece_kernel(z_ref, acts_ref, *refs):
    tokens, errors, out = refs[:NZ], refs[NZ : 2 * NZ], refs[2 * NZ]
    rows = acts_ref.shape[0] // NZ
    terms = []
    for shift in range(NZ):
        block = lax.rem(z_ref[0] - shift + NZ, NZ)
        acts = acts_ref[pl.ds(pl.multiple_of(block * rows, rows), rows), :]
        terms.append(dot_nn(split3(tokens[shift][...]), acts))
    out[...] = fold3(add_all(terms)) + add_all([ref[...] for ref in errors])


def ordered_mean(dp_ref, pieces, slots):
    for shift in range(NDP):
        slots[lax.rem(dp_ref[0] - shift + NDP, NDP)] = pieces[shift][...]
    return add_all([slots[member] for member in range(NDP)]) * (1.0 / NDP)


def mean_kernel(dp_ref, *refs):
    refs[NDP][...] = ordered_mean(dp_ref, refs[:NDP], refs[NDP + 1])


def stack_kernel(z_ref, *refs):
    for shift in range(NZ):
        refs[NZ][lax.rem(z_ref[0] - shift + NZ, NZ)] = refs[shift][...]


def ortho_kernel(x_ref, *refs):
    ins, split, panel = refs[:NX], refs[NX], refs[NX + 1]
    for shift in range(NX):
        home = lax.rem(x_ref[0] - shift + NX, NX) * NZ
        for block in range(NZ):
            panel[home + block] = ins[shift][block]
    blocks, count = panel.shape[0], panel.shape[1]
    groups = count // 8

    def inner_of(index):
        first = index // 8
        sums = [None] * groups
        for block in range(blocks):
            row = panel[block, index : index + 1, :]
            for group in range(first, groups):
                term = panel[block, group * 8 : group * 8 + 8, :] * row
                sums[group] = term if sums[group] is None else sums[group] + term
        return [None if s is None else jnp.sum(s, axis=1, keepdims=True) for s in sums]

    order = lax.broadcasted_iota(jnp.int32, (8, 1), 0)
    for index in range(count):
        first, place = index // 8, index % 8
        inner = inner_of(index)
        scale = 1.0 / (jnp.sqrt(inner[first][place : place + 1, :]) + ortho_eps)
        weights = []
        for group in range(first, groups):
            weight = inner[group] * (scale * scale)
            if group == first:
                weight = jnp.where(order > place, weight, 0.0)
            weights.append(weight)
        for block in range(blocks):
            row = panel[block, index : index + 1, :]
            for group in range(first, groups):
                if group == first and place == 7:
                    continue
                rows = slice(group * 8, group * 8 + 8)
                panel[block, rows, :] = panel[block, rows, :] - weights[group - first] * row
            panel[block, index : index + 1, :] = row * scale
    for block in range(blocks):
        split[:, block * 128 : block * 128 + 128] = split3(panel[block])


def right_kernel(basis_ref, acts_ref, et_ref, gt_ref, out_ref, tokens, errors):
    step = pl.program_id(0)

    @pl.when(step == 0)
    def _():
        tokens[...] = jnp.zeros_like(tokens)
        errors[...] = jnp.zeros_like(errors)

    basis = basis_ref[...]
    tokens[...] += dot_nt(basis, acts_ref[...])
    errors[...] += dot_nt(basis, et_ref[...])

    @pl.when(step == pl.num_programs(0) - 1)
    def _():
        grads = dot_nt(split3(fold3(tokens[...])), gt_ref[...])
        out_ref[...] = fold3(grads) + fold3(errors[...])


def final_kernel(dp_ref, *refs):
    pieces = refs[:NDP]
    (basis_ref, acts_ref, et_ref, gt_ref, weight, moment1, moment2) = refs[NDP : NDP + 7]
    (new_weight, new_moment1, new_moment2, new_error, q_new, slots, factor) = refs[NDP + 7 :]
    step = pl.program_id(0)

    @pl.when(step == 0)
    def _():
        mean = ordered_mean(dp_ref, pieces, slots)
        q_new[...] = mean
        stack = split3(mean)
        rows = mean.shape[0]
        hi, mid, lo = stack[:rows], stack[rows : 2 * rows], stack[2 * rows :]
        factor[...] = jnp.concatenate([hi, hi, hi, mid, mid, lo], axis=0)

    basis = basis_ref[...]
    rows = basis.shape[0] // 3
    hi, mid, lo = basis[:rows], basis[rows : 2 * rows], basis[2 * rows :]
    approx = dot_tn(factor[...], jnp.concatenate([hi, mid, lo, hi, mid, hi], axis=0))
    field = dot_nn(gt_ref[...], acts_ref[...]) + et_ref[...].astype(F32)
    new_error[...] = (field - approx).astype(BF16)

    @pl.when(step == 0)
    def _():
        first = beta_one * moment1[...] + (1.0 - beta_one) * approx
        second = beta_two * moment2[...] + (1.0 - beta_two) * approx * approx
        new_moment1[...] = first
        new_moment2[...] = second
        new_weight[...] = weight[...] - learn_rate * (first / corr_one) / (
            jnp.sqrt(second / corr_two) + adam_eps
        )


def call(kernel, outs, args, specs=None, scratch=(), limit=16, flops=0, moved=0, **more):
    return pl.pallas_call(
        kernel,
        out_shape=outs,
        in_specs=specs or [SMEM] + [VMEM] * (len(args) - 1),
        out_specs=jax.tree.map(lambda _: VMEM, outs),
        scratch_shapes=scratch,
        compiler_params=pltpu.CompilerParams(vmem_limit_bytes=limit * MIB),
        cost_estimate=pl.CostEstimate(flops=flops, bytes_accessed=moved, transcendentals=0),
        **more,
    )(*args)


def along_x(value, shift):
    return lax.ppermute(
        value, "mp", [(x * NZ + z, (x + shift) % NX * NZ + z) for x in range(NX) for z in range(NZ)]
    )


def along_z(value, shift):
    return lax.ppermute(
        value, "mp", [(x * NZ + z, x * NZ + (z + shift) % NZ) for x in range(NX) for z in range(NZ)]
    )


def along_dp(value, shift):
    return lax.ppermute(value, "dp", [(d, (d + shift) % NDP) for d in range(NDP)])


def spread(move, value, members):
    return [value] + [move(value, shift) for shift in range(1, members)]


def swap(move, values):
    return [values[0]] + [move(values[shift], shift) for shift in range(1, len(values))]


def shards(acts, grad_out, error_buffer, q_prev, weight, moment1, moment2):
    member = lax.axis_index("mp")
    x = (member // NZ).astype(jnp.int32).reshape(1)
    z = (member % NZ).astype(jnp.int32).reshape(1)
    dp = lax.axis_index("dp").astype(jnp.int32).reshape(1)
    gt, et = grad_out.T, error_buffer.T
    rank, ff = q_prev.shape
    tokens, model = acts.shape[0], et.shape[1]
    array = jax.ShapeDtypeStruct

    gathered = lax.all_gather(acts, "mp", axis=1, tiled=True)

    part = array((rank, tokens // NZ), F32)
    factor = call(
        token_kernel, [part] * NZ, (z, q_prev, gt),
        scratch=[pltpu.VMEM((NZ, rank, tokens // NZ), F32)],
        flops=6 * rank * ff * tokens, moved=2 * ff * tokens,
    )
    factor = swap(along_z, factor)
    factor = call(sum_kernel, part, tuple(factor), specs=[VMEM] * NZ, moved=8 * 16384)
    factor = spread(along_x, factor, NX)
    factor = call(sum_kernel, part, tuple(factor), specs=[VMEM] * NX, moved=4 * 16384)
    factor = spread(along_z, factor, NZ)

    wide = array((rank, model // NX), F32)
    narrow = array((rank, model // NX // NZ), F32)
    errors = call(
        error_kernel, [wide] * NX, (x, q_prev, et),
        scratch=[pltpu.VMEM((NX, rank, model // NX), F32)],
        flops=6 * rank * ff * model, moved=2 * ff * model,
    )
    errors = swap(along_x, errors)
    errors = call(
        split_sum_kernel, [narrow] * NZ, (z, *errors),
        scratch=[pltpu.VMEM((NZ, *narrow.shape), F32)], moved=4 * 131072,
    )
    errors = swap(along_z, errors)

    panel = call(piece_kernel, narrow, (z, acts, *factor, *errors), moved=MIB)
    panel = spread(along_dp, panel, NDP)
    panel = call(
        mean_kernel, narrow, (dp, *panel), scratch=[pltpu.VMEM((NDP, *narrow.shape), F32)], moved=131072
    )
    panel = spread(along_z, panel, NZ)
    panel = call(stack_kernel, array((NZ, *narrow.shape), F32), (z, *panel), moved=131072)
    panel = spread(along_x, panel, NX)
    split = call(
        ortho_kernel, array((3 * rank, model), BF16), (x, *panel),
        scratch=[pltpu.VMEM((NX * NZ, *narrow.shape), F32)], flops=MIB, moved=4 * MIB,
    )

    tile = 512
    right = pl.pallas_call(
        right_kernel,
        grid=(model // tile,),
        out_shape=array((rank, ff), F32),
        in_specs=[
            pl.BlockSpec((3 * rank, tile), lambda i: (0, i)),
            pl.BlockSpec((tokens, tile), lambda i: (0, i)),
            pl.BlockSpec((ff, tile), lambda i: (0, i)),
            pl.BlockSpec((ff, tokens), lambda i: (0, 0)),
        ],
        out_specs=pl.BlockSpec((rank, ff), lambda i: (0, 0)),
        scratch_shapes=[pltpu.VMEM((3 * rank, tokens), F32), pltpu.VMEM((3 * rank, ff), F32)],
        compiler_params=pltpu.CompilerParams(vmem_limit_bytes=24 * MIB),
        cost_estimate=pl.CostEstimate(flops=6 * rank * model * 1472, bytes_accessed=12 * MIB, transcendentals=0),
    )(split, gathered, et, gt)
    right = spread(along_dp, right, NDP)

    whole = lambda i, dp: (0, 0)
    turn = lambda i, dp: (0, lax.rem(dp[0] + i, model // tile))
    block = array((ff, tile), F32)
    outs = pl.pallas_call(
        final_kernel,
        grid_spec=pltpu.PrefetchScalarGridSpec(
            num_scalar_prefetch=1,
            grid=(model // tile,),
            in_specs=[pl.BlockSpec((rank, ff), whole)] * NDP
            + [
                pl.BlockSpec((3 * rank, tile), turn),
                pl.BlockSpec((tokens, tile), turn),
                pl.BlockSpec((ff, tile), turn),
                pl.BlockSpec((ff, tokens), whole),
            ]
            + [pl.BlockSpec((ff, tile), whole)] * 3,
            out_specs=[pl.BlockSpec((ff, tile), whole)] * 3
            + [pl.BlockSpec((ff, tile), turn), pl.BlockSpec((rank, ff), whole)],
            scratch_shapes=[pltpu.VMEM((NDP, rank, ff), F32), pltpu.VMEM((6 * rank, ff), BF16)],
        ),
        out_shape=[block] * 3 + [array((ff, model), BF16), array((rank, ff), F32)],
        compiler_params=pltpu.CompilerParams(vmem_limit_bytes=32 * MIB),
        cost_estimate=pl.CostEstimate(
            flops=2 * model * ff * (tokens + 6 * rank), bytes_accessed=22 * MIB, transcendentals=0
        ),
    )(dp, *right, split, gathered, et, gt, weight.T, moment1.T, moment2.T)
    new_weight, new_moment1, new_moment2, new_error, q_new = outs
    return (new_weight.T, new_moment1.T, new_moment2.T, new_error.T, q_new)


def solution(mesh):
    placed = (
        P("dp", "mp"),
        P("dp", "mp"),
        P("dp", "mp"),
        P(None, "mp"),
        P("dp", "mp"),
        P("dp", "mp"),
        P("dp", "mp"),
    )
    return jax.shard_map(
        shards,
        mesh=mesh,
        in_specs=placed,
        out_specs=(P("dp", "mp"), P("dp", "mp"), P("dp", "mp"), P("dp", "mp"), P(None, "mp")),
        check_vma=False,
    )
```

```python
import functools

import jax
import jax.numpy as jnp
from jax import lax
from jax.experimental import pallas as pl
from jax.experimental.pallas import tpu as pltpu
from jax.sharding import PartitionSpec as P

ortho_eps = 1e-08
adam_eps = 1e-08
beta_one = 0.9
beta_two = 0.95
learn_rate = 0.01
corr_one = 1.0 - 0.9**10
corr_two = 1.0 - 0.95**10

NX, NZ, NDP = 4, 8, 8
NMP = NX * NZ
ROWS = 384
LANES = 128
F32, BF16 = jnp.float32, jnp.bfloat16
MIB = 1 << 20
SMEM = pl.BlockSpec(memory_space=pltpu.SMEM)
VMEM = pl.BlockSpec(memory_space=pltpu.VMEM)


def split3(value):
    hi = value.astype(BF16)
    rest = value - hi.astype(F32)
    mid = rest.astype(BF16)
    lo = (rest - mid.astype(F32)).astype(BF16)
    return jnp.concatenate([hi, mid, lo], axis=0)


def fold3(stacked):
    rows = stacked.shape[0] // 3
    return stacked[:rows] + (stacked[rows : 2 * rows] + stacked[2 * rows :])


def dot_nn(a, b):
    return lax.dot_general(a, b, (((1,), (0,)), ((), ())), preferred_element_type=F32)


def dot_nt(a, b):
    return lax.dot_general(a, b, (((1,), (1,)), ((), ())), preferred_element_type=F32)


def dot_tn(a, b):
    return lax.dot_general(a, b, (((0,), (0,)), ((), ())), preferred_element_type=F32)


def add_all(values):
    while len(values) > 1:
        values = [a + b for a, b in zip(values[::2], values[1::2])] + values[len(values) // 2 * 2 :]
    return values[0]


def lanes(array, block):
    return array[:, block * LANES : (block + 1) * LANES]


def wide(ref, count):
    return jnp.concatenate([ref[block] for block in range(count)], axis=1)


def token_kernel(q_ref, gt_ref, out):
    total = fold3(dot_nn(split3(q_ref[...]), gt_ref[...]))
    columns = total.shape[1] // LANES
    for row in range(total.shape[0] // 8):
        for column in range(columns):
            out[row * columns + column] = lanes(total[row * 8 : row * 8 + 8], column)


def error_kernel(q_ref, et_ref, tokens, out):
    tile = add_all([tokens[member] for member in range(NMP)])
    split = split3(q_ref[...])
    group = 4
    for start in range(0, NMP, group):
        part = fold3(dot_nn(split, et_ref[:, start * LANES : (start + group) * LANES]))
        for block in range(group):
            out[start + block, 0:8, :] = tile
            out[start + block, 8:, :] = lanes(part, block)


def piece_kernel(acts_ref, mixed, out):
    blocks = acts_ref.shape[0] // LANES
    terms = []
    for block in range(blocks):
        factor = jnp.concatenate([mixed[row * blocks + block, 0:8, :] for row in range(NMP // blocks)], axis=0)
        terms.append(dot_nn(split3(factor), acts_ref[block * LANES : (block + 1) * LANES, :]))
    piece = fold3(add_all(terms)) + add_all([mixed[member, 8:, :] for member in range(NMP)])
    for member in range(NDP):
        out[member] = piece


def mean_kernel(pieces, out):
    mean = add_all([pieces[member] for member in range(NDP)]) * (1.0 / NDP)
    for member in range(NMP):
        out[member] = mean


def ortho_kernel(panel_ref, split, panel):
    panel[...] = panel_ref[...]
    blocks, count = panel.shape[0], panel.shape[1]
    groups = count // 8

    def inner_of(index):
        first = index // 8
        sums = [None] * groups
        for block in range(blocks):
            row = panel[block, index : index + 1, :]
            for group in range(first, groups):
                term = panel[block, group * 8 : group * 8 + 8, :] * row
                sums[group] = term if sums[group] is None else sums[group] + term
        return [None if s is None else jnp.sum(s, axis=1, keepdims=True) for s in sums]

    order = lax.broadcasted_iota(jnp.int32, (8, 1), 0)
    for index in range(count):
        first, place = index // 8, index % 8
        inner = inner_of(index)
        scale = 1.0 / (jnp.sqrt(inner[first][place : place + 1, :]) + ortho_eps)
        weights = []
        for group in range(first, groups):
            weight = inner[group] * (scale * scale)
            if group == first:
                weight = jnp.where(order > place, weight, 0.0)
            weights.append(weight)
        for block in range(blocks):
            row = panel[block, index : index + 1, :]
            for group in range(first, groups):
                if group == first and place == 7:
                    continue
                rows = slice(group * 8, group * 8 + 8)
                panel[block, rows, :] = panel[block, rows, :] - weights[group - first] * row
            panel[block, index : index + 1, :] = row * scale
    for block in range(blocks):
        split[block] = split3(panel[block])


def field_kernel(x_ref, acts1, near0, near1, near3, far_a, far_b, basis_ref, et_ref, gt_ref, field, right, acts2, tokens1,
                 tokens2, errors):
    step = pl.program_id(0)

    @pl.when(step == 0)
    def _():
        tokens1[...] = jnp.zeros_like(tokens1)
        tokens2[...] = jnp.zeros_like(tokens2)
        errors[...] = jnp.zeros_like(errors)

    for place, ref in enumerate((near0, near0, near1, near1, near3, near3, far_a, far_b)):

        @pl.when(step == place)
        def _():
            acts2[...] = ref[...]

    count = acts2.shape[0]
    first = wide(acts1.at[:, 0], count)
    second = wide(acts2, count)
    error = et_ref[...]
    basis = wide(basis_ref, count)
    grad = dot_nn(gt_ref[:, :ROWS], first) + dot_nn(gt_ref[:, ROWS:], second)
    field[chunk_at(step, x_ref[0])] = grad + error.astype(F32)
    tokens1[...] += dot_nt(basis, first)
    tokens2[...] += dot_nt(basis, second)
    errors[...] += dot_nt(basis, error)

    @pl.when(step == pl.num_programs(0) - 1)
    def _():
        grads = dot_nt(split3(fold3(tokens1[...])), gt_ref[:, :ROWS])
        grads = grads + dot_nt(split3(fold3(tokens2[...])), gt_ref[:, ROWS:])
        total = fold3(grads) + fold3(errors[...])
        for member in range(NDP):
            right[member] = total


def shift_at(step):
    turn = step // 2
    return jnp.where(turn >= 2, 5 - turn, turn)


def chunk_at(step, x):
    return lax.rem(x - shift_at(step) + NX, NX) * 2 + lax.rem(step, 2)


def final_kernel(dp_ref, pieces, basis_ref, field, weight, moment1, moment2, new_weight, new_moment1, new_moment2,
                 new_error, q_new, updated, rounded, sems):
    mean = add_all([pieces[member] for member in range(NDP)]) * (1.0 / NDP)
    q_new[...] = mean
    stack = split3(mean)
    rows = mean.shape[0]
    hi, mid, lo = stack[:rows], stack[rows : 2 * rows], stack[2 * rows :]
    factor = jnp.concatenate([hi, hi, hi, mid, mid, lo], axis=0)
    chunks = field.shape[0]
    count = basis_ref.shape[0] // chunks

    def approx_of(chunk):
        basis = jnp.concatenate([basis_ref[chunk * count + block] for block in range(count)], axis=1)
        hi, mid, lo = basis[:rows], basis[rows : 2 * rows], basis[2 * rows :]
        return dot_tn(factor, jnp.concatenate([hi, mid, lo, hi, mid, hi], axis=0))

    update = approx_of(dp_ref[0])
    first = beta_one * moment1[...] + (1.0 - beta_one) * update
    second = beta_two * moment2[...] + (1.0 - beta_two) * update * update
    updated[0] = first
    updated[1] = second
    updated[2] = weight[...] - learn_rate * (first / corr_one) / (jnp.sqrt(second / corr_two) + adam_eps)
    copies = []

    def send(source, target):
        copy = pltpu.make_async_copy(source, target, sems.at[len(copies)])
        copy.start()
        copies.append(copy)

    send(updated.at[0], new_moment1)
    send(updated.at[1], new_moment2)
    send(updated.at[2], new_weight)
    width = field.shape[2]
    for chunk in range(chunks):
        rounded[chunk] = (field[chunk] - approx_of(chunk)).astype(BF16)
        send(rounded.at[chunk], new_error.at[:, chunk * width : (chunk + 1) * width])
    for copy in copies:
        copy.wait()


def call(kernel, outs, args, specs=None, out_specs=None, scratch=(), limit=16, flops=0, moved=0):
    return pl.pallas_call(
        kernel,
        out_shape=outs,
        in_specs=specs or [VMEM] * len(args),
        out_specs=out_specs or jax.tree.map(lambda _: VMEM, outs),
        scratch_shapes=scratch,
        compiler_params=pltpu.CompilerParams(vmem_limit_bytes=limit * MIB),
        cost_estimate=pl.CostEstimate(flops=flops, bytes_accessed=moved, transcendentals=0),
    )(*args)


def along_x(value, shift):
    return lax.ppermute(
        value, "mp", [(x * NZ + z, (x + shift) % NX * NZ + z) for x in range(NX) for z in range(NZ)]
    )


def gather_z(value):
    return lax.all_gather(value, "mp", axis=0, axis_index_groups=[[x * NZ + z for z in range(NZ)] for x in range(NX)])


def exchange(value, axis):
    return lax.all_to_all(value, axis, 0, 0)


def shards(acts, grad_out, error_buffer, q_prev, weight, moment1, moment2):
    x = (lax.axis_index("mp") // NZ).astype(jnp.int32).reshape(1)
    dp = lax.axis_index("dp").astype(jnp.int32).reshape(1)
    gt, et = grad_out.T, error_buffer.T
    rank, ff = q_prev.shape
    tokens, model = acts.shape[0], et.shape[1]
    array = jax.ShapeDtypeStruct

    near0 = gather_z(acts[ROWS:])
    head = acts[:ROWS]
    acts1 = gather_z(jnp.stack([head] + [along_x(head, shift) for shift in range(1, NX)]))
    near1, near3 = along_x(near0, 1), along_x(near0, 3)
    far_a, far_b = along_x(near1[: NZ // 2], 1), along_x(near3[NZ // 2 :], 3)

    factor = call(
        token_kernel, array((NMP, 8, LANES), F32), (q_prev, gt), flops=6 * rank * ff * tokens, moved=2 * ff * tokens
    )
    factor = exchange(factor, "mp")
    mixed = call(
        error_kernel, array((NMP, 8 + rank, LANES), F32), (q_prev, et, factor),
        flops=6 * rank * ff * model, moved=2 * ff * model,
    )
    mixed = exchange(mixed, "mp")
    panel = call(piece_kernel, array((NDP, rank, LANES), F32), (acts, mixed), moved=MIB)
    panel = exchange(panel, "dp")
    panel = call(mean_kernel, array((NMP, rank, LANES), F32), (panel,), moved=MIB)
    panel = exchange(panel, "mp")
    basis = call(
        ortho_kernel, array((NMP, 3 * rank, LANES), BF16), (panel,),
        scratch=[pltpu.VMEM((NMP, rank, LANES), F32)], flops=MIB, moved=4 * MIB,
    )

    chunks, count = 8, NZ // 2
    width = model // chunks
    half = lambda first: lambda i, x: (jnp.clip(i - first, 0, 1), 0, 0)
    whole = lambda i, x: (0, 0, 0)
    near = (count, tokens - ROWS, LANES)
    field, right = pl.pallas_call(
        field_kernel,
        grid_spec=pltpu.PrefetchScalarGridSpec(
            num_scalar_prefetch=1,
            grid=(chunks,),
            in_specs=[
                pl.BlockSpec((count, 1, ROWS, LANES), lambda i, x: (lax.rem(i, 2), shift_at(i), 0, 0)),
                pl.BlockSpec(near, half(0)),
                pl.BlockSpec(near, half(2)),
                pl.BlockSpec(near, half(4)),
                pl.BlockSpec(near, whole),
                pl.BlockSpec(near, whole),
                pl.BlockSpec((count, 3 * rank, LANES), lambda i, x: (chunk_at(i, x[0]), 0, 0)),
                pl.BlockSpec((ff, width), lambda i, x: (0, chunk_at(i, x[0]))),
                pl.BlockSpec((ff, tokens), lambda i, x: (0, 0)),
            ],
            out_specs=[VMEM, VMEM],
            scratch_shapes=[
                pltpu.VMEM(near, BF16),
                pltpu.VMEM((3 * rank, ROWS), F32),
                pltpu.VMEM((3 * rank, tokens - ROWS), F32),
                pltpu.VMEM((3 * rank, ff), F32),
            ],
        ),
        out_shape=[array((chunks, ff, width), F32), array((NDP, rank, ff), F32)],
        compiler_params=pltpu.CompilerParams(vmem_limit_bytes=36 * MIB),
        cost_estimate=pl.CostEstimate(flops=2 * model * ff * tokens, bytes_accessed=20 * MIB, transcendentals=0),
    )(x, acts1, near0, near1, near3, far_a, far_b, basis, et, gt)
    right = exchange(right, "dp")

    block = array((ff, width), F32)
    anywhere = pl.BlockSpec(memory_space=pl.ANY)
    outs = call(
        final_kernel,
        [block] * 3 + [array((ff, model), BF16), array((rank, ff), F32)],
        (dp, right, basis, field, weight.T, moment1.T, moment2.T),
        specs=[SMEM] + [VMEM] * 6,
        out_specs=[anywhere] * 4 + [VMEM],
        scratch=[
            pltpu.VMEM((3, ff, width), F32),
            pltpu.VMEM((chunks, ff, width), BF16),
            pltpu.SemaphoreType.DMA((3 + chunks,)),
        ],
        limit=32, flops=12 * rank * model * ff, moved=20 * MIB,
    )
    new_weight, new_moment1, new_moment2, new_error, q_new = outs
    return (new_weight.T, new_moment1.T, new_moment2.T, new_error.T, q_new)


def solution(mesh):
    placed = (
        P("dp", "mp"),
        P("dp", "mp"),
        P("dp", "mp"),
        P(None, "mp"),
        P("dp", "mp"),
        P("dp", "mp"),
        P("dp", "mp"),
    )
    return jax.shard_map(
        shards,
        mesh=mesh,
        in_specs=placed,
        out_specs=(P("dp", "mp"), P("dp", "mp"), P("dp", "mp"), P("dp", "mp"), P(None, "mp")),
        check_vma=False,
    )
```

```python
import jax
import jax.numpy as jnp
import numpy as np
from jax import lax
from jax.experimental import pallas as pl
from jax.experimental.pallas import tpu as pltpu
from jax.sharding import PartitionSpec as P

ortho_eps = 1e-08
adam_eps = 1e-08
beta_one = 0.9
beta_two = 0.95
learn_rate = 0.01
corr_one = 1.0 - 0.9**10
corr_two = 1.0 - 0.95**10

NX, NZ, NDP = 4, 8, 8
NMP = NX * NZ
ROWS = 512
LANES = 128
F32, BF16 = jnp.float32, jnp.bfloat16
MIB = 1 << 20
SMEM = pl.BlockSpec(memory_space=pltpu.SMEM)
VMEM = pl.BlockSpec(memory_space=pltpu.VMEM)
HBM = pl.BlockSpec(memory_space=pltpu.HBM)

RING4 = ([1, 0, 3, 2], [3, 2, 1, 0])
RING8 = ([1, 0, 3, 2, 5, 4, 7, 6], [7, 2, 1, 4, 3, 6, 5, 0], [3, 6, 5, 0, 7, 2, 1, 4])
ALONG_Z = [[x * NZ + to for x in range(NX) for to in level] for level in RING8]
ALONG_X = [[to * NZ + z for to in level for z in range(NZ)] for level in RING4]
ALONG_DP = [[1, 0, 3, 2, 5, 4, 7, 6]] + [[to * 2 + core for to in level for core in range(2)] for level in RING4]


def met(levels, members):
    held = [[member] for member in range(members)]
    for level in levels:
        held = [held[member] + held[level[member]] for member in range(members)]
    return np.array(held, np.int32)


def split3(value):
    hi = value.astype(BF16)
    rest = value - hi.astype(F32)
    mid = rest.astype(BF16)
    lo = (rest - mid.astype(F32)).astype(BF16)
    return jnp.concatenate([hi, mid, lo], axis=0)


def fold3(stacked):
    rows = stacked.shape[0] // 3
    return stacked[:rows] + (stacked[rows : 2 * rows] + stacked[2 * rows :])


def dot_nn(a, b):
    return lax.dot_general(a, b, (((1,), (0,)), ((), ())), preferred_element_type=F32)


def dot_nt(a, b):
    return lax.dot_general(a, b, (((1,), (1,)), ((), ())), preferred_element_type=F32)


def dot_tn(a, b):
    return lax.dot_general(a, b, (((0,), (0,)), ((), ())), preferred_element_type=F32)


def add_all(values):
    while len(values) > 1:
        values = [a + b for a, b in zip(values[::2], values[1::2])] + values[len(values) // 2 * 2 :]
    return values[0]


def lanes(array, block):
    return array[:, block * LANES : (block + 1) * LANES]


def wide(ref, count):
    return jnp.concatenate([ref[block] for block in range(count)], axis=1)


def lanes(array, block):
    return array[:, block * LANES : (block + 1) * LANES]


def add_all(values):
    while len(values) > 1:
        values = [a + b for a, b in zip(values[::2], values[1::2])]
    return values[0]


def token_kernel(q_hbm, gt_hbm, out, q_ref, gt_ref, sems):
    copies = [pltpu.make_async_copy(q_hbm, q_ref, sems.at[0]), pltpu.make_async_copy(gt_hbm, gt_ref, sems.at[1])]
    for copy in copies:
        copy.start()
    for copy in copies:
        copy.wait()
    out[...] = fold3(dot_nn(split3(q_ref[...]), gt_ref[...]))


def error_kernel(q_hbm, et_hbm, out, q_ref, et_ref, sems):
    count = et_ref.shape[0]
    width = et_ref.shape[2]
    copies = [
        pltpu.make_async_copy(et_hbm.at[:, chunk * width : (chunk + 1) * width], et_ref.at[chunk], sems.at[chunk])
        for chunk in range(count)
    ]
    first = pltpu.make_async_copy(q_hbm, q_ref, sems.at[count])
    first.start()
    for copy in copies:
        copy.start()
    first.wait()
    split = split3(q_ref[...])
    blocks = width // LANES
    for chunk in range(count):
        copies[chunk].wait()
        part = fold3(dot_nn(split, et_ref[chunk]))
        for block in range(blocks):
            out[chunk * blocks + block] = lanes(part, block)


def piece_kernel(factor, acts_ref, errors, out):
    piece = fold3(dot_nn(split3(factor[...]), acts_ref[...]))
    out[0] = piece + add_all([errors[member] for member in range(NMP)])


def ortho_kernel(place_ref, mine, theirs, split, panel):
    for block in range(NMP // 2):
        panel[place_ref[block]] = mine[block] * (1.0 / NDP)
        panel[place_ref[NMP // 2 + block]] = theirs[block] * (1.0 / NDP)
    blocks, count = panel.shape[0], panel.shape[1]
    groups = count // 8

    def inner_of(index):
        first = index // 8
        sums = [None] * groups
        for block in range(blocks):
            row = panel[block, index : index + 1, :]
            for group in range(first, groups):
                term = panel[block, group * 8 : group * 8 + 8, :] * row
                sums[group] = term if sums[group] is None else sums[group] + term
        return [None if s is None else jnp.sum(s, axis=1, keepdims=True) for s in sums]

    order = lax.broadcasted_iota(jnp.int32, (8, 1), 0)
    for index in range(count):
        first, place = index // 8, index % 8
        inner = inner_of(index)
        scale = 1.0 / (jnp.sqrt(inner[first][place : place + 1, :]) + ortho_eps)
        weights = []
        for group in range(first, groups):
            weight = inner[group] * (scale * scale)
            if group == first:
                weight = jnp.where(order > place, weight, 0.0)
            weights.append(weight)
        for block in range(blocks):
            row = panel[block, index : index + 1, :]
            for group in range(first, groups):
                if group == first and place == 7:
                    continue
                rows = slice(group * 8, group * 8 + 8)
                panel[block, rows, :] = panel[block, rows, :] - weights[group - first] * row
            panel[block, index : index + 1, :] = row * scale
    for block in range(blocks):
        split[block] = split3(panel[block])


def field_kernel(x_ref, place_ref, head, *refs):
    tails = refs[:8]
    basis_ref, et_hbm, gt_hbm, field, right, acts_v, error_v, gt_v, field_v, total = refs[8:18]
    tail_sems, head_sems, error_sems, field_sems = refs[18:]
    steps, count = acts_v.shape[0], acts_v.shape[1]
    below = pl.ds(ROWS, acts_v.shape[2] - ROWS)

    def block_at(step, k):
        turn = step // 2
        shift = jnp.where(turn >= 2, 5 - turn, turn)
        return lax.rem(x_ref[0] - shift + NX, NX) * NZ + place_ref[lax.rem(step, 2) * count + k]

    def fetch(step):
        for k in range(count):
            block = block_at(step, k)
            pltpu.make_async_copy(head.at[block], acts_v.at[step, k, pl.ds(0, ROWS)], head_sems.at[step]).start()
            columns = pl.ds(pl.multiple_of(block * LANES, LANES), LANES)
            pltpu.make_async_copy(et_hbm.at[:, columns], error_v.at[step, k], error_sems.at[step]).start()

    gt_copy = pltpu.make_async_copy(gt_hbm, gt_v, tail_sems.at[steps])
    gt_copy.start()
    fetch(0)
    for step in range(steps):
        pltpu.make_async_copy(tails[step], acts_v.at[step, :, below], tail_sems.at[step]).start()
        if step == 0:
            fetch(1)
    total[...] = jnp.zeros_like(total)
    gt_copy.wait()

    def body(step, carry):
        @pl.when(step + 2 < steps)
        def _():
            fetch(step + 2)

        top = acts_v.at[step, :, pl.ds(0, ROWS)]
        pltpu.make_async_copy(top, top, head_sems.at[step]).wait()
        bottom = acts_v.at[step, :, below]
        pltpu.make_async_copy(bottom, bottom, tail_sems.at[step]).wait()
        pltpu.make_async_copy(error_v.at[step], error_v.at[step], error_sems.at[step]).wait()
        blocks = [block_at(step, k) for k in range(count)]
        acts = jnp.concatenate([acts_v[step, k] for k in range(count)], axis=1)
        error = jnp.concatenate([error_v[step, k] for k in range(count)], axis=1)
        basis = jnp.concatenate([basis_ref[block] for block in blocks], axis=1)
        value = dot_nn(gt_v[...], acts) + error.astype(F32)
        for k in range(count):
            field_v[step, k] = lanes(value, k)
            pltpu.make_async_copy(field_v.at[step, k], field.at[blocks[k]], field_sems.at[step]).start()
        hi = value.astype(BF16)
        mid = (value - hi.astype(F32)).astype(BF16)
        total[...] += dot_nt(hi, basis) + dot_nt(mid, basis)
        return carry

    lax.fori_loop(0, steps, body, 0)
    right[...] = fold3(total[...].T)
    for step in range(steps):
        pltpu.make_async_copy(field_v.at[step], field_v.at[step], field_sems.at[step]).wait()


def final_kernel(dp_ref, sum_ref, basis_ref, field, weight, moment1, moment2, new_weight, new_moment1, new_moment2,
                 new_error, q_new, field_v, updated, rounded, field_sems, sems):
    chunks, width = rounded.shape[0], rounded.shape[2]
    count = width // LANES
    reads = []
    for chunk in range(chunks):
        blocks = pl.ds(chunk * count, count)
        reads.append(pltpu.make_async_copy(field.at[blocks], field_v.at[blocks], field_sems.at[chunk]))
        reads[-1].start()
    mean = sum_ref[...] * (1.0 / NDP)
    q_new[...] = mean
    rows, ff = mean.shape
    stack = split3(mean.T)
    hi, mid, lo = stack[:ff], stack[ff : 2 * ff], stack[2 * ff :]
    factor = jnp.concatenate([hi, hi, hi, mid, mid, lo], axis=1)

    def approx_of(chunk):
        basis = jnp.concatenate([basis_ref[chunk * count + block] for block in range(count)], axis=1)
        hi, mid, lo = basis[:rows], basis[rows : 2 * rows], basis[2 * rows :]
        return dot_nn(factor, jnp.concatenate([hi, mid, lo, hi, mid, hi], axis=0))

    copies = []

    def send(source, target):
        copy = pltpu.make_async_copy(source, target, sems.at[len(copies)])
        copy.start()
        copies.append(copy)

    update = approx_of(dp_ref[0])
    first = beta_one * moment1[...] + (1.0 - beta_one) * update
    second = beta_two * moment2[...] + (1.0 - beta_two) * update * update
    updated[0] = first
    updated[1] = second
    updated[2] = weight[...] - learn_rate * (first / corr_one) / (jnp.sqrt(second / corr_two) + adam_eps)
    send(updated.at[0], new_moment1)
    send(updated.at[1], new_moment2)
    send(updated.at[2], new_weight)
    for chunk in range(chunks):
        approx = approx_of(chunk)
        reads[chunk].wait()
        for block in range(count):
            columns = slice(block * LANES, (block + 1) * LANES)
            rounded[chunk, :, columns] = (field_v[chunk * count + block] - lanes(approx, block)).astype(BF16)
        send(rounded.at[chunk], new_error.at[:, chunk * width : (chunk + 1) * width])
    for copy in copies:
        copy.wait()


def call(kernel, outs, args, specs=None, out_specs=None, scratch=(), limit=16, flops=0, moved=0):
    return pl.pallas_call(
        kernel,
        out_shape=outs,
        in_specs=specs or [VMEM] * len(args),
        out_specs=out_specs or jax.tree.map(lambda _: VMEM, outs),
        scratch_shapes=scratch,
        compiler_params=pltpu.CompilerParams(vmem_limit_bytes=limit * MIB),
        cost_estimate=pl.CostEstimate(flops=flops, bytes_accessed=moved, transcendentals=0),
    )(*args)


def swap(value, axis, level):
    return lax.ppermute(value, axis, list(enumerate(level)))


def total(value, axis, levels):
    for level in levels:
        value = value + swap(value, axis, level)
    return value


def along_x(value, shift):
    return lax.ppermute(
        value, "mp", [(x * NZ + z, (x + shift) % NX * NZ + z) for x in range(NX) for z in range(NZ)]
    )


def shards(acts, grad_out, error_buffer, q_prev, weight, moment1, moment2):
    member = lax.axis_index("mp")
    x = (member // NZ).astype(jnp.int32).reshape(1)
    place = jnp.asarray(met(ALONG_Z + ALONG_X, NMP))[member]
    place_z = jnp.asarray(met(RING8, NZ))[member % NZ]
    dp = lax.axis_index("dp").astype(jnp.int32).reshape(1)
    gt, et = grad_out.T, error_buffer.T
    rank, ff = q_prev.shape
    tokens, model = acts.shape[0], et.shape[1]
    array = jax.ShapeDtypeStruct

    head = lax.all_gather(acts[:ROWS], "mp", axis=0)

    factor = call(
        token_kernel, array((rank, tokens), F32), (q_prev, gt), specs=[HBM] * 2,
        scratch=[pltpu.VMEM((rank, ff), F32), pltpu.VMEM((ff, tokens), BF16), pltpu.SemaphoreType.DMA((2,))],
        limit=60, flops=6 * rank * ff * tokens, moved=2 * ff * tokens,
    )
    errors = call(
        error_kernel, array((NMP, rank, LANES), F32), (q_prev, et), specs=[HBM] * 2,
        scratch=[
            pltpu.VMEM((rank, ff), F32), pltpu.VMEM((8, ff, model // 8), BF16), pltpu.SemaphoreType.DMA((9,)),
        ],
        limit=58, flops=6 * rank * ff * model, moved=2 * ff * model,
    )
    errors = lax.all_to_all(errors, "mp", 0, 0)
    factor = total(factor, "mp", ALONG_Z + ALONG_X)

    tail = acts[ROWS:][None]
    for level in ALONG_Z[:2]:
        tail = jnp.concatenate([tail, swap(tail, "mp", level)])
    near0 = (tail, swap(tail, "mp", ALONG_Z[2]))
    near1 = [along_x(part, 1) for part in near0]
    near3 = [along_x(part, 3) for part in near0]
    far = (along_x(near1[0], 1), along_x(near3[1], 3))

    panel = call(piece_kernel, array((1, rank, LANES), F32), (factor, acts, errors), moved=MIB)
    panel = total(panel, "dp", ALONG_DP)
    levels = ALONG_Z + ALONG_X
    for level in levels[:-1]:
        panel = jnp.concatenate([panel, swap(panel, "mp", level)])
    basis = call(
        ortho_kernel, array((NMP, 3 * rank, LANES), BF16), (place, panel, swap(panel, "mp", levels[-1])),
        specs=[SMEM, VMEM, VMEM], scratch=[pltpu.VMEM((NMP, rank, LANES), F32)], flops=MIB, moved=4 * MIB,
    )

    chunks, count = 8, NZ // 2
    width = model // chunks
    field, right = call(
        field_kernel,
        [array((NMP, ff, LANES), F32), array((rank, ff), F32)],
        (x, place_z, head, *near0, *near1, *near3, *far, basis, et, gt),
        specs=[SMEM, SMEM] + [HBM] * 9 + [VMEM, HBM, HBM],
        out_specs=[HBM, VMEM],
        scratch=[
            pltpu.VMEM((chunks, count, tokens, LANES), BF16),
            pltpu.VMEM((chunks, count, ff, LANES), BF16),
            pltpu.VMEM((ff, tokens), BF16),
            pltpu.VMEM((chunks, count, ff, LANES), F32),
            pltpu.VMEM((ff, 3 * rank), F32),
            pltpu.SemaphoreType.DMA((chunks + 1,)),
            pltpu.SemaphoreType.DMA((chunks,)),
            pltpu.SemaphoreType.DMA((chunks,)),
            pltpu.SemaphoreType.DMA((chunks,)),
        ],
        limit=49, flops=2 * model * ff * tokens, moved=13 * MIB,
    )
    right = total(right, "dp", ALONG_DP)

    block = array((ff, width), F32)
    outs = call(
        final_kernel,
        [block] * 3 + [array((ff, model), BF16), array((rank, ff), F32)],
        (dp, right, basis, field, weight.T, moment1.T, moment2.T),
        specs=[SMEM, VMEM, VMEM, HBM, VMEM, VMEM, VMEM],
        out_specs=[HBM] * 4 + [VMEM],
        scratch=[
            pltpu.VMEM((NMP, ff, LANES), F32),
            pltpu.VMEM((3, ff, width), F32),
            pltpu.VMEM((chunks, ff, width), BF16),
            pltpu.SemaphoreType.DMA((chunks,)),
            pltpu.SemaphoreType.DMA((3 + chunks,)),
        ],
        limit=57, flops=12 * rank * model * ff, moved=20 * MIB,
    )
    new_weight, new_moment1, new_moment2, new_error, q_new = outs
    return (new_weight.T, new_moment1.T, new_moment2.T, new_error.T, q_new)


def solution(mesh):
    placed = (
        P("dp", "mp"),
        P("dp", "mp"),
        P("dp", "mp"),
        P(None, "mp"),
        P("dp", "mp"),
        P("dp", "mp"),
        P("dp", "mp"),
    )
    return jax.shard_map(
        shards,
        mesh=mesh,
        in_specs=placed,
        out_specs=(P("dp", "mp"), P("dp", "mp"), P("dp", "mp"), P("dp", "mp"), P(None, "mp")),
        check_vma=False,
    )
```

```python
import jax
import jax.numpy as jnp
import numpy as np
from jax import lax
from jax.experimental import pallas as pl
from jax.experimental.pallas import tpu as pltpu
from jax.sharding import PartitionSpec as P

ortho_eps = 1e-08
adam_eps = 1e-08
beta_one = 0.9
beta_two = 0.95
learn_rate = 0.01
corr_one = 1.0 - 0.9**10
corr_two = 1.0 - 0.95**10

NX, NZ, NDP = 4, 8, 8
NMP = NX * NZ
LANES = 128
F32, BF16 = jnp.float32, jnp.bfloat16
MIB = 1 << 20
SMEM = pl.BlockSpec(memory_space=pltpu.SMEM)
VMEM = pl.BlockSpec(memory_space=pltpu.VMEM)
HBM = pl.BlockSpec(memory_space=pltpu.HBM)

RING4 = ([1, 0, 3, 2], [3, 2, 1, 0])
RING8 = ([1, 0, 3, 2, 5, 4, 7, 6], [7, 2, 1, 4, 3, 6, 5, 0], [3, 6, 5, 0, 7, 2, 1, 4])
ALONG_Z = [[x * NZ + to for x in range(NX) for to in level] for level in RING8]
ALONG_X = [[to * NZ + z for to in level for z in range(NZ)] for level in RING4]
ALONG_DP = [[1, 0, 3, 2, 5, 4, 7, 6]] + [[to * 2 + core for to in level for core in range(2)] for level in RING4]


def met(levels, members):
    held = [[member] for member in range(members)]
    for level in levels:
        held = [held[member] + held[level[member]] for member in range(members)]
    return np.array(held, np.int32)


def split3(value):
    hi = value.astype(BF16)
    rest = value - hi.astype(F32)
    mid = rest.astype(BF16)
    lo = (rest - mid.astype(F32)).astype(BF16)
    return jnp.concatenate([hi, mid, lo], axis=0)


def fold3(stacked):
    rows = stacked.shape[0] // 3
    return stacked[:rows] + (stacked[rows : 2 * rows] + stacked[2 * rows :])


def dot_nn(a, b):
    return lax.dot_general(a, b, (((1,), (0,)), ((), ())), preferred_element_type=F32)


def dot_nt(a, b):
    return lax.dot_general(a, b, (((1,), (1,)), ((), ())), preferred_element_type=F32)


def dot_tn(a, b):
    return lax.dot_general(a, b, (((0,), (0,)), ((), ())), preferred_element_type=F32)


def add_all(values):
    while len(values) > 1:
        values = [a + b for a, b in zip(values[::2], values[1::2])] + values[len(values) // 2 * 2 :]
    return values[0]


def lanes(array, block):
    return array[:, block * LANES : (block + 1) * LANES]


def wide(ref, count):
    return jnp.concatenate([ref[block] for block in range(count)], axis=1)


def lanes(array, block):
    return array[:, block * LANES : (block + 1) * LANES]


def add_all(values):
    while len(values) > 1:
        values = [a + b for a, b in zip(values[::2], values[1::2])]
    return values[0]


def token_kernel(q_hbm, gt_hbm, out, q_ref, gt_ref, sems):
    copies = [pltpu.make_async_copy(q_hbm, q_ref, sems.at[0]), pltpu.make_async_copy(gt_hbm, gt_ref, sems.at[1])]
    for copy in copies:
        copy.start()
    for copy in copies:
        copy.wait()
    out[...] = fold3(dot_nn(split3(q_ref[...]), gt_ref[...]))


def error_kernel(q_hbm, et_hbm, out, q_ref, et_ref, sems):
    count = et_ref.shape[0]
    width = et_ref.shape[2]
    copies = [
        pltpu.make_async_copy(et_hbm.at[:, chunk * width : (chunk + 1) * width], et_ref.at[chunk], sems.at[chunk])
        for chunk in range(count)
    ]
    first = pltpu.make_async_copy(q_hbm, q_ref, sems.at[count])
    first.start()
    for copy in copies:
        copy.start()
    first.wait()
    split = split3(q_ref[...])
    blocks = width // LANES
    for chunk in range(count):
        copies[chunk].wait()
        part = fold3(dot_nn(split, et_ref[chunk]))
        for block in range(blocks):
            out[chunk * blocks + block] = lanes(part, block)


def piece_kernel(factor, acts_ref, errors, out):
    piece = fold3(dot_nn(split3(factor[...]), acts_ref[...]))
    out[0] = piece + add_all([errors[member] for member in range(NMP)])


def ortho_kernel(member_ref, place_ref, mine, theirs, acts_ref, split, tokens, panel):
    member = member_ref[0]
    for block in range(NMP // 2):
        panel[place_ref[member, block]] = mine[block] * (1.0 / NDP)
        panel[place_ref[member, NMP // 2 + block]] = theirs[block] * (1.0 / NDP)
    blocks, count = panel.shape[0], panel.shape[1]
    groups = count // 8

    def inner_of(index):
        first = index // 8
        sums = [None] * groups
        for block in range(blocks):
            row = panel[block, index : index + 1, :]
            for group in range(first, groups):
                term = panel[block, group * 8 : group * 8 + 8, :] * row
                sums[group] = term if sums[group] is None else sums[group] + term
        return [None if s is None else jnp.sum(s, axis=1, keepdims=True) for s in sums]

    order = lax.broadcasted_iota(jnp.int32, (8, 1), 0)
    for index in range(count):
        first, place = index // 8, index % 8
        inner = inner_of(index)
        scale = 1.0 / (jnp.sqrt(inner[first][place : place + 1, :]) + ortho_eps)
        weights = []
        for group in range(first, groups):
            weight = inner[group] * (scale * scale)
            if group == first:
                weight = jnp.where(order > place, weight, 0.0)
            weights.append(weight)
        for block in range(blocks):
            row = panel[block, index : index + 1, :]
            for group in range(first, groups):
                if group == first and place == 7:
                    continue
                rows = slice(group * 8, group * 8 + 8)
                panel[block, rows, :] = panel[block, rows, :] - weights[group - first] * row
            panel[block, index : index + 1, :] = row * scale
    for block in range(blocks):
        split[block] = split3(panel[block])
    tokens[...] = fold3(dot_nt(split[member], acts_ref[...]))


def errors_kernel(basis_ref, et_hbm, out, et_ref, sems):
    chunks, width = et_ref.shape[0], et_ref.shape[2]
    copies = [
        pltpu.make_async_copy(et_hbm.at[:, chunk * width : (chunk + 1) * width], et_ref.at[chunk], sems.at[chunk])
        for chunk in range(chunks)
    ]
    for copy in copies:
        copy.start()
    total = None
    for chunk in range(chunks):
        copies[chunk].wait()
        part = dot_nt(et_ref[chunk], wide(basis_ref, chunk, width))
        total = part if total is None else total + part
    out[...] = fold3(total.T)


def right_kernel(tokens, gt_ref, errors, out):
    out[...] = fold3(dot_nt(split3(tokens[...]), gt_ref[...])) + errors[...]


def wide(ref, chunk, width):
    count = width // LANES
    return jnp.concatenate([ref[chunk * count + block] for block in range(count)], axis=1)


def final_kernel(dp_ref, sum_ref, basis_ref, acts_hbm, et_hbm, gt_hbm, weight, moment1, moment2, new_weight, new_moment1,
                 new_moment2, new_error, q_new, acts_v, error_v, gt_v, updated, rounded, acts_sems, error_sems, sems):
    chunks, width = rounded.shape[0], rounded.shape[2]
    count = width // LANES
    gt_copy = pltpu.make_async_copy(gt_hbm, gt_v, sems.at[3])
    gt_copy.start()
    reads = []
    for chunk in range(chunks):
        blocks = pl.ds(chunk * count, count)
        columns = pl.ds(chunk * width, width)
        reads.append(pltpu.make_async_copy(acts_hbm.at[blocks], acts_v.at[blocks], acts_sems.at[chunk]))
        reads.append(pltpu.make_async_copy(et_hbm.at[:, columns], error_v.at[chunk], error_sems.at[chunk]))
    for copy in reads:
        copy.start()
    mean = sum_ref[...] * (1.0 / NDP)
    q_new[...] = mean
    rows, ff = mean.shape
    stack = split3(mean.T)
    hi, mid, lo = stack[:ff], stack[ff : 2 * ff], stack[2 * ff :]
    factor = jnp.concatenate([hi, hi, hi, mid, mid, lo], axis=1)

    def approx_of(chunk):
        basis = wide(basis_ref, chunk, width)
        hi, mid, lo = basis[:rows], basis[rows : 2 * rows], basis[2 * rows :]
        return dot_nn(factor, jnp.concatenate([hi, mid, lo, hi, mid, hi], axis=0))

    update = approx_of(dp_ref[0])
    first = beta_one * moment1[...] + (1.0 - beta_one) * update
    second = beta_two * moment2[...] + (1.0 - beta_two) * update * update
    updated[0] = first
    updated[1] = second
    updated[2] = weight[...] - learn_rate * (first / corr_one) / (jnp.sqrt(second / corr_two) + adam_eps)
    writes = [
        pltpu.make_async_copy(updated.at[0], new_moment1, sems.at[0]),
        pltpu.make_async_copy(updated.at[1], new_moment2, sems.at[1]),
        pltpu.make_async_copy(updated.at[2], new_weight, sems.at[2]),
    ]
    for copy in writes:
        copy.start()
    gt_copy.wait()

    def body(chunk, carry):
        blocks = pl.ds(chunk * count, count)
        pltpu.make_async_copy(acts_v.at[blocks], acts_v.at[blocks], acts_sems.at[chunk]).wait()
        pltpu.make_async_copy(error_v.at[chunk], error_v.at[chunk], error_sems.at[chunk]).wait()
        field = dot_nn(gt_v[...], wide(acts_v, chunk, width)) + error_v[chunk].astype(F32)
        rounded[chunk] = (field - approx_of(chunk)).astype(BF16)
        columns = pl.ds(pl.multiple_of(chunk * width, width), width)
        pltpu.make_async_copy(rounded.at[chunk], new_error.at[:, columns], error_sems.at[chunk]).start()
        return carry

    lax.fori_loop(0, chunks, body, 0)
    for copy in writes:
        copy.wait()
    for chunk in range(chunks):
        pltpu.make_async_copy(rounded.at[chunk], rounded.at[chunk], error_sems.at[chunk]).wait()


def call(kernel, outs, args, specs=None, out_specs=None, scratch=(), limit=16, flops=0, moved=0):
    return pl.pallas_call(
        kernel,
        out_shape=outs,
        in_specs=specs or [VMEM] * len(args),
        out_specs=out_specs or jax.tree.map(lambda _: VMEM, outs),
        scratch_shapes=scratch,
        compiler_params=pltpu.CompilerParams(vmem_limit_bytes=limit * MIB),
        cost_estimate=pl.CostEstimate(flops=flops, bytes_accessed=moved, transcendentals=0),
    )(*args)


def swap(value, axis, level):
    return lax.ppermute(value, axis, list(enumerate(level)))


def total(value, axis, levels):
    for level in levels:
        value = value + swap(value, axis, level)
    return value


def shards(acts, grad_out, error_buffer, q_prev, weight, moment1, moment2):
    member = lax.axis_index("mp").astype(jnp.int32).reshape(1)
    dp = lax.axis_index("dp").astype(jnp.int32).reshape(1)
    gt, et = grad_out.T, error_buffer.T
    rank, ff = q_prev.shape
    tokens, model = acts.shape[0], et.shape[1]
    chunks, width = 8, model // 8
    array = jax.ShapeDtypeStruct
    along = ALONG_Z + ALONG_X

    gathered = lax.all_gather(acts, "mp", axis=0)

    factor = call(
        token_kernel, array((rank, tokens), F32), (q_prev, gt), specs=[HBM] * 2,
        scratch=[pltpu.VMEM((rank, ff), F32), pltpu.VMEM((ff, tokens), BF16), pltpu.SemaphoreType.DMA((2,))],
        limit=60, flops=6 * rank * ff * tokens, moved=2 * ff * tokens,
    )
    factor, late = lax.optimization_barrier((factor, q_prev))
    errors = call(
        error_kernel, array((NMP, rank, LANES), F32), (late, et), specs=[HBM] * 2,
        scratch=[
            pltpu.VMEM((rank, ff), F32), pltpu.VMEM((chunks, ff, width), BF16), pltpu.SemaphoreType.DMA((9,)),
        ],
        limit=58, flops=6 * rank * ff * model, moved=2 * ff * model,
    )
    factor, errors = lax.optimization_barrier((total(factor, "mp", along[:1]), errors))
    errors = lax.all_to_all(errors, "mp", 0, 0)
    factor = total(factor, "mp", along[1:])

    panel = call(piece_kernel, array((1, rank, LANES), F32), (factor, acts, errors), moved=MIB)
    panel = total(panel, "dp", ALONG_DP)
    for level in along[:-1]:
        panel = jnp.concatenate([panel, swap(panel, "mp", level)])
    basis, factor = call(
        ortho_kernel, [array((NMP, 3 * rank, LANES), BF16), array((rank, tokens), F32)],
        (member, jnp.asarray(met(along, NMP)), panel, swap(panel, "mp", along[-1]), acts),
        specs=[SMEM, SMEM, VMEM, VMEM, VMEM],
        scratch=[pltpu.VMEM((NMP, rank, LANES), F32)], flops=MIB, moved=4 * MIB,
    )

    errors = call(
        errors_kernel, array((rank, ff), F32), (basis, et), specs=[VMEM, HBM],
        scratch=[pltpu.VMEM((chunks, ff, width), BF16), pltpu.SemaphoreType.DMA((chunks,))],
        limit=16, flops=6 * rank * ff * model, moved=2 * ff * model,
    )
    factor = total(factor, "mp", along)
    right = call(
        right_kernel, array((rank, ff), F32), (factor, gt, errors), flops=6 * rank * ff * tokens, moved=2 * ff * tokens
    )
    right = total(right, "dp", ALONG_DP)

    block = array((ff, width), F32)
    outs = call(
        final_kernel,
        [block] * 3 + [array((ff, model), BF16), array((rank, ff), F32)],
        (dp, right, basis, gathered, et, gt, weight.T, moment1.T, moment2.T),
        specs=[SMEM, VMEM, VMEM, HBM, HBM, HBM, VMEM, VMEM, VMEM],
        out_specs=[HBM] * 4 + [VMEM],
        scratch=[
            pltpu.VMEM((NMP, tokens, LANES), BF16),
            pltpu.VMEM((chunks, ff, width), BF16),
            pltpu.VMEM((ff, tokens), BF16),
            pltpu.VMEM((3, ff, width), F32),
            pltpu.VMEM((chunks, ff, width), BF16),
            pltpu.SemaphoreType.DMA((chunks,)),
            pltpu.SemaphoreType.DMA((chunks,)),
            pltpu.SemaphoreType.DMA((4,)),
        ],
        limit=56, flops=2 * model * ff * (tokens + 6 * rank), moved=22 * MIB,
    )
    new_weight, new_moment1, new_moment2, new_error, q_new = outs
    return (new_weight.T, new_moment1.T, new_moment2.T, new_error.T, q_new)


def solution(mesh):
    placed = (
        P("dp", "mp"),
        P("dp", "mp"),
        P("dp", "mp"),
        P(None, "mp"),
        P("dp", "mp"),
        P("dp", "mp"),
        P("dp", "mp"),
    )
    return jax.shard_map(
        shards,
        mesh=mesh,
        in_specs=placed,
        out_specs=(P("dp", "mp"), P("dp", "mp"), P("dp", "mp"), P("dp", "mp"), P(None, "mp")),
        check_vma=False,
    )
```

```python
import jax
import jax.numpy as jnp
import numpy as np
from jax import lax
from jax.experimental import pallas as pl
from jax.experimental.pallas import tpu as pltpu
from jax.sharding import PartitionSpec as P

ortho_eps = 1e-08
adam_eps = 1e-08
beta_one = 0.9
beta_two = 0.95
learn_rate = 0.01
corr_one = 1.0 - 0.9**10
corr_two = 1.0 - 0.95**10

NX, NZ, NDP = 4, 8, 8
NMP = NX * NZ
FACTOR = 32
LANES = 128
F32, BF16 = jnp.float32, jnp.bfloat16
MIB = 1 << 20
SMEM = pl.BlockSpec(memory_space=pltpu.SMEM)
VMEM = pl.BlockSpec(memory_space=pltpu.VMEM)
HBM = pl.BlockSpec(memory_space=pltpu.HBM)

RING4 = ([1, 0, 3, 2], [3, 2, 1, 0])
RING8 = ([1, 0, 3, 2, 5, 4, 7, 6], [7, 2, 1, 4, 3, 6, 5, 0], [3, 6, 5, 0, 7, 2, 1, 4])
ALONG_Z = [[x * NZ + to for x in range(NX) for to in level] for level in RING8]
ALONG_X = [[to * NZ + z for to in level for z in range(NZ)] for level in RING4]
ALONG_DP = [[1, 0, 3, 2, 5, 4, 7, 6]] + [[to * 2 + core for to in level for core in range(2)] for level in RING4]


def met(levels, members):
    held = [[member] for member in range(members)]
    for level in levels:
        held = [held[member] + held[level[member]] for member in range(members)]
    return np.array(held, np.int32)


def split3(value):
    hi = value.astype(BF16)
    rest = value - hi.astype(F32)
    mid = rest.astype(BF16)
    lo = (rest - mid.astype(F32)).astype(BF16)
    return jnp.concatenate([hi, mid, lo], axis=0)


def fold3(stacked):
    rows = stacked.shape[0] // 3
    return stacked[:rows] + (stacked[rows : 2 * rows] + stacked[2 * rows :])


def dot_nn(a, b):
    return lax.dot_general(a, b, (((1,), (0,)), ((), ())), preferred_element_type=F32)


def dot_nt(a, b):
    return lax.dot_general(a, b, (((1,), (1,)), ((), ())), preferred_element_type=F32)


def dot_tn(a, b):
    return lax.dot_general(a, b, (((0,), (0,)), ((), ())), preferred_element_type=F32)


def add_all(values):
    while len(values) > 1:
        values = [a + b for a, b in zip(values[::2], values[1::2])] + values[len(values) // 2 * 2 :]
    return values[0]


def lanes(array, block):
    return array[:, block * LANES : (block + 1) * LANES]


def wide(ref, count):
    return jnp.concatenate([ref[block] for block in range(count)], axis=1)


def lanes(array, block):
    return array[:, block * LANES : (block + 1) * LANES]


def add_all(values):
    while len(values) > 1:
        values = [a + b for a, b in zip(values[::2], values[1::2])]
    return values[0]


def tiles_of(value, out):
    columns = value.shape[1] // LANES
    for row in range(value.shape[0] // 8):
        for column in range(columns):
            out[row * columns + column] = lanes(value[row * 8 : row * 8 + 8], column)


def rows_of(tiles, column, columns, rows):
    return jnp.concatenate([tiles[row * columns + column] for row in range(rows // 8)], axis=0)


def error_kernel(member_ref, core_ref, place_ref, q_hbm, et_hbm, keep, send, q_ref, et_ref, parts, sems):
    count, width = et_ref.shape[0], et_ref.shape[2]
    copies = [
        pltpu.make_async_copy(et_hbm.at[:, chunk * width : (chunk + 1) * width], et_ref.at[chunk], sems.at[chunk])
        for chunk in range(count)
    ]
    first = pltpu.make_async_copy(q_hbm, q_ref, sems.at[count])
    first.start()
    for copy in copies:
        copy.start()
    first.wait()
    split = split3(q_ref[...])
    blocks = width // LANES
    half = parts.shape[1] // 2
    for chunk in range(count):
        copies[chunk].wait()
        part = fold3(dot_nn(split, et_ref[chunk]))
        for block in range(blocks):
            parts[chunk * blocks + block] = lanes(part, block)
    lower = core_ref[0] == 0
    for place in range(NMP):
        block = parts[place_ref[member_ref[0], place]]
        keep[place] = jnp.where(lower, block[:half], block[half:])
        send[place] = jnp.where(lower, block[half:], block[:half])


def token_kernel(q_hbm, gt_hbm, out, q_ref, gt_ref, sems):
    copies = [pltpu.make_async_copy(q_hbm, q_ref, sems.at[0]), pltpu.make_async_copy(gt_hbm, gt_ref, sems.at[1])]
    for copy in copies:
        copy.start()
    for copy in copies:
        copy.wait()
    tiles_of(fold3(dot_nn(split3(q_ref[...]), gt_ref[...])), out)


def store_blocks(value, out, start):
    for block in range(value.shape[0]):
        out[start + 2 * block] = value[block, :8]
        out[start + 2 * block + 1] = value[block, 8:]


def load_blocks(ref, start, count):
    return jnp.stack(
        [jnp.concatenate([ref[start + 2 * block], ref[start + 2 * block + 1]], axis=0) for block in range(count)]
    )


def open_kernel(tokens, mine, theirs, message, keep):
    message[:FACTOR] = tokens[...]
    both = mine[...] + theirs[...]
    half = both.shape[0] // 2
    keep[...] = both[:half]
    store_blocks(both[half:], message, FACTOR)


def halve_kernel(sent, kept, came, message, keep):
    message[:FACTOR] = sent[:FACTOR] + came[:FACTOR]
    count = kept.shape[0]
    both = kept[...] + load_blocks(came, FACTOR, count)
    keep[...] = both[: count // 2]
    store_blocks(both[count // 2 :], message, FACTOR)


def piece_kernel(core_ref, acts_ref, sent, kept, came, keep, send):
    blocks = acts_ref.shape[0] // LANES
    terms = []
    for block in range(blocks):
        factor = rows_of(sent, block, blocks, FACTOR) + rows_of(came, block, blocks, FACTOR)
        terms.append(dot_nn(split3(factor), acts_ref[block * LANES : (block + 1) * LANES, :]))
    while len(terms) > 1:
        terms = [a + b for a, b in zip(terms[::2], terms[1::2])]
    piece = fold3(terms[0])
    half = piece.shape[0] // 2
    lower = core_ref[0] == 0
    keep[...] = jnp.where(lower, piece[:half], piece[half:]) + (kept[...] + load_blocks(came, FACTOR, 1))[0]
    send[...] = jnp.where(lower, piece[half:], piece[:half])


def start_kernel(core_ref, mine, theirs, acts_ref, message):
    lower = core_ref[0] == 0
    first, second = mine[...] * (1.0 / NDP), theirs[...] * (1.0 / NDP)
    panel = jnp.concatenate([jnp.where(lower, first, second), jnp.where(lower, second, first)], axis=0)
    tiles_of(fold3(dot_nt(split3(panel), acts_ref[...])), message)
    store_blocks(first[None], message, FACTOR)


def double_kernel(sent, came, message):
    count = sent.shape[0] - FACTOR
    message[:FACTOR] = sent[:FACTOR] + came[:FACTOR]
    message[FACTOR : FACTOR + count] = sent[FACTOR:]
    message[FACTOR + count :] = came[FACTOR:]


def last_kernel(sent, came, factor, rows):
    count = sent.shape[0] - FACTOR
    factor[...] = sent[:FACTOR] + came[:FACTOR]
    rows[:count] = sent[FACTOR:]
    rows[count:] = came[FACTOR:]


def ortho_kernel(member_ref, core_ref, place_ref, mine, theirs, tokens, gt_ref, et_hbm, split, right, panel, et_ref, sems):
    chunks, width = et_ref.shape[0], et_ref.shape[2]
    copies = [
        pltpu.make_async_copy(et_hbm.at[:, chunk * width : (chunk + 1) * width], et_ref.at[chunk], sems.at[chunk])
        for chunk in range(chunks)
    ]
    for copy in copies:
        copy.start()
    member = member_ref[0]
    lower = core_ref[0] == 0
    half = panel.shape[1] // 2
    for place in range(NMP):
        first = jnp.concatenate([mine[2 * place], mine[2 * place + 1]], axis=0)
        second = jnp.concatenate([theirs[2 * place], theirs[2 * place + 1]], axis=0)
        block = place_ref[member, place]
        panel[block, :half] = jnp.where(lower, first, second)
        panel[block, half:] = jnp.where(lower, second, first)
    square = panel.shape[1:]
    same = lax.broadcasted_iota(jnp.int32, square, 0) == lax.broadcasted_iota(jnp.int32, square, 1)
    panel[NMP] = jnp.where(same, 1.0, 0.0)
    blocks, count = NMP, panel.shape[1]
    groups = count // 8

    def inner_of(index):
        first = index // 8
        sums = [None] * groups
        for block in range(blocks):
            row = panel[block, index : index + 1, :]
            for group in range(first, groups):
                term = panel[block, group * 8 : group * 8 + 8, :] * row
                sums[group] = term if sums[group] is None else sums[group] + term
        return [None if s is None else jnp.sum(s, axis=1, keepdims=True) for s in sums]

    order = lax.broadcasted_iota(jnp.int32, (8, 1), 0)
    for index in range(count):
        first, place = index // 8, index % 8
        inner = inner_of(index)
        scale = 1.0 / (jnp.sqrt(inner[first][place : place + 1, :]) + ortho_eps)
        weights = []
        for group in range(first, groups):
            weight = inner[group] * (scale * scale)
            if group == first:
                weight = jnp.where(order > place, weight, 0.0)
            weights.append(weight)
        for block in range(blocks + 1):
            row = panel[block, index : index + 1, :]
            for group in range(first, groups):
                if group == first and place == 7:
                    continue
                rows = slice(group * 8, group * 8 + 8)
                panel[block, rows, :] = panel[block, rows, :] - weights[group - first] * row
            panel[block, index : index + 1, :] = row * scale
    for block in range(blocks):
        split[block] = split3(panel[block])
    columns = gt_ref.shape[1] // LANES
    factor = jnp.concatenate([rows_of(tokens, column, columns, FACTOR) for column in range(columns)], axis=1)
    grads = fold3(dot_nt(split3(factor), gt_ref[...]))
    total = None
    for chunk in range(chunks):
        copies[chunk].wait()
        part = dot_nt(et_ref[chunk], wide(split, chunk, width))
        total = part if total is None else total + part
    turned = lax.dot_general(
        panel[NMP][:, :count], grads, (((1,), (0,)), ((), ())), precision=lax.Precision.HIGHEST,
        preferred_element_type=F32,
    )
    right[...] = turned + fold3(total.T)


def wide(ref, count):
    return jnp.concatenate([ref[block] for block in range(count)], axis=1)


def lanes(array, block):
    return array[:, block * LANES : (block + 1) * LANES]


def add_all(values):
    while len(values) > 1:
        values = [a + b for a, b in zip(values[::2], values[1::2])]
    return values[0]


def tiles_of(value, out):
    columns = value.shape[1] // LANES
    for row in range(value.shape[0] // 8):
        for column in range(columns):
            out[row * columns + column] = lanes(value[row * 8 : row * 8 + 8], column)


def rows_of(tiles, column, columns, rows):
    return jnp.concatenate([tiles[row * columns + column] for row in range(rows // 8)], axis=0)


def error_kernel(member_ref, core_ref, place_ref, q_hbm, et_hbm, keep, send, q_ref, et_ref, parts, sems):
    count, width = et_ref.shape[0], et_ref.shape[2]
    copies = [
        pltpu.make_async_copy(et_hbm.at[:, chunk * width : (chunk + 1) * width], et_ref.at[chunk], sems.at[chunk])
        for chunk in range(count)
    ]
    first = pltpu.make_async_copy(q_hbm, q_ref, sems.at[count])
    first.start()
    for copy in copies:
        copy.start()
    first.wait()
    split = split3(q_ref[...])
    blocks = width // LANES
    half = parts.shape[1] // 2
    for chunk in range(count):
        copies[chunk].wait()
        part = fold3(dot_nn(split, et_ref[chunk]))
        for block in range(blocks):
            parts[chunk * blocks + block] = lanes(part, block)
    lower = core_ref[0] == 0
    for place in range(NMP):
        block = parts[place_ref[member_ref[0], place]]
        keep[place] = jnp.where(lower, block[:half], block[half:])
        send[place] = jnp.where(lower, block[half:], block[:half])


def token_kernel(q_hbm, gt_hbm, out, q_ref, gt_ref, sems):
    copies = [pltpu.make_async_copy(q_hbm, q_ref, sems.at[0]), pltpu.make_async_copy(gt_hbm, gt_ref, sems.at[1])]
    for copy in copies:
        copy.start()
    for copy in copies:
        copy.wait()
    tiles_of(fold3(dot_nn(split3(q_ref[...]), gt_ref[...])), out)


def store_blocks(value, out, start):
    for block in range(value.shape[0]):
        out[start + 2 * block] = value[block, :8]
        out[start + 2 * block + 1] = value[block, 8:]


def load_blocks(ref, start, count):
    return jnp.stack(
        [jnp.concatenate([ref[start + 2 * block], ref[start + 2 * block + 1]], axis=0) for block in range(count)]
    )


def open_kernel(tokens, mine, theirs, message, keep):
    message[:FACTOR] = tokens[...]
    both = mine[...] + theirs[...]
    half = both.shape[0] // 2
    keep[...] = both[:half]
    store_blocks(both[half:], message, FACTOR)


def halve_kernel(sent, kept, came, message, keep):
    message[:FACTOR] = sent[:FACTOR] + came[:FACTOR]
    count = kept.shape[0]
    both = kept[...] + load_blocks(came, FACTOR, count)
    keep[...] = both[: count // 2]
    store_blocks(both[count // 2 :], message, FACTOR)


def piece_kernel(core_ref, acts_ref, sent, kept, came, keep, send):
    blocks = acts_ref.shape[0] // LANES
    terms = []
    for block in range(blocks):
        factor = rows_of(sent, block, blocks, FACTOR) + rows_of(came, block, blocks, FACTOR)
        terms.append(dot_nn(split3(factor), acts_ref[block * LANES : (block + 1) * LANES, :]))
    while len(terms) > 1:
        terms = [a + b for a, b in zip(terms[::2], terms[1::2])]
    piece = fold3(terms[0])
    half = piece.shape[0] // 2
    lower = core_ref[0] == 0
    keep[...] = jnp.where(lower, piece[:half], piece[half:]) + (kept[...] + load_blocks(came, FACTOR, 1))[0]
    send[...] = jnp.where(lower, piece[half:], piece[:half])


def start_kernel(core_ref, mine, theirs, acts_ref, message):
    lower = core_ref[0] == 0
    first, second = mine[...] * (1.0 / NDP), theirs[...] * (1.0 / NDP)
    panel = jnp.concatenate([jnp.where(lower, first, second), jnp.where(lower, second, first)], axis=0)
    tiles_of(fold3(dot_nt(split3(panel), acts_ref[...])), message)
    store_blocks(first[None], message, FACTOR)


def double_kernel(sent, came, message):
    count = sent.shape[0] - FACTOR
    message[:FACTOR] = sent[:FACTOR] + came[:FACTOR]
    message[FACTOR : FACTOR + count] = sent[FACTOR:]
    message[FACTOR + count :] = came[FACTOR:]


def last_kernel(sent, came, factor, rows):
    count = sent.shape[0] - FACTOR
    factor[...] = sent[:FACTOR] + came[:FACTOR]
    rows[:count] = sent[FACTOR:]
    rows[count:] = came[FACTOR:]


def ortho_kernel(member_ref, core_ref, place_ref, mine, theirs, tokens, gt_ref, et_hbm, split, right, panel, et_ref, sems):
    chunks, width = et_ref.shape[0], et_ref.shape[2]
    copies = [
        pltpu.make_async_copy(et_hbm.at[:, chunk * width : (chunk + 1) * width], et_ref.at[chunk], sems.at[chunk])
        for chunk in range(chunks)
    ]
    for copy in copies:
        copy.start()
    member = member_ref[0]
    lower = core_ref[0] == 0
    half = panel.shape[1] // 2
    for place in range(NMP):
        first = jnp.concatenate([mine[2 * place], mine[2 * place + 1]], axis=0)
        second = jnp.concatenate([theirs[2 * place], theirs[2 * place + 1]], axis=0)
        block = place_ref[member, place]
        panel[block, :half] = jnp.where(lower, first, second)
        panel[block, half:] = jnp.where(lower, second, first)
    square = panel.shape[1:]
    same = lax.broadcasted_iota(jnp.int32, square, 0) == lax.broadcasted_iota(jnp.int32, square, 1)
    panel[NMP] = jnp.where(same, 1.0, 0.0)
    blocks, count = NMP, panel.shape[1]
    groups = count // 8

    def inner_of(index):
        first = index // 8
        sums = [None] * groups
        for block in range(blocks):
            row = panel[block, index : index + 1, :]
            for group in range(first, groups):
                term = panel[block, group * 8 : group * 8 + 8, :] * row
                sums[group] = term if sums[group] is None else sums[group] + term
        return [None if s is None else jnp.sum(s, axis=1, keepdims=True) for s in sums]

    order = lax.broadcasted_iota(jnp.int32, (8, 1), 0)
    for index in range(count):
        first, place = index // 8, index % 8
        inner = inner_of(index)
        scale = 1.0 / (jnp.sqrt(inner[first][place : place + 1, :]) + ortho_eps)
        weights = []
        for group in range(first, groups):
            weight = inner[group] * (scale * scale)
            if group == first:
                weight = jnp.where(order > place, weight, 0.0)
            weights.append(weight)
        for block in range(blocks + 1):
            row = panel[block, index : index + 1, :]
            for group in range(first, groups):
                if group == first and place == 7:
                    continue
                rows = slice(group * 8, group * 8 + 8)
                panel[block, rows, :] = panel[block, rows, :] - weights[group - first] * row
            panel[block, index : index + 1, :] = row * scale
    for block in range(blocks):
        split[block] = split3(panel[block])
    columns = gt_ref.shape[1] // LANES
    factor = jnp.concatenate([rows_of(tokens, column, columns, FACTOR) for column in range(columns)], axis=1)
    grads = fold3(dot_nt(split3(factor), gt_ref[...]))
    total = None
    for chunk in range(chunks):
        copies[chunk].wait()
        part = dot_nt(et_ref[chunk], wide(split, chunk, width))
        total = part if total is None else total + part
    turned = lax.dot_general(
        panel[NMP][:, :count], grads, (((1,), (0,)), ((), ())), precision=lax.Precision.HIGHEST,
        preferred_element_type=F32,
    )
    right[...] = turned + fold3(total.T)


def errors_kernel(basis_ref, et_hbm, out, et_ref, sems):
    chunks, width = et_ref.shape[0], et_ref.shape[2]
    copies = [
        pltpu.make_async_copy(et_hbm.at[:, chunk * width : (chunk + 1) * width], et_ref.at[chunk], sems.at[chunk])
        for chunk in range(chunks)
    ]
    for copy in copies:
        copy.start()
    total = None
    for chunk in range(chunks):
        copies[chunk].wait()
        part = dot_nt(et_ref[chunk], wide(basis_ref, chunk, width))
        total = part if total is None else total + part
    out[...] = fold3(total.T)


def right_kernel(tokens, gt_ref, errors, out):
    out[...] = fold3(dot_nt(split3(tokens[...]), gt_ref[...])) + errors[...]


def wide(ref, chunk, width):
    count = width // LANES
    return jnp.concatenate([ref[chunk * count + block] for block in range(count)], axis=1)


def final_kernel(dp_ref, sum_ref, basis_ref, acts_hbm, et_hbm, gt_hbm, weight, moment1, moment2, new_weight, new_moment1,
                 new_moment2, new_error, q_new, acts_v, error_v, gt_v, updated, rounded, acts_sems, error_sems, sems):
    chunks, width = rounded.shape[0], rounded.shape[2]
    count = width // LANES
    gt_copy = pltpu.make_async_copy(gt_hbm, gt_v, sems.at[3])
    gt_copy.start()
    reads = []
    for chunk in range(chunks):
        blocks = pl.ds(chunk * count, count)
        columns = pl.ds(chunk * width, width)
        reads.append(pltpu.make_async_copy(acts_hbm.at[blocks], acts_v.at[blocks], acts_sems.at[chunk]))
        reads.append(pltpu.make_async_copy(et_hbm.at[:, columns], error_v.at[chunk], error_sems.at[chunk]))
    for copy in reads:
        copy.start()
    mean = sum_ref[...] * (1.0 / NDP)
    q_new[...] = mean
    rows, ff = mean.shape
    stack = split3(mean.T)
    hi, mid, lo = stack[:ff], stack[ff : 2 * ff], stack[2 * ff :]
    factor = jnp.concatenate([hi, hi, hi, mid, mid, lo], axis=1)

    def approx_of(chunk):
        basis = wide(basis_ref, chunk, width)
        hi, mid, lo = basis[:rows], basis[rows : 2 * rows], basis[2 * rows :]
        return dot_nn(factor, jnp.concatenate([hi, mid, lo, hi, mid, hi], axis=0))

    update = approx_of(dp_ref[0])
    first = beta_one * moment1[...] + (1.0 - beta_one) * update
    second = beta_two * moment2[...] + (1.0 - beta_two) * update * update
    updated[0] = first
    updated[1] = second
    updated[2] = weight[...] - learn_rate * (first / corr_one) / (jnp.sqrt(second / corr_two) + adam_eps)
    writes = [
        pltpu.make_async_copy(updated.at[0], new_moment1, sems.at[0]),
        pltpu.make_async_copy(updated.at[1], new_moment2, sems.at[1]),
        pltpu.make_async_copy(updated.at[2], new_weight, sems.at[2]),
    ]
    for copy in writes:
        copy.start()
    gt_copy.wait()

    def body(chunk, carry):
        blocks = pl.ds(chunk * count, count)
        pltpu.make_async_copy(acts_v.at[blocks], acts_v.at[blocks], acts_sems.at[chunk]).wait()
        pltpu.make_async_copy(error_v.at[chunk], error_v.at[chunk], error_sems.at[chunk]).wait()
        field = dot_nn(gt_v[...], wide(acts_v, chunk, width)) + error_v[chunk].astype(F32)
        rounded[chunk] = (field - approx_of(chunk)).astype(BF16)
        columns = pl.ds(pl.multiple_of(chunk * width, width), width)
        pltpu.make_async_copy(rounded.at[chunk], new_error.at[:, columns], error_sems.at[chunk]).start()
        return carry

    lax.fori_loop(0, chunks, body, 0)
    for copy in writes:
        copy.wait()
    for chunk in range(chunks):
        pltpu.make_async_copy(rounded.at[chunk], rounded.at[chunk], error_sems.at[chunk]).wait()


def call(kernel, outs, args, specs=None, out_specs=None, scratch=(), limit=16, flops=0, moved=0):
    return pl.pallas_call(
        kernel,
        out_shape=outs,
        in_specs=specs or [VMEM] * len(args),
        out_specs=out_specs or jax.tree.map(lambda _: VMEM, outs),
        scratch_shapes=scratch,
        compiler_params=pltpu.CompilerParams(vmem_limit_bytes=limit * MIB),
        cost_estimate=pl.CostEstimate(flops=flops, bytes_accessed=moved, transcendentals=0),
    )(*args)


def swap(value, axis, level):
    return lax.ppermute(value, axis, list(enumerate(level)))


def total(value, axis, levels):
    for level in levels:
        value = value + swap(value, axis, level)
    return value


def shards(acts, grad_out, error_buffer, q_prev, weight, moment1, moment2):
    member = lax.axis_index("mp").astype(jnp.int32).reshape(1)
    dp = lax.axis_index("dp").astype(jnp.int32).reshape(1)
    core = dp % 2
    gt, et = grad_out.T, error_buffer.T
    rank, ff = q_prev.shape
    tokens, model = acts.shape[0], et.shape[1]
    chunks, width = 8, model // 8
    array = jax.ShapeDtypeStruct
    along = ALONG_Z + ALONG_X

    gathered = lax.all_gather(acts, "mp", axis=0)

    half = rank // 2
    table = jnp.asarray(met(along, NMP))
    blocks = array((NMP, half, LANES), F32)
    mine, send = call(
        error_kernel, [blocks, blocks], (member, core, table, q_prev, et), specs=[SMEM] * 3 + [HBM] * 2,
        scratch=[
            pltpu.VMEM((rank, ff), F32), pltpu.VMEM((chunks, ff, width), BF16), pltpu.VMEM((NMP, rank, LANES), F32),
            pltpu.SemaphoreType.DMA((chunks + 1,)),
        ],
        limit=60, flops=6 * rank * ff * model, moved=2 * ff * model,
    )
    theirs = swap(send, "dp", ALONG_DP[0])
    factor = call(
        token_kernel, array((FACTOR, 8, LANES), F32), (q_prev, gt), specs=[HBM] * 2,
        scratch=[pltpu.VMEM((rank, ff), F32), pltpu.VMEM((ff, tokens), BF16), pltpu.SemaphoreType.DMA((2,))],
        limit=58, flops=6 * rank * ff * tokens, moved=2 * ff * tokens,
    )
    count = NMP // 2
    message = lambda tiles: array((FACTOR + tiles, 8, LANES), F32)
    kept = lambda count: array((count, half, LANES), F32)
    sent, keep = call(open_kernel, [message(2 * count), kept(count)], (factor, mine, theirs), moved=MIB)
    for level in along[:0:-1]:
        came = swap(sent, "mp", level)
        count //= 2
        sent, keep = call(halve_kernel, [message(2 * count), kept(count)], (sent, keep, came), moved=MIB)
    came = swap(sent, "mp", along[0])

    piece = array((half, LANES), F32)
    keep, send = call(
        piece_kernel, [piece, piece], (core, acts, sent, keep, came), specs=[SMEM] + [VMEM] * 4, moved=MIB
    )
    keep = total(keep + swap(send, "dp", ALONG_DP[0]), "dp", ALONG_DP[1:])
    sent = call(
        start_kernel, message(2), (core, keep, swap(keep, "dp", ALONG_DP[0]), acts), specs=[SMEM] + [VMEM] * 3, moved=MIB
    )
    for place, level in enumerate(along[:-1]):
        sent = call(double_kernel, message(4 << place), (sent, swap(sent, "mp", level)), moved=MIB)
    factor, mine = call(
        last_kernel, [array((FACTOR, 8, LANES), F32), array((2 * NMP, 8, LANES), F32)],
        (sent, swap(sent, "mp", along[-1])), moved=MIB,
    )
    basis, right = call(
        ortho_kernel, [array((NMP, 3 * rank, LANES), BF16), array((rank, ff), F32)],
        (member, core, table, mine, swap(mine, "dp", ALONG_DP[0]), factor, gt, et),
        specs=[SMEM] * 3 + [VMEM] * 4 + [HBM],
        scratch=[
            pltpu.VMEM((NMP + 1, rank, LANES), F32),
            pltpu.VMEM((chunks, ff, width), BF16),
            pltpu.SemaphoreType.DMA((chunks,)),
        ],
        limit=24, flops=8 * rank * ff * model, moved=2 * ff * model,
    )
    right = total(right, "dp", ALONG_DP)

    block = array((ff, width), F32)
    outs = call(
        final_kernel,
        [block] * 3 + [array((ff, model), BF16), array((rank, ff), F32)],
        (dp, right, basis, gathered, et, gt, weight.T, moment1.T, moment2.T),
        specs=[SMEM, VMEM, VMEM, HBM, HBM, HBM, VMEM, VMEM, VMEM],
        out_specs=[HBM] * 4 + [VMEM],
        scratch=[
            pltpu.VMEM((NMP, tokens, LANES), BF16),
            pltpu.VMEM((chunks, ff, width), BF16),
            pltpu.VMEM((ff, tokens), BF16),
            pltpu.VMEM((3, ff, width), F32),
            pltpu.VMEM((chunks, ff, width), BF16),
            pltpu.SemaphoreType.DMA((chunks,)),
            pltpu.SemaphoreType.DMA((chunks,)),
            pltpu.SemaphoreType.DMA((4,)),
        ],
        limit=56, flops=2 * model * ff * (tokens + 6 * rank), moved=22 * MIB,
    )
    new_weight, new_moment1, new_moment2, new_error, q_new = outs
    return (new_weight.T, new_moment1.T, new_moment2.T, new_error.T, q_new)


def solution(mesh):
    placed = (
        P("dp", "mp"),
        P("dp", "mp"),
        P("dp", "mp"),
        P(None, "mp"),
        P("dp", "mp"),
        P("dp", "mp"),
        P("dp", "mp"),
    )
    return jax.shard_map(
        shards,
        mesh=mesh,
        in_specs=placed,
        out_specs=(P("dp", "mp"), P("dp", "mp"), P("dp", "mp"), P("dp", "mp"), P(None, "mp")),
        check_vma=False,
    )
```

```python
import functools

import jax
import jax.numpy as jnp
import numpy as np
from jax import lax
from jax.experimental import pallas as pl
from jax.experimental.pallas import tpu as pltpu
from jax.sharding import PartitionSpec as P

ortho_eps = 1e-08
adam_eps = 1e-08
beta_one = 0.9
beta_two = 0.95
learn_rate = 0.01
corr_one = 1.0 - 0.9**10
corr_two = 1.0 - 0.95**10

NX, NZ, NDP = 4, 8, 8
NMP = NX * NZ
FACTOR = 32
LANES = 128
F32, BF16 = jnp.float32, jnp.bfloat16
MIB = 1 << 20
SMEM = pl.BlockSpec(memory_space=pltpu.SMEM)
VMEM = pl.BlockSpec(memory_space=pltpu.VMEM)
HBM = pl.BlockSpec(memory_space=pltpu.HBM)

RING4 = ([1, 0, 3, 2], [3, 2, 1, 0])
RING8 = ([3, 6, 5, 0, 7, 2, 1, 4], [7, 2, 1, 4, 3, 6, 5, 0], [1, 0, 3, 2, 5, 4, 7, 6])
ALONG_Z = [[x * NZ + to for x in range(NX) for to in level] for level in RING8]
ALONG_X = [[to * NZ + z for to in level for z in range(NZ)] for level in RING4]
ALONG_DP = [[1, 0, 3, 2, 5, 4, 7, 6]] + [[to * 2 + core for to in level for core in range(2)] for level in RING4]


def met(levels, members):
    held = [[member] for member in range(members)]
    for level in levels:
        held = [held[member] + held[level[member]] for member in range(members)]
    return np.array(held, np.int32)


def split3(value):
    hi = value.astype(BF16)
    rest = value - hi.astype(F32)
    mid = rest.astype(BF16)
    lo = (rest - mid.astype(F32)).astype(BF16)
    return jnp.concatenate([hi, mid, lo], axis=0)


def fold3(stacked):
    rows = stacked.shape[0] // 3
    return stacked[:rows] + (stacked[rows : 2 * rows] + stacked[2 * rows :])


def dot_nn(a, b):
    return lax.dot_general(a, b, (((1,), (0,)), ((), ())), preferred_element_type=F32)


def dot_nt(a, b):
    return lax.dot_general(a, b, (((1,), (1,)), ((), ())), preferred_element_type=F32)


def dot_tn(a, b):
    return lax.dot_general(a, b, (((0,), (0,)), ((), ())), preferred_element_type=F32)


def add_all(values):
    while len(values) > 1:
        values = [a + b for a, b in zip(values[::2], values[1::2])] + values[len(values) // 2 * 2 :]
    return values[0]


def lanes(array, block):
    return array[:, block * LANES : (block + 1) * LANES]


def tiles_of(value, out):
    columns = value.shape[1] // LANES
    for row in range(value.shape[0] // 8):
        for column in range(columns):
            out[row * columns + column] = lanes(value[row * 8 : row * 8 + 8], column)


def rows_of(tiles, column, columns, rows):
    return jnp.concatenate([tiles[row * columns + column] for row in range(rows // 8)], axis=0)


def error_kernel(member_ref, core_ref, place_ref, q_hbm, et_hbm, keep, send, q_ref, et_ref, parts, sems):
    count, width = et_ref.shape[0], et_ref.shape[2]
    copies = [
        pltpu.make_async_copy(et_hbm.at[:, chunk * width : (chunk + 1) * width], et_ref.at[chunk], sems.at[chunk])
        for chunk in range(count)
    ]
    first = pltpu.make_async_copy(q_hbm, q_ref, sems.at[count])
    first.start()
    for copy in copies:
        copy.start()
    first.wait()
    split = split3(q_ref[...])
    blocks = width // LANES
    half = parts.shape[1] // 2
    for chunk in range(count):
        copies[chunk].wait()
        part = fold3(dot_nn(split, et_ref[chunk]))
        for block in range(blocks):
            parts[chunk * blocks + block] = lanes(part, block)
    lower = core_ref[0] == 0
    for place in range(NMP):
        block = parts[place_ref[member_ref[0], place]]
        keep[place] = jnp.where(lower, block[:half], block[half:])
        send[place] = jnp.where(lower, block[half:], block[:half])


def token_kernel(q_hbm, gt_hbm, out, q_ref, gt_ref, sems):
    copies = [pltpu.make_async_copy(q_hbm, q_ref, sems.at[0]), pltpu.make_async_copy(gt_hbm, gt_ref, sems.at[1])]
    for copy in copies:
        copy.start()
    for copy in copies:
        copy.wait()
    tiles_of(fold3(dot_nn(split3(q_ref[...]), gt_ref[...])), out)


def store_blocks(value, out, start):
    for block in range(value.shape[0]):
        out[start + 2 * block] = value[block, :8]
        out[start + 2 * block + 1] = value[block, 8:]


def load_blocks(ref, start, count):
    return jnp.stack(
        [jnp.concatenate([ref[start + 2 * block], ref[start + 2 * block + 1]], axis=0) for block in range(count)]
    )


def open_kernel(tokens, mine, theirs, message, keep):
    message[:FACTOR] = tokens[...]
    both = mine[...] + theirs[...]
    half = both.shape[0] // 2
    keep[...] = both[:half]
    store_blocks(both[half:], message, FACTOR)


def halve_kernel(sent, kept, came, message, keep):
    message[:FACTOR] = sent[:FACTOR] + came[:FACTOR]
    count = kept.shape[0]
    both = kept[...] + load_blocks(came, FACTOR, count)
    keep[...] = both[: count // 2]
    store_blocks(both[count // 2 :], message, FACTOR)


def piece_kernel(core_ref, sent, kept, came, *refs):
    acts_refs, keep, send = refs[:NX], refs[NX], refs[NX + 1]
    blocks = acts_refs[0].shape[0] // LANES
    half = keep.shape[1]
    lower = core_ref[0] == 0
    errors = kept[...] + load_blocks(came, FACTOR, NX)
    factors = []
    for block in range(blocks):
        factors.append(split3(rows_of(sent, block, blocks, FACTOR) + rows_of(came, block, blocks, FACTOR)))
    factor = jnp.concatenate(factors, axis=1)
    for place in range(NX):
        piece = fold3(dot_nn(factor, acts_refs[place][...]))
        keep[place] = jnp.where(lower, piece[:half], piece[half:]) + errors[place]
        send[place] = jnp.where(lower, piece[half:], piece[:half])


def start_kernel(core_ref, mine, theirs, *refs):
    acts_refs, message = refs[:NX], refs[NX]
    lower = core_ref[0] == 0
    total = None
    for place in range(NX):
        first, second = mine[place] * (1.0 / NDP), theirs[place] * (1.0 / NDP)
        panel = jnp.concatenate([jnp.where(lower, first, second), jnp.where(lower, second, first)], axis=0)
        part = dot_nt(split3(panel), acts_refs[place][...])
        total = part if total is None else total + part
    tiles_of(fold3(total), message)
    store_blocks(mine[...] * (1.0 / NDP), message, FACTOR)


def double_kernel(sent, came, message):
    count = sent.shape[0] - FACTOR
    message[:FACTOR] = sent[:FACTOR] + came[:FACTOR]
    message[FACTOR : FACTOR + count] = sent[FACTOR:]
    message[FACTOR + count :] = came[FACTOR:]


def last_kernel(sent, came, factor, rows):
    count = sent.shape[0] - FACTOR
    factor[...] = sent[:FACTOR] + came[:FACTOR]
    rows[:count] = sent[FACTOR:]
    rows[count:] = came[FACTOR:]


def ortho_kernel(member_ref, core_ref, place_ref, mine, theirs, tokens, gt_ref, et_hbm, split, right, panel, et_ref, sems):
    chunks, width = et_ref.shape[0], et_ref.shape[2]
    copies = [
        pltpu.make_async_copy(et_hbm.at[:, chunk * width : (chunk + 1) * width], et_ref.at[chunk], sems.at[chunk])
        for chunk in range(chunks)
    ]
    for copy in copies:
        copy.start()
    member = member_ref[0]
    lower = core_ref[0] == 0
    half = panel.shape[1] // 2
    for place in range(NMP):
        first = jnp.concatenate([mine[2 * place], mine[2 * place + 1]], axis=0)
        second = jnp.concatenate([theirs[2 * place], theirs[2 * place + 1]], axis=0)
        block = place_ref[member, place]
        panel[block, :half] = jnp.where(lower, first, second)
        panel[block, half:] = jnp.where(lower, second, first)
    square = panel.shape[1:]
    same = lax.broadcasted_iota(jnp.int32, square, 0) == lax.broadcasted_iota(jnp.int32, square, 1)
    panel[NMP] = jnp.where(same, 1.0, 0.0)
    blocks, count = NMP, panel.shape[1]
    groups = count // 8

    def inner_of(index):
        first = index // 8
        sums = [None] * groups
        for block in range(blocks):
            row = panel[block, index : index + 1, :]
            for group in range(first, groups):
                term = panel[block, group * 8 : group * 8 + 8, :] * row
                sums[group] = term if sums[group] is None else sums[group] + term
        return [None if s is None else jnp.sum(s, axis=1, keepdims=True) for s in sums]

    order = lax.broadcasted_iota(jnp.int32, (8, 1), 0)
    for index in range(count):
        first, place = index // 8, index % 8
        inner = inner_of(index)
        scale = 1.0 / (jnp.sqrt(inner[first][place : place + 1, :]) + ortho_eps)
        weights = []
        for group in range(first, groups):
            weight = inner[group] * (scale * scale)
            if group == first:
                weight = jnp.where(order > place, weight, 0.0)
            weights.append(weight)
        for block in range(blocks + 1):
            row = panel[block, index : index + 1, :]
            for group in range(first, groups):
                if group == first and place == 7:
                    continue
                rows = slice(group * 8, group * 8 + 8)
                panel[block, rows, :] = panel[block, rows, :] - weights[group - first] * row
            panel[block, index : index + 1, :] = row * scale
    for block in range(blocks):
        split[block] = split3(panel[block])
    columns = gt_ref.shape[1] // LANES
    factor = jnp.concatenate([rows_of(tokens, column, columns, FACTOR) for column in range(columns)], axis=1)
    grads = fold3(dot_nt(split3(factor), gt_ref[...]))
    total = None
    for chunk in range(chunks):
        copies[chunk].wait()
        part = dot_nt(et_ref[chunk], wide(split, chunk, width))
        total = part if total is None else total + part
    turned = lax.dot_general(
        panel[NMP][:, :count], grads, (((1,), (0,)), ((), ())), precision=lax.Precision.HIGHEST,
        preferred_element_type=F32,
    )
    right[...] = turned + fold3(total.T)


def wide(ref, chunk, width):
    count = width // LANES
    return jnp.concatenate([ref[chunk * count + block] for block in range(count)], axis=1)


def field_kernel(start, acts_hbm, et_hbm, gt_hbm, field, acts_v, error_v, gt_v, acts_sems, error_sems, gt_sem):
    chunks, width = error_v.shape[0], error_v.shape[2]
    count = width // LANES
    gt_copy = pltpu.make_async_copy(gt_hbm, gt_v, gt_sem)
    gt_copy.start()
    for chunk in range(chunks):
        blocks = pl.ds(start + chunk * count, count)
        columns = pl.ds(start * LANES + chunk * width, width)
        place = pl.ds(chunk * count, count)
        pltpu.make_async_copy(acts_hbm.at[blocks], acts_v.at[place], acts_sems.at[chunk]).start()
        pltpu.make_async_copy(et_hbm.at[:, columns], error_v.at[chunk], error_sems.at[chunk]).start()
    gt_copy.wait()

    def body(chunk, carry):
        place = pl.ds(chunk * count, count)
        pltpu.make_async_copy(acts_v.at[place], acts_v.at[place], acts_sems.at[chunk]).wait()
        pltpu.make_async_copy(error_v.at[chunk], error_v.at[chunk], error_sems.at[chunk]).wait()
        value = dot_nn(gt_v[...], wide(acts_v, chunk, width)) + error_v[chunk].astype(F32)
        for block in range(count):
            field[chunk * count + block] = lanes(value, block)
        return carry

    lax.fori_loop(0, chunks, body, 0)


def final_kernel(dp_ref, sum_ref, basis_ref, lower, upper, weight, moment1, moment2, new_weight, new_moment1,
                 new_moment2, new_error, q_new, updated, rounded, sems):
    mean = sum_ref[...] * (1.0 / NDP)
    q_new[...] = mean
    rows, ff = mean.shape
    stack = split3(mean.T)
    hi, mid, lo = stack[:ff], stack[ff : 2 * ff], stack[2 * ff :]
    factor = jnp.concatenate([hi, hi, hi, mid, mid, lo], axis=1)
    chunks, width = rounded.shape[0], rounded.shape[2]
    count = width // LANES

    def approx_of(chunk):
        basis = wide(basis_ref, chunk, width)
        hi, mid, lo = basis[:rows], basis[rows : 2 * rows], basis[2 * rows :]
        return dot_nn(factor, jnp.concatenate([hi, mid, lo, hi, mid, hi], axis=0))

    copies = []

    def send(source, target):
        copy = pltpu.make_async_copy(source, target, sems.at[len(copies)])
        copy.start()
        copies.append(copy)

    update = approx_of(dp_ref[0])
    first = beta_one * moment1[...] + (1.0 - beta_one) * update
    second = beta_two * moment2[...] + (1.0 - beta_two) * update * update
    updated[0] = first
    updated[1] = second
    updated[2] = weight[...] - learn_rate * (first / corr_one) / (jnp.sqrt(second / corr_two) + adam_eps)
    send(updated.at[0], new_moment1)
    send(updated.at[1], new_moment2)
    send(updated.at[2], new_weight)
    for chunk in range(chunks):
        approx = approx_of(chunk)
        field = lower if chunk < chunks // 2 else upper
        first = chunk % (chunks // 2) * count
        for block in range(count):
            columns = slice(block * LANES, (block + 1) * LANES)
            rounded[chunk, :, columns] = (field[first + block] - lanes(approx, block)).astype(BF16)
        send(rounded.at[chunk], new_error.at[:, chunk * width : (chunk + 1) * width])
    for copy in copies:
        copy.wait()


def call(kernel, outs, args, specs=None, out_specs=None, scratch=(), limit=16, flops=0, moved=0):
    return pl.pallas_call(
        kernel,
        out_shape=outs,
        in_specs=specs or [VMEM] * len(args),
        out_specs=out_specs or jax.tree.map(lambda _: VMEM, outs),
        scratch_shapes=scratch,
        compiler_params=pltpu.CompilerParams(vmem_limit_bytes=limit * MIB),
        cost_estimate=pl.CostEstimate(flops=flops, bytes_accessed=moved, transcendentals=0),
    )(*args)


def swap(value, axis, level):
    return lax.ppermute(value, axis, list(enumerate(level)))


def total(value, axis, levels):
    for level in levels:
        value = value + swap(value, axis, level)
    return value


def shards(acts, grad_out, error_buffer, q_prev, weight, moment1, moment2):
    member = lax.axis_index("mp").astype(jnp.int32).reshape(1)
    dp = lax.axis_index("dp").astype(jnp.int32).reshape(1)
    core = dp % 2
    gt, et = grad_out.T, error_buffer.T
    rank, ff = q_prev.shape
    tokens, model = acts.shape[0], et.shape[1]
    chunks, width = 8, model // 8
    array = jax.ShapeDtypeStruct

    gathered = lax.all_gather(acts, "mp", axis=0)

    half = rank // 2
    table = jnp.asarray(met(ALONG_X + ALONG_Z, NMP))
    blocks = array((NMP, half, LANES), F32)
    mine, send = call(
        error_kernel, [blocks, blocks], (member, core, table, q_prev, et), specs=[SMEM] * 3 + [HBM] * 2,
        scratch=[
            pltpu.VMEM((rank, ff), F32), pltpu.VMEM((chunks, ff, width), BF16), pltpu.VMEM((NMP, rank, LANES), F32),
            pltpu.SemaphoreType.DMA((chunks + 1,)),
        ],
        limit=60, flops=6 * rank * ff * model, moved=2 * ff * model,
    )
    theirs = swap(send, "dp", ALONG_DP[0])
    factor = call(
        token_kernel, array((FACTOR, 8, LANES), F32), (q_prev, gt), specs=[HBM] * 2,
        scratch=[pltpu.VMEM((rank, ff), F32), pltpu.VMEM((ff, tokens), BF16), pltpu.SemaphoreType.DMA((2,))],
        limit=58, flops=6 * rank * ff * tokens, moved=2 * ff * tokens,
    )
    count = NMP // 2
    message = lambda tiles: array((FACTOR + tiles, 8, LANES), F32)
    kept = lambda count: array((count, half, LANES), F32)
    sent, keep = call(open_kernel, [message(2 * count), kept(count)], (factor, mine, theirs), moved=MIB)
    ring = [acts] + [swap(acts, "mp", level) for level in ALONG_X]
    ring.append(swap(acts, "mp", [(x + 2) % NX * NZ + z for x in range(NX) for z in range(NZ)]))
    for level in ALONG_Z[:0:-1]:
        came = swap(sent, "mp", level)
        count //= 2
        sent, keep = call(halve_kernel, [message(2 * count), kept(count)], (sent, keep, came), moved=MIB)
    came = swap(sent, "mp", ALONG_Z[0])

    keep, send = call(
        piece_kernel, [kept(NX), kept(NX)], (core, sent, keep, came, *ring), specs=[SMEM] + [VMEM] * 7, moved=MIB
    )
    keep = keep + swap(send, "dp", ALONG_DP[0])
    keep = keep[:2] + swap(keep[2:], "mp", ALONG_X[1])
    keep = keep[:1] + swap(keep[1:], "mp", ALONG_X[0])
    keep = total(keep, "dp", ALONG_DP[1:])
    for level in ALONG_X:
        keep = jnp.concatenate([keep, swap(keep, "mp", level)])
    sent = call(
        start_kernel, message(2 * NX), (core, keep, swap(keep, "dp", ALONG_DP[0]), *ring),
        specs=[SMEM] + [VMEM] * 6, moved=MIB,
    )
    for place, level in enumerate(ALONG_Z[:-1]):
        sent = call(double_kernel, message(4 * NX << place), (sent, swap(sent, "mp", level)), moved=MIB)
    factor, mine = call(
        last_kernel, [array((FACTOR, 8, LANES), F32), array((2 * NMP, 8, LANES), F32)],
        (sent, swap(sent, "mp", ALONG_Z[-1])), moved=MIB,
    )
    basis, right = call(
        ortho_kernel, [array((NMP, 3 * rank, LANES), BF16), array((rank, ff), F32)],
        (member, core, table, mine, swap(mine, "dp", ALONG_DP[0]), factor, gt, et),
        specs=[SMEM] * 3 + [VMEM] * 4 + [HBM],
        scratch=[
            pltpu.VMEM((NMP + 1, rank, LANES), F32),
            pltpu.VMEM((chunks, ff, width), BF16),
            pltpu.SemaphoreType.DMA((chunks,)),
        ],
        limit=24, flops=8 * rank * ff * model, moved=2 * ff * model,
    )
    right, gathered = lax.optimization_barrier((right, gathered))
    halves = []
    for part, level in enumerate(ALONG_DP[1:]):
        half = call(
            functools.partial(field_kernel, part * NMP // 2), array((NMP // 2, ff, LANES), F32), (gathered, et, gt),
            specs=[HBM] * 3,
            scratch=[
                pltpu.VMEM((NMP // 2, tokens, LANES), BF16),
                pltpu.VMEM((chunks // 2, ff, width), BF16),
                pltpu.VMEM((ff, tokens), BF16),
                pltpu.SemaphoreType.DMA((chunks // 2,)),
                pltpu.SemaphoreType.DMA((chunks // 2,)),
                pltpu.SemaphoreType.DMA,
            ],
            limit=48, flops=model * ff * tokens, moved=10 * MIB,
        )
        right, half = lax.optimization_barrier((total(right, "dp", [level]), half))
        halves.append(half)
    right = total(right, "dp", ALONG_DP[:1])

    block = array((ff, width), F32)
    outs = call(
        final_kernel,
        [block] * 3 + [array((ff, model), BF16), array((rank, ff), F32)],
        (dp, right, basis, *halves, weight.T, moment1.T, moment2.T),
        specs=[SMEM] + [VMEM] * 7,
        out_specs=[HBM] * 4 + [VMEM],
        scratch=[
            pltpu.VMEM((3, ff, width), F32),
            pltpu.VMEM((chunks, ff, width), BF16),
            pltpu.SemaphoreType.DMA((3 + chunks,)),
        ],
        limit=24, flops=12 * rank * model * ff, moved=20 * MIB,
    )
    new_weight, new_moment1, new_moment2, new_error, q_new = outs
    return (new_weight.T, new_moment1.T, new_moment2.T, new_error.T, q_new)


def solution(mesh):
    placed = (
        P("dp", "mp"),
        P("dp", "mp"),
        P("dp", "mp"),
        P(None, "mp"),
        P("dp", "mp"),
        P("dp", "mp"),
        P("dp", "mp"),
    )
    return jax.shard_map(
        shards,
        mesh=mesh,
        in_specs=placed,
        out_specs=(P("dp", "mp"), P("dp", "mp"), P("dp", "mp"), P("dp", "mp"), P(None, "mp")),
        check_vma=False,
    )
```

```python
import functools

import jax
import jax.numpy as jnp
import numpy as np
from jax import lax
from jax.experimental import pallas as pl
from jax.experimental.pallas import tpu as pltpu
from jax.sharding import PartitionSpec as P

ortho_eps = 1e-08
adam_eps = 1e-08
beta_one = 0.9
beta_two = 0.95
learn_rate = 0.01
corr_one = 1.0 - 0.9**10
corr_two = 1.0 - 0.95**10

NX, NZ, NDP = 4, 8, 8
NMP = NX * NZ
FACTOR = 32
QUARTER = FACTOR // NX
LANES = 128
F32, BF16 = jnp.float32, jnp.bfloat16
MIB = 1 << 20
SMEM = pl.BlockSpec(memory_space=pltpu.SMEM)
VMEM = pl.BlockSpec(memory_space=pltpu.VMEM)
HBM = pl.BlockSpec(memory_space=pltpu.HBM)

RING4 = ([1, 0, 3, 2], [3, 2, 1, 0])
RING8 = ([3, 6, 5, 0, 7, 2, 1, 4], [7, 2, 1, 4, 3, 6, 5, 0], [1, 0, 3, 2, 5, 4, 7, 6])
ALONG_Z = [[x * NZ + to for x in range(NX) for to in level] for level in RING8]
ALONG_X = [[to * NZ + z for to in level for z in range(NZ)] for level in RING4]
ALONG_DP = [[1, 0, 3, 2, 5, 4, 7, 6]] + [[to * 2 + core for to in level for core in range(2)] for level in RING4]


def met(levels, members):
    held = [[member] for member in range(members)]
    for level in levels:
        held = [held[member] + held[level[member]] for member in range(members)]
    return np.array(held, np.int32)


def split3(value):
    hi = value.astype(BF16)
    rest = value - hi.astype(F32)
    mid = rest.astype(BF16)
    lo = (rest - mid.astype(F32)).astype(BF16)
    return jnp.concatenate([hi, mid, lo], axis=0)


def fold3(stacked):
    rows = stacked.shape[0] // 3
    return stacked[:rows] + (stacked[rows : 2 * rows] + stacked[2 * rows :])


def dot_nn(a, b):
    return lax.dot_general(a, b, (((1,), (0,)), ((), ())), preferred_element_type=F32)


def dot_nt(a, b):
    return lax.dot_general(a, b, (((1,), (1,)), ((), ())), preferred_element_type=F32)


def dot_tn(a, b):
    return lax.dot_general(a, b, (((0,), (0,)), ((), ())), preferred_element_type=F32)


def add_all(values):
    while len(values) > 1:
        values = [a + b for a, b in zip(values[::2], values[1::2])] + values[len(values) // 2 * 2 :]
    return values[0]


def lanes(array, block):
    return array[:, block * LANES : (block + 1) * LANES]


def tiles_of(value, out):
    columns = value.shape[1] // LANES
    for row in range(value.shape[0] // 8):
        for column in range(columns):
            out[row * columns + column] = lanes(value[row * 8 : row * 8 + 8], column)


def rows_of(tiles, column, columns, rows):
    return jnp.concatenate([tiles[row * columns + column] for row in range(rows // 8)], axis=0)


def error_kernel(member_ref, core_ref, place_ref, q_hbm, et_hbm, keep, send, q_ref, et_ref, parts, sems):
    count, width = et_ref.shape[0], et_ref.shape[2]
    copies = [
        pltpu.make_async_copy(et_hbm.at[:, chunk * width : (chunk + 1) * width], et_ref.at[chunk], sems.at[chunk])
        for chunk in range(count)
    ]
    first = pltpu.make_async_copy(q_hbm, q_ref, sems.at[count])
    first.start()
    for copy in copies:
        copy.start()
    first.wait()
    split = split3(q_ref[...])
    blocks = width // LANES
    half = parts.shape[1] // 2
    for chunk in range(count):
        copies[chunk].wait()
        part = fold3(dot_nn(split, et_ref[chunk]))
        for block in range(blocks):
            parts[chunk * blocks + block] = lanes(part, block)
    lower = core_ref[0] == 0
    for place in range(NMP):
        block = parts[place_ref[member_ref[0], place]]
        keep[place] = jnp.where(lower, block[:half], block[half:])
        send[place] = jnp.where(lower, block[half:], block[:half])


def token_kernel(q_hbm, gt_hbm, out, q_ref, gt_ref, sems):
    copies = [pltpu.make_async_copy(q_hbm, q_ref, sems.at[0]), pltpu.make_async_copy(gt_hbm, gt_ref, sems.at[1])]
    for copy in copies:
        copy.start()
    for copy in copies:
        copy.wait()
    tiles_of(fold3(dot_nn(split3(q_ref[...]), gt_ref[...])), out)


def store_blocks(value, out, start):
    for block in range(value.shape[0]):
        out[start + 2 * block] = value[block, :8]
        out[start + 2 * block + 1] = value[block, 8:]


def load_blocks(ref, start, count):
    return jnp.stack(
        [jnp.concatenate([ref[start + 2 * block], ref[start + 2 * block + 1]], axis=0) for block in range(count)]
    )


def open_kernel(tokens, mine, theirs, message, keep):
    message[:FACTOR] = tokens[...]
    both = mine[...] + theirs[...]
    half = both.shape[0] // 2
    keep[...] = both[:half]
    store_blocks(both[half:], message, FACTOR)


def halve_kernel(sent, kept, came, message, keep):
    message[:FACTOR] = sent[:FACTOR] + came[:FACTOR]
    count = kept.shape[0]
    both = kept[...] + load_blocks(came, FACTOR, count)
    keep[...] = both[: count // 2]
    store_blocks(both[count // 2 :], message, FACTOR)


def piece_kernel(member_ref, core_ref, place_ref, sent, kept, came, *refs):
    acts_refs, keep, send = refs[:NX], refs[NX], refs[NX + 1]
    blocks = acts_refs[0].shape[0] // LANES
    half = keep.shape[1]
    lower = core_ref[0] == 0
    errors = kept[...] + load_blocks(came, FACTOR, NX)
    factors = []
    for block in range(blocks):
        factors.append(split3(rows_of(sent, block, blocks, FACTOR) + rows_of(came, block, blocks, FACTOR)))
    factor = jnp.concatenate(factors, axis=1)
    for place in range(NX):
        x = lax.div(place_ref[member_ref[0], place], NZ)
        piece = fold3(dot_nn(factor, acts_refs[place][...]))
        keep[x] = jnp.where(lower, piece[:half], piece[half:]) + errors[place]
        send[x] = jnp.where(lower, piece[half:], piece[:half])


def start_kernel(member_ref, core_ref, place_ref, mine, theirs, *refs):
    acts_refs, message = refs[:NX], refs[NX]
    lower = core_ref[0] == 0
    rows = acts_refs[0].shape[0] // NX
    home = lax.div(member_ref[0], NZ)
    quarter = pl.ds(pl.multiple_of(home * rows, rows), rows)
    total = None
    for place in range(NX):
        x = lax.div(place_ref[member_ref[0], place], NZ)
        first, second = mine[x] * (1.0 / NDP), theirs[x] * (1.0 / NDP)
        panel = jnp.concatenate([jnp.where(lower, first, second), jnp.where(lower, second, first)], axis=0)
        part = dot_nt(split3(panel), acts_refs[place][quarter, :])
        total = part if total is None else total + part
    tiles_of(fold3(total), message)
    store_blocks(mine[home][None] * (1.0 / NDP), message, QUARTER)


def double_kernel(sent, came, message):
    count = sent.shape[0] - QUARTER
    message[:QUARTER] = sent[:QUARTER] + came[:QUARTER]
    message[QUARTER : QUARTER + count] = sent[QUARTER:]
    message[QUARTER + count :] = came[QUARTER:]


def part_kernel(sent, came, factor, rows):
    each = sent.shape[0] // 2
    count = each - QUARTER
    for place in range(NX):
        ref = sent if place < 2 else came
        start = place % 2 * each
        factor[place * QUARTER : (place + 1) * QUARTER] = ref[start : start + QUARTER]
        rows[place * count : (place + 1) * count] = ref[start + QUARTER : start + each]


def ortho_kernel(member_ref, core_ref, place_ref, mine, theirs, tokens, gt_ref, et_hbm, split, right, panel, et_ref, factors,
                 sems):
    chunks, width = et_ref.shape[0], et_ref.shape[2]
    copies = [
        pltpu.make_async_copy(et_hbm.at[:, chunk * width : (chunk + 1) * width], et_ref.at[chunk], sems.at[chunk])
        for chunk in range(chunks)
    ]
    for copy in copies:
        copy.start()
    member = member_ref[0]
    lower = core_ref[0] == 0
    half = panel.shape[1] // 2
    for place in range(NMP):
        first = jnp.concatenate([mine[2 * place], mine[2 * place + 1]], axis=0)
        second = jnp.concatenate([theirs[2 * place], theirs[2 * place + 1]], axis=0)
        block = place_ref[member, place]
        panel[block, :half] = jnp.where(lower, first, second)
        panel[block, half:] = jnp.where(lower, second, first)
    square = panel.shape[1:]
    same = lax.broadcasted_iota(jnp.int32, square, 0) == lax.broadcasted_iota(jnp.int32, square, 1)
    panel[NMP] = jnp.where(same, 1.0, 0.0)
    blocks, count = NMP, panel.shape[1]
    groups = count // 8

    def inner_of(index):
        first = index // 8
        sums = [None] * groups
        for block in range(blocks):
            row = panel[block, index : index + 1, :]
            for group in range(first, groups):
                term = panel[block, group * 8 : group * 8 + 8, :] * row
                sums[group] = term if sums[group] is None else sums[group] + term
        return [None if s is None else jnp.sum(s, axis=1, keepdims=True) for s in sums]

    order = lax.broadcasted_iota(jnp.int32, (8, 1), 0)
    for index in range(count):
        first, place = index // 8, index % 8
        inner = inner_of(index)
        scale = 1.0 / (jnp.sqrt(inner[first][place : place + 1, :]) + ortho_eps)
        weights = []
        for group in range(first, groups):
            weight = inner[group] * (scale * scale)
            if group == first:
                weight = jnp.where(order > place, weight, 0.0)
            weights.append(weight)
        for block in range(blocks + 1):
            row = panel[block, index : index + 1, :]
            for group in range(first, groups):
                if group == first and place == 7:
                    continue
                rows = slice(group * 8, group * 8 + 8)
                panel[block, rows, :] = panel[block, rows, :] - weights[group - first] * row
            panel[block, index : index + 1, :] = row * scale
    for block in range(blocks):
        split[block] = split3(panel[block])
    columns = factors.shape[2] // LANES
    for place in range(NX):
        tiles = tokens.at[pl.ds(place * QUARTER, QUARTER)]
        factors[lax.div(place_ref[member, place * NZ], NZ)] = jnp.concatenate(
            [rows_of(tiles, column, columns, FACTOR) for column in range(columns)], axis=1
        )
    factor = jnp.concatenate([factors[x] for x in range(NX)], axis=1)
    grads = fold3(dot_nt(split3(factor), gt_ref[...]))
    total = None
    for chunk in range(chunks):
        copies[chunk].wait()
        part = dot_nt(et_ref[chunk], wide(split, chunk, width))
        total = part if total is None else total + part
    turned = lax.dot_general(
        panel[NMP][:, :count], grads, (((1,), (0,)), ((), ())), precision=lax.Precision.HIGHEST,
        preferred_element_type=F32,
    )
    right[...] = turned + fold3(total.T)


def wide(ref, chunk, width):
    count = width // LANES
    return jnp.concatenate([ref[chunk * count + block] for block in range(count)], axis=1)


def field_kernel(start, acts_hbm, et_hbm, gt_hbm, field, acts_v, error_v, gt_v, acts_sems, error_sems, gt_sem):
    chunks, width = error_v.shape[0], error_v.shape[2]
    count = width // LANES
    gt_copy = pltpu.make_async_copy(gt_hbm, gt_v, gt_sem)
    gt_copy.start()
    for chunk in range(chunks):
        blocks = pl.ds(start + chunk * count, count)
        columns = pl.ds(start * LANES + chunk * width, width)
        place = pl.ds(chunk * count, count)
        pltpu.make_async_copy(acts_hbm.at[blocks], acts_v.at[place], acts_sems.at[chunk]).start()
        pltpu.make_async_copy(et_hbm.at[:, columns], error_v.at[chunk], error_sems.at[chunk]).start()
    gt_copy.wait()

    def body(chunk, carry):
        place = pl.ds(chunk * count, count)
        pltpu.make_async_copy(acts_v.at[place], acts_v.at[place], acts_sems.at[chunk]).wait()
        pltpu.make_async_copy(error_v.at[chunk], error_v.at[chunk], error_sems.at[chunk]).wait()
        value = dot_nn(gt_v[...], wide(acts_v, chunk, width)) + error_v[chunk].astype(F32)
        for block in range(count):
            field[chunk * count + block] = lanes(value, block)
        return carry

    lax.fori_loop(0, chunks, body, 0)


def final_kernel(dp_ref, sum_ref, basis_ref, lower, upper, weight, moment1, moment2, new_weight, new_moment1,
                 new_moment2, new_error, q_new, updated, rounded, sems):
    mean = sum_ref[...] * (1.0 / NDP)
    q_new[...] = mean
    rows, ff = mean.shape
    stack = split3(mean.T)
    hi, mid, lo = stack[:ff], stack[ff : 2 * ff], stack[2 * ff :]
    factor = jnp.concatenate([hi, hi, hi, mid, mid, lo], axis=1)
    chunks, width = rounded.shape[0], rounded.shape[2]
    count = width // LANES

    def approx_of(chunk):
        basis = wide(basis_ref, chunk, width)
        hi, mid, lo = basis[:rows], basis[rows : 2 * rows], basis[2 * rows :]
        return dot_nn(factor, jnp.concatenate([hi, mid, lo, hi, mid, hi], axis=0))

    copies = []

    def send(source, target):
        copy = pltpu.make_async_copy(source, target, sems.at[len(copies)])
        copy.start()
        copies.append(copy)

    update = approx_of(dp_ref[0])
    first = beta_one * moment1[...] + (1.0 - beta_one) * update
    second = beta_two * moment2[...] + (1.0 - beta_two) * update * update
    updated[0] = first
    updated[1] = second
    updated[2] = weight[...] - learn_rate * (first / corr_one) / (jnp.sqrt(second / corr_two) + adam_eps)
    send(updated.at[0], new_moment1)
    send(updated.at[1], new_moment2)
    send(updated.at[2], new_weight)
    for chunk in range(chunks):
        approx = approx_of(chunk)
        field = lower if chunk < chunks // 2 else upper
        first = chunk % (chunks // 2) * count
        for block in range(count):
            columns = slice(block * LANES, (block + 1) * LANES)
            rounded[chunk, :, columns] = (field[first + block] - lanes(approx, block)).astype(BF16)
        send(rounded.at[chunk], new_error.at[:, chunk * width : (chunk + 1) * width])
    for copy in copies:
        copy.wait()


def call(kernel, outs, args, specs=None, out_specs=None, scratch=(), limit=16, flops=0, moved=0):
    return pl.pallas_call(
        kernel,
        out_shape=outs,
        in_specs=specs or [VMEM] * len(args),
        out_specs=out_specs or jax.tree.map(lambda _: VMEM, outs),
        scratch_shapes=scratch,
        compiler_params=pltpu.CompilerParams(vmem_limit_bytes=int(limit * MIB)),
        cost_estimate=pl.CostEstimate(flops=flops, bytes_accessed=moved, transcendentals=0),
    )(*args)


def swap(value, axis, level):
    return lax.ppermute(value, axis, list(enumerate(level)))


def total(value, axis, levels):
    for level in levels:
        value = value + swap(value, axis, level)
    return value


def shards(acts, grad_out, error_buffer, q_prev, weight, moment1, moment2):
    member = lax.axis_index("mp").astype(jnp.int32).reshape(1)
    dp = lax.axis_index("dp").astype(jnp.int32).reshape(1)
    core = dp % 2
    gt, et = grad_out.T, error_buffer.T
    rank, ff = q_prev.shape
    tokens, model = acts.shape[0], et.shape[1]
    chunks, width = 8, model // 8
    array = jax.ShapeDtypeStruct

    gathered = lax.all_gather(acts, "mp", axis=0)

    half = rank // 2
    table = jnp.asarray(met(ALONG_X + ALONG_Z, NMP))
    blocks = array((NMP, half, LANES), F32)
    mine, send = call(
        error_kernel, [blocks, blocks], (member, core, table, q_prev, et), specs=[SMEM] * 3 + [HBM] * 2,
        scratch=[
            pltpu.VMEM((rank, ff), F32), pltpu.VMEM((chunks, ff, width), BF16), pltpu.VMEM((NMP, rank, LANES), F32),
            pltpu.SemaphoreType.DMA((chunks + 1,)),
        ],
        limit=56, flops=6 * rank * ff * model, moved=2 * ff * model,
    )
    theirs = swap(send, "dp", ALONG_DP[0])
    factor = call(
        token_kernel, array((FACTOR, 8, LANES), F32), (q_prev, gt), specs=[HBM] * 2,
        scratch=[pltpu.VMEM((rank, ff), F32), pltpu.VMEM((ff, tokens), BF16), pltpu.SemaphoreType.DMA((2,))],
        limit=16, flops=6 * rank * ff * tokens, moved=2 * ff * tokens,
    )
    count = NMP // 2
    message = lambda tiles: array((FACTOR + tiles, 8, LANES), F32)
    kept = lambda count: array((count, half, LANES), F32)
    sent, keep = call(open_kernel, [message(2 * count), kept(count)], (factor, mine, theirs), moved=MIB)
    ring = [acts] + [swap(acts, "mp", level) for level in ALONG_X]
    ring.append(swap(acts, "mp", [(x + 2) % NX * NZ + z for x in range(NX) for z in range(NZ)]))
    for place, level in enumerate(ALONG_Z[:0:-1]):
        came = swap(sent, "mp", level)
        count //= 2
        sent, keep = call(halve_kernel, [message(2 * count), kept(count)], (sent, keep, came), moved=MIB)
        if place == 0:
            sent, ring[1:3] = lax.optimization_barrier((sent, ring[1:3]))
    came = swap(sent, "mp", ALONG_Z[0])

    keep, send = call(
        piece_kernel, [kept(NX), kept(NX)], (member, core, table, sent, keep, came, *ring),
        specs=[SMEM] * 3 + [VMEM] * 7, moved=MIB,
    )
    keep = keep + swap(send, "dp", ALONG_DP[0])
    keep = total(total(keep, "mp", ALONG_X), "dp", ALONG_DP[1:])
    sent = call(
        start_kernel, array((QUARTER + 2, 8, LANES), F32), (member, core, table, keep, swap(keep, "dp", ALONG_DP[0]), *ring),
        specs=[SMEM] * 3 + [VMEM] * 6, moved=MIB,
    )
    for place, level in enumerate(ALONG_Z):
        came = swap(sent, "mp", level)
        sent = call(double_kernel, array((QUARTER + (4 << place), 8, LANES), F32), (sent, came), moved=MIB)
    sent = jnp.concatenate([sent, swap(sent, "mp", ALONG_X[0])])
    factor, mine = call(
        part_kernel, [array((FACTOR, 8, LANES), F32), array((2 * NMP, 8, LANES), F32)],
        (sent, swap(sent, "mp", ALONG_X[1])), moved=MIB,
    )
    basis, right = call(
        ortho_kernel, [array((NMP, 3 * rank, LANES), BF16), array((rank, ff), F32)],
        (member, core, jnp.asarray(met(ALONG_Z + ALONG_X, NMP)), mine, swap(mine, "dp", ALONG_DP[0]), factor, gt, et),
        specs=[SMEM] * 3 + [VMEM] * 4 + [HBM],
        scratch=[
            pltpu.VMEM((NMP + 1, rank, LANES), F32),
            pltpu.VMEM((chunks, ff, width), BF16),
            pltpu.VMEM((NX, rank, tokens // NX), F32),
            pltpu.SemaphoreType.DMA((chunks,)),
        ],
        limit=24, flops=8 * rank * ff * model, moved=2 * ff * model,
    )
    right, gathered = lax.optimization_barrier((total(right, "dp", ALONG_DP[1:2]), gathered))
    halves = []
    for part, level in enumerate((ALONG_DP[2], ALONG_DP[0])):
        half = call(
            functools.partial(field_kernel, part * NMP // 2), array((NMP // 2, ff, LANES), F32), (gathered, et, gt),
            specs=[HBM] * 3,
            scratch=[
                pltpu.VMEM((NMP // 2, tokens, LANES), BF16),
                pltpu.VMEM((chunks // 2, ff, width), BF16),
                pltpu.VMEM((ff, tokens), BF16),
                pltpu.SemaphoreType.DMA((chunks // 2,)),
                pltpu.SemaphoreType.DMA((chunks // 2,)),
                pltpu.SemaphoreType.DMA,
            ],
            limit=48, flops=model * ff * tokens, moved=10 * MIB,
        )
        right, half = lax.optimization_barrier((total(right, "dp", [level]), half))
        halves.append(half)

    block = array((ff, width), F32)
    outs = call(
        final_kernel,
        [block] * 3 + [array((ff, model), BF16), array((rank, ff), F32)],
        (dp, right, basis, *halves, weight.T, moment1.T, moment2.T),
        specs=[SMEM] + [VMEM] * 7,
        out_specs=[HBM] * 4 + [VMEM],
        scratch=[
            pltpu.VMEM((3, ff, width), F32),
            pltpu.VMEM((chunks, ff, width), BF16),
            pltpu.SemaphoreType.DMA((3 + chunks,)),
        ],
        limit=24, flops=12 * rank * model * ff, moved=20 * MIB,
    )
    new_weight, new_moment1, new_moment2, new_error, q_new = outs
    return (new_weight.T, new_moment1.T, new_moment2.T, new_error.T, q_new)


def solution(mesh):
    placed = (
        P("dp", "mp"),
        P("dp", "mp"),
        P("dp", "mp"),
        P(None, "mp"),
        P("dp", "mp"),
        P("dp", "mp"),
        P("dp", "mp"),
    )
    return jax.shard_map(
        shards,
        mesh=mesh,
        in_specs=placed,
        out_specs=(P("dp", "mp"), P("dp", "mp"), P("dp", "mp"), P("dp", "mp"), P(None, "mp")),
        check_vma=False,
    )
```

```python
import functools

import jax
import jax.numpy as jnp
import numpy as np
from jax import lax
from jax.experimental import pallas as pl
from jax.experimental.pallas import tpu as pltpu
from jax.sharding import PartitionSpec as P

ortho_eps = 1e-08
adam_eps = 1e-08
beta_one = 0.9
beta_two = 0.95
learn_rate = 0.01
corr_one = 1.0 - 0.9**10
corr_two = 1.0 - 0.95**10

NX, NZ, NDP = 4, 8, 8
NMP = NX * NZ
FACTOR = 32
QUARTER = FACTOR // NX
LANES = 128
F32, BF16 = jnp.float32, jnp.bfloat16
MIB = 1 << 20
SMEM = pl.BlockSpec(memory_space=pltpu.SMEM)
VMEM = pl.BlockSpec(memory_space=pltpu.VMEM)
HBM = pl.BlockSpec(memory_space=pltpu.HBM)

RING4 = ([1, 0, 3, 2], [3, 2, 1, 0])
RING8 = ([3, 6, 5, 0, 7, 2, 1, 4], [7, 2, 1, 4, 3, 6, 5, 0], [1, 0, 3, 2, 5, 4, 7, 6])
ALONG_Z = [[x * NZ + to for x in range(NX) for to in level] for level in RING8]
ALONG_X = [[to * NZ + z for to in level for z in range(NZ)] for level in RING4]
ALONG_DP = [[1, 0, 3, 2, 5, 4, 7, 6]] + [[to * 2 + core for to in level for core in range(2)] for level in RING4]


def met(levels, members):
    held = [[member] for member in range(members)]
    for level in levels:
        held = [held[member] + held[level[member]] for member in range(members)]
    return np.array(held, np.int32)


def split3(value):
    hi = value.astype(BF16)
    rest = value - hi.astype(F32)
    mid = rest.astype(BF16)
    lo = (rest - mid.astype(F32)).astype(BF16)
    return jnp.concatenate([hi, mid, lo], axis=0)


def fold3(stacked):
    rows = stacked.shape[0] // 3
    return stacked[:rows] + (stacked[rows : 2 * rows] + stacked[2 * rows :])


def dot_nn(a, b):
    return lax.dot_general(a, b, (((1,), (0,)), ((), ())), preferred_element_type=F32)


def dot_nt(a, b):
    return lax.dot_general(a, b, (((1,), (1,)), ((), ())), preferred_element_type=F32)


def dot_tn(a, b):
    return lax.dot_general(a, b, (((0,), (0,)), ((), ())), preferred_element_type=F32)


def add_all(values):
    while len(values) > 1:
        values = [a + b for a, b in zip(values[::2], values[1::2])] + values[len(values) // 2 * 2 :]
    return values[0]


def lanes(array, block):
    return array[:, block * LANES : (block + 1) * LANES]


def tiles_of(value, out):
    columns = value.shape[1] // LANES
    for row in range(value.shape[0] // 8):
        for column in range(columns):
            out[row * columns + column] = lanes(value[row * 8 : row * 8 + 8], column)


def rows_of(tiles, column, columns, rows):
    return jnp.concatenate([tiles[row * columns + column] for row in range(rows // 8)], axis=0)


def error_kernel(member_ref, core_ref, place_ref, q_hbm, et_hbm, keep, send, q_ref, et_ref, parts, sems):
    count, width = et_ref.shape[0], et_ref.shape[2]
    copies = [
        pltpu.make_async_copy(et_hbm.at[:, chunk * width : (chunk + 1) * width], et_ref.at[chunk], sems.at[chunk])
        for chunk in range(count)
    ]
    first = pltpu.make_async_copy(q_hbm, q_ref, sems.at[count])
    first.start()
    for copy in copies:
        copy.start()
    first.wait()
    split = split3(q_ref[...])
    blocks = width // LANES
    half = parts.shape[1] // 2
    for chunk in range(count):
        copies[chunk].wait()
        part = fold3(dot_nn(split, et_ref[chunk]))
        for block in range(blocks):
            parts[chunk * blocks + block] = lanes(part, block)
    lower = core_ref[0] == 0
    for place in range(NMP):
        block = parts[place_ref[member_ref[0], place]]
        keep[place] = jnp.where(lower, block[:half], block[half:])
        send[place] = jnp.where(lower, block[half:], block[:half])


def token_kernel(q_hbm, gt_hbm, out, q_ref, gt_ref, sems):
    copies = [pltpu.make_async_copy(q_hbm, q_ref, sems.at[0]), pltpu.make_async_copy(gt_hbm, gt_ref, sems.at[1])]
    for copy in copies:
        copy.start()
    for copy in copies:
        copy.wait()
    tiles_of(fold3(dot_nn(split3(q_ref[...]), gt_ref[...])), out)


def store_blocks(value, out, start):
    for block in range(value.shape[0]):
        out[start + 2 * block] = value[block, :8]
        out[start + 2 * block + 1] = value[block, 8:]


def load_blocks(ref, start, count):
    return jnp.stack(
        [jnp.concatenate([ref[start + 2 * block], ref[start + 2 * block + 1]], axis=0) for block in range(count)]
    )


def open_kernel(tokens, mine, theirs, message, keep):
    message[:FACTOR] = tokens[...]
    both = mine[...] + theirs[...]
    half = both.shape[0] // 2
    keep[...] = both[:half]
    store_blocks(both[half:], message, FACTOR)


def halve_kernel(sent, kept, came, message, keep):
    message[:FACTOR] = sent[:FACTOR] + came[:FACTOR]
    count = kept.shape[0]
    both = kept[...] + load_blocks(came, FACTOR, count)
    keep[...] = both[: count // 2]
    store_blocks(both[count // 2 :], message, FACTOR)


def piece_kernel(member_ref, core_ref, place_ref, sent, kept, came, *refs):
    acts_refs, keep, send = refs[:NX], refs[NX], refs[NX + 1]
    blocks = acts_refs[0].shape[0] // LANES
    half = keep.shape[1]
    lower = core_ref[0] == 0
    errors = kept[...] + load_blocks(came, FACTOR, NX)
    factors = []
    for block in range(blocks):
        factors.append(split3(rows_of(sent, block, blocks, FACTOR) + rows_of(came, block, blocks, FACTOR)))
    factor = jnp.concatenate(factors, axis=1)
    for place in range(NX):
        x = lax.div(place_ref[member_ref[0], place], NZ)
        piece = fold3(dot_nn(factor, acts_refs[place][...]))
        keep[x] = jnp.where(lower, piece[:half], piece[half:]) + errors[place]
        send[x] = jnp.where(lower, piece[half:], piece[:half])


def start_kernel(member_ref, core_ref, place_ref, mine, theirs, *refs):
    acts_refs, message = refs[:NX], refs[NX]
    lower = core_ref[0] == 0
    rows = acts_refs[0].shape[0] // NX
    home = lax.div(member_ref[0], NZ)
    quarter = pl.ds(pl.multiple_of(home * rows, rows), rows)
    total = None
    for place in range(NX):
        x = lax.div(place_ref[member_ref[0], place], NZ)
        first, second = mine[x] * (1.0 / NDP), theirs[x] * (1.0 / NDP)
        panel = jnp.concatenate([jnp.where(lower, first, second), jnp.where(lower, second, first)], axis=0)
        part = dot_nt(split3(panel), acts_refs[place][quarter, :])
        total = part if total is None else total + part
    tiles_of(fold3(total), message)
    store_blocks(mine[home][None] * (1.0 / NDP), message, QUARTER)


def double_kernel(sent, came, message):
    count = sent.shape[0] - QUARTER
    message[:QUARTER] = sent[:QUARTER] + came[:QUARTER]
    message[QUARTER : QUARTER + count] = sent[QUARTER:]
    message[QUARTER + count :] = came[QUARTER:]


def part_kernel(sent, came, factor, rows):
    each = sent.shape[0] // 2
    count = each - QUARTER
    for place in range(NX):
        ref = sent if place < 2 else came
        start = place % 2 * each
        factor[place * QUARTER : (place + 1) * QUARTER] = ref[start : start + QUARTER]
        rows[place * count : (place + 1) * count] = ref[start + QUARTER : start + each]


def ortho_kernel(member_ref, core_ref, place_ref, mine, theirs, tokens, gt_ref, et_hbm, split, right, panel, et_ref, factors,
                 sems):
    chunks, width = et_ref.shape[0], et_ref.shape[2]
    copies = [
        pltpu.make_async_copy(et_hbm.at[:, chunk * width : (chunk + 1) * width], et_ref.at[chunk], sems.at[chunk])
        for chunk in range(chunks)
    ]
    for copy in copies:
        copy.start()
    member = member_ref[0]
    lower = core_ref[0] == 0
    half = panel.shape[1] // 2
    for place in range(NMP):
        first = jnp.concatenate([mine[2 * place], mine[2 * place + 1]], axis=0)
        second = jnp.concatenate([theirs[2 * place], theirs[2 * place + 1]], axis=0)
        block = place_ref[member, place]
        panel[block, :half] = jnp.where(lower, first, second)
        panel[block, half:] = jnp.where(lower, second, first)
    square = panel.shape[1:]
    same = lax.broadcasted_iota(jnp.int32, square, 0) == lax.broadcasted_iota(jnp.int32, square, 1)
    panel[NMP] = jnp.where(same, 1.0, 0.0)
    columns = factors.shape[2] // LANES
    for place in range(NX):
        tiles = tokens.at[pl.ds(place * QUARTER, QUARTER)]
        factors[lax.div(place_ref[member, place * NZ], NZ)] = jnp.concatenate(
            [rows_of(tiles, column, columns, FACTOR) for column in range(columns)], axis=1
        )
    factor = jnp.concatenate([factors[x] for x in range(NX)], axis=1)
    grads = fold3(dot_nt(split3(factor), gt_ref[...]))
    for copy in copies:
        copy.wait()
    total = None
    for chunk in range(chunks):
        part = dot_nt(et_ref[chunk], split3(wide(panel, chunk, width)))
        total = part if total is None else total + part
    grads = grads + fold3(total.T)
    blocks, count = NMP, panel.shape[1]
    groups = count // 8

    def inner_of(index):
        first = index // 8
        sums = [None] * groups
        for block in range(blocks):
            row = panel[block, index : index + 1, :]
            for group in range(first, groups):
                term = panel[block, group * 8 : group * 8 + 8, :] * row
                sums[group] = term if sums[group] is None else sums[group] + term
        return [None if s is None else jnp.sum(s, axis=1, keepdims=True) for s in sums]

    order = lax.broadcasted_iota(jnp.int32, (8, 1), 0)
    for index in range(count):
        first, place = index // 8, index % 8
        inner = inner_of(index)
        scale = 1.0 / (jnp.sqrt(inner[first][place : place + 1, :]) + ortho_eps)
        weights = []
        for group in range(first, groups):
            weight = inner[group] * (scale * scale)
            if group == first:
                weight = jnp.where(order > place, weight, 0.0)
            weights.append(weight)
        for block in range(blocks + 1):
            row = panel[block, index : index + 1, :]
            for group in range(first, groups):
                if group == first and place == 7:
                    continue
                rows = slice(group * 8, group * 8 + 8)
                panel[block, rows, :] = panel[block, rows, :] - weights[group - first] * row
            panel[block, index : index + 1, :] = row * scale
    for block in range(blocks):
        split[block] = split3(panel[block])
    turned = lax.dot_general(
        panel[NMP][:, :count], grads, (((1,), (0,)), ((), ())), precision=lax.Precision.HIGHEST,
        preferred_element_type=F32,
    )
    right[...] = turned


def wide(ref, chunk, width):
    count = width // LANES
    return jnp.concatenate([ref[chunk * count + block] for block in range(count)], axis=1)


def field_kernel(start, acts_hbm, et_hbm, gt_hbm, field, acts_v, error_v, gt_v, acts_sems, error_sems, gt_sem):
    chunks, width = error_v.shape[0], error_v.shape[2]
    count = width // LANES
    gt_copy = pltpu.make_async_copy(gt_hbm, gt_v, gt_sem)
    gt_copy.start()
    for chunk in range(chunks):
        blocks = pl.ds(start + chunk * count, count)
        columns = pl.ds(start * LANES + chunk * width, width)
        place = pl.ds(chunk * count, count)
        pltpu.make_async_copy(acts_hbm.at[blocks], acts_v.at[place], acts_sems.at[chunk]).start()
        pltpu.make_async_copy(et_hbm.at[:, columns], error_v.at[chunk], error_sems.at[chunk]).start()
    gt_copy.wait()

    def body(chunk, carry):
        place = pl.ds(chunk * count, count)
        pltpu.make_async_copy(acts_v.at[place], acts_v.at[place], acts_sems.at[chunk]).wait()
        pltpu.make_async_copy(error_v.at[chunk], error_v.at[chunk], error_sems.at[chunk]).wait()
        value = dot_nn(gt_v[...], wide(acts_v, chunk, width)) + error_v[chunk].astype(F32)
        for block in range(count):
            field[chunk * count + block] = lanes(value, block)
        return carry

    lax.fori_loop(0, chunks, body, 0)


def final_kernel(dp_ref, sum_ref, basis_ref, lower, upper, weight, moment1, moment2, new_weight, new_moment1,
                 new_moment2, new_error, q_new, updated, rounded, sems):
    mean = sum_ref[...] * (1.0 / NDP)
    q_new[...] = mean
    rows, ff = mean.shape
    stack = split3(mean.T)
    hi, mid, lo = stack[:ff], stack[ff : 2 * ff], stack[2 * ff :]
    factor = jnp.concatenate([hi, hi, hi, mid, mid, lo], axis=1)
    chunks, width = rounded.shape[0], rounded.shape[2]
    count = width // LANES

    def approx_of(chunk):
        basis = wide(basis_ref, chunk, width)
        hi, mid, lo = basis[:rows], basis[rows : 2 * rows], basis[2 * rows :]
        return dot_nn(factor, jnp.concatenate([hi, mid, lo, hi, mid, hi], axis=0))

    copies = []

    def send(source, target):
        copy = pltpu.make_async_copy(source, target, sems.at[len(copies)])
        copy.start()
        copies.append(copy)

    update = approx_of(dp_ref[0])
    first = beta_one * moment1[...] + (1.0 - beta_one) * update
    second = beta_two * moment2[...] + (1.0 - beta_two) * update * update
    updated[0] = first
    updated[1] = second
    updated[2] = weight[...] - learn_rate * (first / corr_one) / (jnp.sqrt(second / corr_two) + adam_eps)
    send(updated.at[0], new_moment1)
    send(updated.at[1], new_moment2)
    send(updated.at[2], new_weight)
    for chunk in range(chunks):
        approx = approx_of(chunk)
        field = lower if chunk < chunks // 2 else upper
        first = chunk % (chunks // 2) * count
        for block in range(count):
            columns = slice(block * LANES, (block + 1) * LANES)
            rounded[chunk, :, columns] = (field[first + block] - lanes(approx, block)).astype(BF16)
        send(rounded.at[chunk], new_error.at[:, chunk * width : (chunk + 1) * width])
    for copy in copies:
        copy.wait()


def call(kernel, outs, args, specs=None, out_specs=None, scratch=(), limit=16, flops=0, moved=0):
    return pl.pallas_call(
        kernel,
        out_shape=outs,
        in_specs=specs or [VMEM] * len(args),
        out_specs=out_specs or jax.tree.map(lambda _: VMEM, outs),
        scratch_shapes=scratch,
        compiler_params=pltpu.CompilerParams(vmem_limit_bytes=int(limit * MIB)),
        cost_estimate=pl.CostEstimate(flops=flops, bytes_accessed=moved, transcendentals=0),
    )(*args)


def swap(value, axis, level):
    return lax.ppermute(value, axis, list(enumerate(level)))


def total(value, axis, levels):
    for level in levels:
        value = value + swap(value, axis, level)
    return value


def shards(acts, grad_out, error_buffer, q_prev, weight, moment1, moment2):
    member = lax.axis_index("mp").astype(jnp.int32).reshape(1)
    dp = lax.axis_index("dp").astype(jnp.int32).reshape(1)
    core = dp % 2
    gt, et = grad_out.T, error_buffer.T
    rank, ff = q_prev.shape
    tokens, model = acts.shape[0], et.shape[1]
    chunks, width = 8, model // 8
    array = jax.ShapeDtypeStruct

    gathered = lax.all_gather(acts, "mp", axis=0)

    ring = [acts] + [swap(acts, "mp", level) for level in ALONG_X]
    ring.append(swap(acts, "mp", [(x + 2) % NX * NZ + z for x in range(NX) for z in range(NZ)]))

    half = rank // 2
    table = jnp.asarray(met(ALONG_X + ALONG_Z, NMP))
    blocks = array((NMP, half, LANES), F32)
    mine, send = call(
        error_kernel, [blocks, blocks], (member, core, table, q_prev, et), specs=[SMEM] * 3 + [HBM] * 2,
        scratch=[
            pltpu.VMEM((rank, ff), F32), pltpu.VMEM((chunks, ff, width), BF16), pltpu.VMEM((NMP, rank, LANES), F32),
            pltpu.SemaphoreType.DMA((chunks + 1,)),
        ],
        limit=56, flops=6 * rank * ff * model, moved=2 * ff * model,
    )
    theirs = swap(send, "dp", ALONG_DP[0])
    factor = call(
        token_kernel, array((FACTOR, 8, LANES), F32), (q_prev, gt), specs=[HBM] * 2,
        scratch=[pltpu.VMEM((rank, ff), F32), pltpu.VMEM((ff, tokens), BF16), pltpu.SemaphoreType.DMA((2,))],
        limit=16, flops=6 * rank * ff * tokens, moved=2 * ff * tokens,
    )
    theirs, factor, ring[1:3] = lax.optimization_barrier((theirs, factor, ring[1:3]))
    count = NMP // 2
    message = lambda tiles: array((FACTOR + tiles, 8, LANES), F32)
    kept = lambda count: array((count, half, LANES), F32)
    sent, keep = call(open_kernel, [message(2 * count), kept(count)], (factor, mine, theirs), moved=MIB)
    for place, level in enumerate(ALONG_Z[:0:-1]):
        came = swap(sent, "mp", level)
        count //= 2
        sent, keep = call(halve_kernel, [message(2 * count), kept(count)], (sent, keep, came), moved=MIB)
        if place == 0:
            sent, ring[3] = lax.optimization_barrier((sent, ring[3]))
    came = swap(sent, "mp", ALONG_Z[0])

    keep, send = call(
        piece_kernel, [kept(NX), kept(NX)], (member, core, table, sent, keep, came, *ring),
        specs=[SMEM] * 3 + [VMEM] * 7, moved=MIB,
    )
    keep = keep + swap(send, "dp", ALONG_DP[0])
    keep = total(total(keep, "mp", ALONG_X), "dp", ALONG_DP[1:])
    sent = call(
        start_kernel, array((QUARTER + 2, 8, LANES), F32), (member, core, table, keep, swap(keep, "dp", ALONG_DP[0]), *ring),
        specs=[SMEM] * 3 + [VMEM] * 6, moved=MIB,
    )
    for place, level in enumerate(ALONG_Z):
        came = swap(sent, "mp", level)
        sent = call(double_kernel, array((QUARTER + (4 << place), 8, LANES), F32), (sent, came), moved=MIB)
    sent = jnp.concatenate([sent, swap(sent, "mp", ALONG_X[0])])
    factor, mine = call(
        part_kernel, [array((FACTOR, 8, LANES), F32), array((2 * NMP, 8, LANES), F32)],
        (sent, swap(sent, "mp", ALONG_X[1])), moved=MIB,
    )
    basis, right = call(
        ortho_kernel, [array((NMP, 3 * rank, LANES), BF16), array((rank, ff), F32)],
        (member, core, jnp.asarray(met(ALONG_Z + ALONG_X, NMP)), mine, swap(mine, "dp", ALONG_DP[0]), factor, gt, et),
        specs=[SMEM] * 3 + [VMEM] * 4 + [HBM],
        scratch=[
            pltpu.VMEM((NMP + 1, rank, LANES), F32),
            pltpu.VMEM((chunks, ff, width), BF16),
            pltpu.VMEM((NX, rank, tokens // NX), F32),
            pltpu.SemaphoreType.DMA((chunks,)),
        ],
        limit=24, flops=8 * rank * ff * model, moved=2 * ff * model,
    )
    right, gathered = lax.optimization_barrier((total(right, "dp", ALONG_DP[1:2]), gathered))
    halves = []
    for part, level in enumerate((ALONG_DP[2], ALONG_DP[0])):
        half = call(
            functools.partial(field_kernel, part * NMP // 2), array((NMP // 2, ff, LANES), F32), (gathered, et, gt),
            specs=[HBM] * 3,
            scratch=[
                pltpu.VMEM((NMP // 2, tokens, LANES), BF16),
                pltpu.VMEM((chunks // 2, ff, width), BF16),
                pltpu.VMEM((ff, tokens), BF16),
                pltpu.SemaphoreType.DMA((chunks // 2,)),
                pltpu.SemaphoreType.DMA((chunks // 2,)),
                pltpu.SemaphoreType.DMA,
            ],
            limit=48, flops=model * ff * tokens, moved=10 * MIB,
        )
        right, half = lax.optimization_barrier((total(right, "dp", [level]), half))
        halves.append(half)

    block = array((ff, width), F32)
    outs = call(
        final_kernel,
        [block] * 3 + [array((ff, model), BF16), array((rank, ff), F32)],
        (dp, right, basis, *halves, weight.T, moment1.T, moment2.T),
        specs=[SMEM] + [VMEM] * 7,
        out_specs=[HBM] * 4 + [VMEM],
        scratch=[
            pltpu.VMEM((3, ff, width), F32),
            pltpu.VMEM((chunks, ff, width), BF16),
            pltpu.SemaphoreType.DMA((3 + chunks,)),
        ],
        limit=24, flops=12 * rank * model * ff, moved=20 * MIB,
    )
    new_weight, new_moment1, new_moment2, new_error, q_new = outs
    return (new_weight.T, new_moment1.T, new_moment2.T, new_error.T, q_new)


def solution(mesh):
    placed = (
        P("dp", "mp"),
        P("dp", "mp"),
        P("dp", "mp"),
        P(None, "mp"),
        P("dp", "mp"),
        P("dp", "mp"),
        P("dp", "mp"),
    )
    return jax.shard_map(
        shards,
        mesh=mesh,
        in_specs=placed,
        out_specs=(P("dp", "mp"), P("dp", "mp"), P("dp", "mp"), P("dp", "mp"), P(None, "mp")),
        check_vma=False,
    )
```

```python
import functools

import jax
import jax.numpy as jnp
import numpy as np
from jax import lax
from jax.experimental import pallas as pl
from jax.experimental.pallas import tpu as pltpu
from jax.sharding import PartitionSpec as P

ortho_eps = 1e-08
adam_eps = 1e-08
beta_one = 0.9
beta_two = 0.95
learn_rate = 0.01
corr_one = 1.0 - 0.9**10
corr_two = 1.0 - 0.95**10

NX, NZ, NDP = 4, 8, 8
NMP = NX * NZ
FACTOR = 32
QUARTER = FACTOR // NX
LANES = 128
F32, BF16 = jnp.float32, jnp.bfloat16
MIB = 1 << 20
SMEM = pl.BlockSpec(memory_space=pltpu.SMEM)
VMEM = pl.BlockSpec(memory_space=pltpu.VMEM)
HBM = pl.BlockSpec(memory_space=pltpu.HBM)

RING4 = ([1, 0, 3, 2], [3, 2, 1, 0])
RING8 = ([3, 6, 5, 0, 7, 2, 1, 4], [7, 2, 1, 4, 3, 6, 5, 0], [1, 0, 3, 2, 5, 4, 7, 6])
ALONG_Z = [[x * NZ + to for x in range(NX) for to in level] for level in RING8]
ALONG_X = [[to * NZ + z for to in level for z in range(NZ)] for level in RING4]
ALONG_DP = [[1, 0, 3, 2, 5, 4, 7, 6]] + [[to * 2 + core for to in level for core in range(2)] for level in RING4]


def met(levels, members):
    held = [[member] for member in range(members)]
    for level in levels:
        held = [held[member] + held[level[member]] for member in range(members)]
    return np.array(held, np.int32)


def split3(value):
    hi = value.astype(BF16)
    rest = value - hi.astype(F32)
    mid = rest.astype(BF16)
    lo = (rest - mid.astype(F32)).astype(BF16)
    return jnp.concatenate([hi, mid, lo], axis=0)


def fold3(stacked):
    rows = stacked.shape[0] // 3
    return stacked[:rows] + (stacked[rows : 2 * rows] + stacked[2 * rows :])


def dot_nn(a, b):
    return lax.dot_general(a, b, (((1,), (0,)), ((), ())), preferred_element_type=F32)


def dot_nt(a, b):
    return lax.dot_general(a, b, (((1,), (1,)), ((), ())), preferred_element_type=F32)


def dot_tn(a, b):
    return lax.dot_general(a, b, (((0,), (0,)), ((), ())), preferred_element_type=F32)


def add_all(values):
    while len(values) > 1:
        values = [a + b for a, b in zip(values[::2], values[1::2])] + values[len(values) // 2 * 2 :]
    return values[0]


def lanes(array, block):
    return array[:, block * LANES : (block + 1) * LANES]


def tiles_of(value, out):
    columns = value.shape[1] // LANES
    for row in range(value.shape[0] // 8):
        for column in range(columns):
            out[row * columns + column] = lanes(value[row * 8 : row * 8 + 8], column)


def rows_of(tiles, column, columns, rows):
    return jnp.concatenate([tiles[row * columns + column] for row in range(rows // 8)], axis=0)


def error_kernel(member_ref, core_ref, place_ref, q_hbm, et_hbm, keep, send, q_ref, et_ref, parts, sems):
    count, width = et_ref.shape[0], et_ref.shape[2]
    copies = [
        pltpu.make_async_copy(et_hbm.at[:, chunk * width : (chunk + 1) * width], et_ref.at[chunk], sems.at[chunk])
        for chunk in range(count)
    ]
    first = pltpu.make_async_copy(q_hbm, q_ref, sems.at[count])
    first.start()
    for copy in copies:
        copy.start()
    first.wait()
    split = split3(q_ref[...])
    blocks = width // LANES
    half = parts.shape[1] // 2
    for chunk in range(count):
        copies[chunk].wait()
        part = fold3(dot_nn(split, et_ref[chunk]))
        for block in range(blocks):
            parts[chunk * blocks + block] = lanes(part, block)
    lower = core_ref[0] == 0
    for place in range(NMP):
        block = parts[place_ref[member_ref[0], place]]
        keep[place] = jnp.where(lower, block[:half], block[half:])
        send[place] = jnp.where(lower, block[half:], block[:half])


def token_kernel(q_hbm, gt_hbm, out, q_ref, gt_ref, sems):
    copies = [pltpu.make_async_copy(q_hbm, q_ref, sems.at[0]), pltpu.make_async_copy(gt_hbm, gt_ref, sems.at[1])]
    for copy in copies:
        copy.start()
    for copy in copies:
        copy.wait()
    total = fold3(dot_nn(split3(q_ref[...]), gt_ref[...]))
    width = total.shape[1] // NX
    for x in range(NX):
        tiles_of(total[:, x * width : (x + 1) * width], out.at[x])


def store_blocks(value, out, start):
    for block in range(value.shape[0]):
        out[start + 2 * block] = value[block, :8]
        out[start + 2 * block + 1] = value[block, 8:]


def load_blocks(ref, start, count):
    return jnp.stack(
        [jnp.concatenate([ref[start + 2 * block], ref[start + 2 * block + 1]], axis=0) for block in range(count)]
    )


def deal_kernel(member_ref, place_ref, acts_ref, *outs):
    rows = outs[0].shape[0]
    for place in range(NX):
        x = lax.div(place_ref[member_ref[0], place * NZ], NZ)
        outs[place][...] = acts_ref[pl.ds(pl.multiple_of(x * rows, rows), rows), :]


def open_kernel(member_ref, place_ref, tokens, mine, theirs, message, keep_tokens, keep):
    half = NX // 2
    for place in range(half):
        for out, other in ((keep_tokens, place), (message, place + half)):
            x = lax.div(place_ref[member_ref[0], other * NZ], NZ)
            out[place * QUARTER : (place + 1) * QUARTER] = tokens[x]
    both = mine[...] + theirs[...]
    count = both.shape[0] // 2
    keep[...] = both[:count]
    store_blocks(both[count:], message, half * QUARTER)


def narrow_kernel(tokens, kept, came, message, keep_tokens, keep):
    count, blocks = tokens.shape[0], kept.shape[0]
    factor = tokens[...] + came[:count]
    both = kept[...] + load_blocks(came, count, blocks)
    keep_tokens[...] = factor[: count // 2]
    keep[...] = both[: blocks // 2]
    message[: count // 2] = factor[count // 2 :]
    store_blocks(both[blocks // 2 :], message, count // 2)


def halve_kernel(tokens, kept, came, message, keep):
    blocks = kept.shape[0]
    message[:QUARTER] = tokens[:QUARTER] + came[:QUARTER]
    both = kept[...] + load_blocks(came, QUARTER, blocks)
    keep[...] = both[: blocks // 2]
    store_blocks(both[blocks // 2 :], message, QUARTER)


def piece_kernel(member_ref, core_ref, place_ref, sent, kept, came, *refs):
    acts_refs, keep, send = refs[:NX], refs[NX], refs[NX + 1]
    columns = acts_refs[0].shape[0] // LANES
    half = keep.shape[1]
    lower = core_ref[0] == 0
    errors = (kept[...] + load_blocks(came, QUARTER, 1))[0]
    factor = jnp.concatenate(
        [rows_of(sent, column, columns, FACTOR) + rows_of(came, column, columns, FACTOR) for column in range(columns)],
        axis=1,
    )
    factor = split3(factor)
    for place in range(NX):
        x = lax.div(place_ref[member_ref[0], place * NZ], NZ)
        piece = fold3(dot_nn(factor, acts_refs[place][...]))
        stays = jnp.where(lower, piece[:half], piece[half:])
        keep[x] = stays + errors if place == 0 else stays
        send[x] = jnp.where(lower, piece[half:], piece[:half])


def start_kernel(member_ref, core_ref, place_ref, mine, theirs, *refs):
    acts_refs, message = refs[:NX], refs[NX]
    lower = core_ref[0] == 0
    total = None
    for place in range(NX):
        x = lax.div(place_ref[member_ref[0], place * NZ], NZ)
        first, second = mine[x] * (1.0 / NDP), theirs[x] * (1.0 / NDP)
        panel = jnp.concatenate([jnp.where(lower, first, second), jnp.where(lower, second, first)], axis=0)
        part = dot_nt(split3(panel), acts_refs[place][...])
        total = part if total is None else total + part
    tiles_of(fold3(total), message)
    store_blocks(mine[lax.div(member_ref[0], NZ)][None] * (1.0 / NDP), message, QUARTER)


def double_kernel(sent, came, message):
    count = sent.shape[0] - QUARTER
    message[:QUARTER] = sent[:QUARTER] + came[:QUARTER]
    message[QUARTER : QUARTER + count] = sent[QUARTER:]
    message[QUARTER + count :] = came[QUARTER:]


def part_kernel(sent, came, factor, rows):
    each = sent.shape[0] // 2
    count = each - QUARTER
    for place in range(NX):
        ref = sent if place < 2 else came
        start = place % 2 * each
        factor[place * QUARTER : (place + 1) * QUARTER] = ref[start : start + QUARTER]
        rows[place * count : (place + 1) * count] = ref[start + QUARTER : start + each]


def ortho_kernel(member_ref, core_ref, place_ref, mine, theirs, tokens, gt_ref, et_hbm, split, right, panel, et_ref, factors,
                 sems):
    chunks, width = et_ref.shape[0], et_ref.shape[2]
    copies = [
        pltpu.make_async_copy(et_hbm.at[:, chunk * width : (chunk + 1) * width], et_ref.at[chunk], sems.at[chunk])
        for chunk in range(chunks)
    ]
    for copy in copies:
        copy.start()
    member = member_ref[0]
    lower = core_ref[0] == 0
    half = panel.shape[1] // 2
    for place in range(NMP):
        first = jnp.concatenate([mine[2 * place], mine[2 * place + 1]], axis=0)
        second = jnp.concatenate([theirs[2 * place], theirs[2 * place + 1]], axis=0)
        block = place_ref[member, place]
        panel[block, :half] = jnp.where(lower, first, second)
        panel[block, half:] = jnp.where(lower, second, first)
    square = panel.shape[1:]
    same = lax.broadcasted_iota(jnp.int32, square, 0) == lax.broadcasted_iota(jnp.int32, square, 1)
    panel[NMP] = jnp.where(same, 1.0, 0.0)
    columns = factors.shape[2] // LANES
    for place in range(NX):
        tiles = tokens.at[pl.ds(place * QUARTER, QUARTER)]
        factors[lax.div(place_ref[member, place * NZ], NZ)] = jnp.concatenate(
            [rows_of(tiles, column, columns, FACTOR) for column in range(columns)], axis=1
        )
    factor = jnp.concatenate([factors[x] for x in range(NX)], axis=1)
    grads = fold3(dot_nt(split3(factor), gt_ref[...]))
    for copy in copies:
        copy.wait()
    total = None
    for chunk in range(chunks):
        part = dot_nt(et_ref[chunk], split3(wide(panel, chunk, width)))
        total = part if total is None else total + part
    grads = grads + fold3(total.T)
    blocks, count = NMP, panel.shape[1]
    groups = count // 8

    def inner_of(index):
        first = index // 8
        sums = [None] * groups
        for block in range(blocks):
            row = panel[block, index : index + 1, :]
            for group in range(first, groups):
                term = panel[block, group * 8 : group * 8 + 8, :] * row
                sums[group] = term if sums[group] is None else sums[group] + term
        return [None if s is None else jnp.sum(s, axis=1, keepdims=True) for s in sums]

    order = lax.broadcasted_iota(jnp.int32, (8, 1), 0)
    for index in range(count):
        first, place = index // 8, index % 8
        inner = inner_of(index)
        scale = 1.0 / (jnp.sqrt(inner[first][place : place + 1, :]) + ortho_eps)
        weights = []
        for group in range(first, groups):
            weight = inner[group] * (scale * scale)
            if group == first:
                weight = jnp.where(order > place, weight, 0.0)
            weights.append(weight)
        for block in range(blocks + 1):
            row = panel[block, index : index + 1, :]
            for group in range(first, groups):
                if group == first and place == 7:
                    continue
                rows = slice(group * 8, group * 8 + 8)
                panel[block, rows, :] = panel[block, rows, :] - weights[group - first] * row
            panel[block, index : index + 1, :] = row * scale
    for block in range(blocks):
        split[block] = split3(panel[block])
    turned = lax.dot_general(
        panel[NMP][:, :count], grads, (((1,), (0,)), ((), ())), precision=lax.Precision.HIGHEST,
        preferred_element_type=F32,
    )
    right[...] = turned


def wide(ref, chunk, width):
    count = width // LANES
    return jnp.concatenate([ref[chunk * count + block] for block in range(count)], axis=1)


def field_kernel(start, acts_hbm, et_hbm, gt_hbm, field, acts_v, error_v, gt_v, acts_sems, error_sems, gt_sem):
    chunks, width = error_v.shape[0], error_v.shape[2]
    count = width // LANES
    gt_copy = pltpu.make_async_copy(gt_hbm, gt_v, gt_sem)
    gt_copy.start()
    for chunk in range(chunks):
        blocks = pl.ds(start + chunk * count, count)
        columns = pl.ds(start * LANES + chunk * width, width)
        place = pl.ds(chunk * count, count)
        pltpu.make_async_copy(acts_hbm.at[blocks], acts_v.at[place], acts_sems.at[chunk]).start()
        pltpu.make_async_copy(et_hbm.at[:, columns], error_v.at[chunk], error_sems.at[chunk]).start()
    gt_copy.wait()

    def body(chunk, carry):
        place = pl.ds(chunk * count, count)
        pltpu.make_async_copy(acts_v.at[place], acts_v.at[place], acts_sems.at[chunk]).wait()
        pltpu.make_async_copy(error_v.at[chunk], error_v.at[chunk], error_sems.at[chunk]).wait()
        value = dot_nn(gt_v[...], wide(acts_v, chunk, width)) + error_v[chunk].astype(F32)
        for block in range(count):
            field[chunk * count + block] = lanes(value, block)
        return carry

    lax.fori_loop(0, chunks, body, 0)


def final_kernel(dp_ref, sum_ref, basis_ref, lower, upper, weight, moment1, moment2, new_weight, new_moment1,
                 new_moment2, new_error, q_new, updated, rounded, sems):
    mean = sum_ref[...] * (1.0 / NDP)
    q_new[...] = mean
    rows, ff = mean.shape
    stack = split3(mean.T)
    hi, mid, lo = stack[:ff], stack[ff : 2 * ff], stack[2 * ff :]
    factor = jnp.concatenate([hi, hi, hi, mid, mid, lo], axis=1)
    chunks, width = rounded.shape[0], rounded.shape[2]
    count = width // LANES

    def approx_of(chunk):
        basis = wide(basis_ref, chunk, width)
        hi, mid, lo = basis[:rows], basis[rows : 2 * rows], basis[2 * rows :]
        return dot_nn(factor, jnp.concatenate([hi, mid, lo, hi, mid, hi], axis=0))

    copies = []

    def send(source, target):
        copy = pltpu.make_async_copy(source, target, sems.at[len(copies)])
        copy.start()
        copies.append(copy)

    update = approx_of(dp_ref[0])
    first = beta_one * moment1[...] + (1.0 - beta_one) * update
    second = beta_two * moment2[...] + (1.0 - beta_two) * update * update
    updated[0] = first
    updated[1] = second
    updated[2] = weight[...] - learn_rate * (first / corr_one) / (jnp.sqrt(second / corr_two) + adam_eps)
    send(updated.at[0], new_moment1)
    send(updated.at[1], new_moment2)
    send(updated.at[2], new_weight)
    for chunk in range(chunks):
        approx = approx_of(chunk)
        field = lower if chunk < chunks // 2 else upper
        first = chunk % (chunks // 2) * count
        for block in range(count):
            columns = slice(block * LANES, (block + 1) * LANES)
            rounded[chunk, :, columns] = (field[first + block] - lanes(approx, block)).astype(BF16)
        send(rounded.at[chunk], new_error.at[:, chunk * width : (chunk + 1) * width])
    for copy in copies:
        copy.wait()


def call(kernel, outs, args, specs=None, out_specs=None, scratch=(), limit=16, flops=0, moved=0):
    return pl.pallas_call(
        kernel,
        out_shape=outs,
        in_specs=specs or [VMEM] * len(args),
        out_specs=out_specs or jax.tree.map(lambda _: VMEM, outs),
        scratch_shapes=scratch,
        compiler_params=pltpu.CompilerParams(vmem_limit_bytes=int(limit * MIB)),
        cost_estimate=pl.CostEstimate(flops=flops, bytes_accessed=moved, transcendentals=0),
    )(*args)


def swap(value, axis, level):
    return lax.ppermute(value, axis, list(enumerate(level)))


def total(value, axis, levels):
    for level in levels:
        value = value + swap(value, axis, level)
    return value


def shards(acts, grad_out, error_buffer, q_prev, weight, moment1, moment2):
    member = lax.axis_index("mp").astype(jnp.int32).reshape(1)
    dp = lax.axis_index("dp").astype(jnp.int32).reshape(1)
    core = dp % 2
    gt, et = grad_out.T, error_buffer.T
    rank, ff = q_prev.shape
    tokens, model = acts.shape[0], et.shape[1]
    chunks, width = 8, model // 8
    array = jax.ShapeDtypeStruct

    gathered = lax.all_gather(acts, "mp", axis=0)

    table = jnp.asarray(met(ALONG_Z + ALONG_X, NMP))
    quarters = call(
        deal_kernel, [array((tokens // NX, LANES), BF16)] * NX, (member, table, acts), specs=[SMEM, SMEM, VMEM], moved=MIB
    )
    late, quarters = lax.optimization_barrier((q_prev, quarters))
    across = [(x + 2) % NX * NZ + z for x in range(NX) for z in range(NZ)]
    ring = [quarters[0]] + [swap(rows, "mp", level) for rows, level in zip(quarters[1:], (*ALONG_X, across))]

    half = rank // 2
    blocks = array((NMP, half, LANES), F32)
    mine, send = call(
        error_kernel, [blocks, blocks], (member, core, table, late, et), specs=[SMEM] * 3 + [HBM] * 2,
        scratch=[
            pltpu.VMEM((rank, ff), F32), pltpu.VMEM((chunks, ff, width), BF16), pltpu.VMEM((NMP, rank, LANES), F32),
            pltpu.SemaphoreType.DMA((chunks + 1,)),
        ],
        limit=56, flops=6 * rank * ff * model, moved=2 * ff * model,
    )
    theirs = swap(send, "dp", ALONG_DP[0])
    factor = call(
        token_kernel, array((NX, QUARTER, 8, LANES), F32), (q_prev, gt), specs=[HBM] * 2,
        scratch=[pltpu.VMEM((rank, ff), F32), pltpu.VMEM((ff, tokens), BF16), pltpu.SemaphoreType.DMA((2,))],
        limit=16, flops=6 * rank * ff * tokens, moved=2 * ff * tokens,
    )
    theirs, factor, ring = lax.optimization_barrier((theirs, factor, ring))
    tiles = lambda count: array((count, 8, LANES), F32)
    kept = lambda count: array((count, half, LANES), F32)
    sent, part, keep = call(
        open_kernel, [tiles(48), tiles(2 * QUARTER), kept(16)], (member, table, factor, mine, theirs),
        specs=[SMEM, SMEM] + [VMEM] * 3, moved=MIB,
    )
    came = swap(sent, "mp", ALONG_X[1])
    sent, part, keep = call(narrow_kernel, [tiles(24), tiles(QUARTER), kept(8)], (part, keep, came), moved=MIB)
    came = swap(sent, "mp", ALONG_X[0])
    for count, level in zip((4, 2, 1), ALONG_Z[::-1]):
        sent, keep = call(halve_kernel, [tiles(QUARTER + 2 * count), kept(count)], (part, keep, came), moved=MIB)
        part, came = sent, swap(sent, "mp", level)

    keep, send = call(
        piece_kernel, [kept(NX), kept(NX)], (member, core, table, sent, keep, came, *ring),
        specs=[SMEM] * 3 + [VMEM] * 7, moved=MIB,
    )
    keep = keep + swap(send, "dp", ALONG_DP[0])
    keep = total(total(keep, "mp", ALONG_X), "dp", ALONG_DP[1:])
    sent = call(
        start_kernel, array((QUARTER + 2, 8, LANES), F32), (member, core, table, keep, swap(keep, "dp", ALONG_DP[0]), *ring),
        specs=[SMEM] * 3 + [VMEM] * 6, moved=MIB,
    )
    for place, level in enumerate(ALONG_Z):
        came = swap(sent, "mp", level)
        sent = call(double_kernel, array((QUARTER + (4 << place), 8, LANES), F32), (sent, came), moved=MIB)
    sent = jnp.concatenate([sent, swap(sent, "mp", ALONG_X[0])])
    factor, mine = call(
        part_kernel, [array((FACTOR, 8, LANES), F32), array((2 * NMP, 8, LANES), F32)],
        (sent, swap(sent, "mp", ALONG_X[1])), moved=MIB,
    )
    basis, right = call(
        ortho_kernel, [array((NMP, 3 * rank, LANES), BF16), array((rank, ff), F32)],
        (member, core, table, mine, swap(mine, "dp", ALONG_DP[0]), factor, gt, et),
        specs=[SMEM] * 3 + [VMEM] * 4 + [HBM],
        scratch=[
            pltpu.VMEM((NMP + 1, rank, LANES), F32),
            pltpu.VMEM((chunks, ff, width), BF16),
            pltpu.VMEM((NX, rank, tokens // NX), F32),
            pltpu.SemaphoreType.DMA((chunks,)),
        ],
        limit=24, flops=8 * rank * ff * model, moved=2 * ff * model,
    )
    right, gathered = lax.optimization_barrier((right, gathered))
    halves = []
    for part, level in enumerate(ALONG_DP[1:]):
        half = call(
            functools.partial(field_kernel, part * NMP // 2), array((NMP // 2, ff, LANES), F32), (gathered, et, gt),
            specs=[HBM] * 3,
            scratch=[
                pltpu.VMEM((NMP // 2, tokens, LANES), BF16),
                pltpu.VMEM((chunks // 2, ff, width), BF16),
                pltpu.VMEM((ff, tokens), BF16),
                pltpu.SemaphoreType.DMA((chunks // 2,)),
                pltpu.SemaphoreType.DMA((chunks // 2,)),
                pltpu.SemaphoreType.DMA,
            ],
            limit=48, flops=model * ff * tokens, moved=10 * MIB,
        )
        right, half = lax.optimization_barrier((total(right, "dp", [level]), half))
        halves.append(half)
    right = total(right, "dp", ALONG_DP[:1])

    block = array((ff, width), F32)
    outs = call(
        final_kernel,
        [block] * 3 + [array((ff, model), BF16), array((rank, ff), F32)],
        (dp, right, basis, *halves, weight.T, moment1.T, moment2.T),
        specs=[SMEM] + [VMEM] * 7,
        out_specs=[HBM] * 4 + [VMEM],
        scratch=[
            pltpu.VMEM((3, ff, width), F32),
            pltpu.VMEM((chunks, ff, width), BF16),
            pltpu.SemaphoreType.DMA((3 + chunks,)),
        ],
        limit=24, flops=12 * rank * model * ff, moved=20 * MIB,
    )
    new_weight, new_moment1, new_moment2, new_error, q_new = outs
    return (new_weight.T, new_moment1.T, new_moment2.T, new_error.T, q_new)


def solution(mesh):
    placed = (
        P("dp", "mp"),
        P("dp", "mp"),
        P("dp", "mp"),
        P(None, "mp"),
        P("dp", "mp"),
        P("dp", "mp"),
        P("dp", "mp"),
    )
    return jax.shard_map(
        shards,
        mesh=mesh,
        in_specs=placed,
        out_specs=(P("dp", "mp"), P("dp", "mp"), P("dp", "mp"), P("dp", "mp"), P(None, "mp")),
        check_vma=False,
    )
```

```python
import functools

import jax
import jax.numpy as jnp
import numpy as np
from jax import lax
from jax.experimental import pallas as pl
from jax.experimental.pallas import tpu as pltpu
from jax.sharding import PartitionSpec as P

ortho_eps = 1e-08
adam_eps = 1e-08
beta_one = 0.9
beta_two = 0.95
learn_rate = 0.01
corr_one = 1.0 - 0.9**10
corr_two = 1.0 - 0.95**10

NX, NZ, NDP = 4, 8, 8
NMP = NX * NZ
FACTOR = 32
QUARTER = FACTOR // NX
LANES = 128
F32, BF16 = jnp.float32, jnp.bfloat16
MIB = 1 << 20
SMEM = pl.BlockSpec(memory_space=pltpu.SMEM)
VMEM = pl.BlockSpec(memory_space=pltpu.VMEM)
HBM = pl.BlockSpec(memory_space=pltpu.HBM)

RING4 = ([1, 0, 3, 2], [3, 2, 1, 0])
RING8 = ([3, 6, 5, 0, 7, 2, 1, 4], [7, 2, 1, 4, 3, 6, 5, 0], [1, 0, 3, 2, 5, 4, 7, 6])
ALONG_Z = [[x * NZ + to for x in range(NX) for to in level] for level in RING8]
ALONG_X = [[to * NZ + z for to in level for z in range(NZ)] for level in RING4]
ALONG_DP = [[1, 0, 3, 2, 5, 4, 7, 6]] + [[to * 2 + core for to in level for core in range(2)] for level in RING4]


def met(levels, members):
    held = [[member] for member in range(members)]
    for level in levels:
        held = [held[member] + held[level[member]] for member in range(members)]
    return np.array(held, np.int32)


def split3(value):
    hi = value.astype(BF16)
    rest = value - hi.astype(F32)
    mid = rest.astype(BF16)
    lo = (rest - mid.astype(F32)).astype(BF16)
    return jnp.concatenate([hi, mid, lo], axis=0)


def fold3(stacked):
    rows = stacked.shape[0] // 3
    return stacked[:rows] + (stacked[rows : 2 * rows] + stacked[2 * rows :])


def dot_nn(a, b):
    return lax.dot_general(a, b, (((1,), (0,)), ((), ())), preferred_element_type=F32)


def dot_nt(a, b):
    return lax.dot_general(a, b, (((1,), (1,)), ((), ())), preferred_element_type=F32)


def dot_tn(a, b):
    return lax.dot_general(a, b, (((0,), (0,)), ((), ())), preferred_element_type=F32)


def add_all(values):
    while len(values) > 1:
        values = [a + b for a, b in zip(values[::2], values[1::2])] + values[len(values) // 2 * 2 :]
    return values[0]


def lanes(array, block):
    return array[:, block * LANES : (block + 1) * LANES]


def tiles_of(value, out):
    columns = value.shape[1] // LANES
    for row in range(value.shape[0] // 8):
        for column in range(columns):
            out[row * columns + column] = lanes(value[row * 8 : row * 8 + 8], column)


def rows_of(tiles, column, columns, rows):
    return jnp.concatenate([tiles[row * columns + column] for row in range(rows // 8)], axis=0)


def error_kernel(member_ref, core_ref, place_ref, q_hbm, et_hbm, keep, send, q_ref, et_ref, parts, sems):
    count, width = et_ref.shape[0], et_ref.shape[2]
    copies = [
        pltpu.make_async_copy(et_hbm.at[:, chunk * width : (chunk + 1) * width], et_ref.at[chunk], sems.at[chunk])
        for chunk in range(count)
    ]
    first = pltpu.make_async_copy(q_hbm, q_ref, sems.at[count])
    first.start()
    for copy in copies:
        copy.start()
    first.wait()
    split = split3(q_ref[...])
    blocks = width // LANES
    half = parts.shape[1] // 2
    for chunk in range(count):
        copies[chunk].wait()
        part = fold3(dot_nn(split, et_ref[chunk]))
        for block in range(blocks):
            parts[chunk * blocks + block] = lanes(part, block)
    lower = core_ref[0] == 0
    for place in range(NMP):
        block = parts[place_ref[member_ref[0], place]]
        keep[place] = jnp.where(lower, block[:half], block[half:])
        send[place] = jnp.where(lower, block[half:], block[:half])


def token_kernel(q_hbm, gt_hbm, out, q_ref, gt_ref, sems):
    copies = [pltpu.make_async_copy(q_hbm, q_ref, sems.at[0]), pltpu.make_async_copy(gt_hbm, gt_ref, sems.at[1])]
    for copy in copies:
        copy.start()
    for copy in copies:
        copy.wait()
    total = fold3(dot_nn(split3(q_ref[...]), gt_ref[...]))
    width = total.shape[1] // NX
    for x in range(NX):
        tiles_of(total[:, x * width : (x + 1) * width], out.at[x])


def store_blocks(value, out, start):
    for block in range(value.shape[0]):
        out[start + 2 * block] = value[block, :8]
        out[start + 2 * block + 1] = value[block, 8:]


def load_blocks(ref, start, count):
    return jnp.stack(
        [jnp.concatenate([ref[start + 2 * block], ref[start + 2 * block + 1]], axis=0) for block in range(count)]
    )


def deal_kernel(member_ref, place_ref, acts_ref, *outs):
    rows = outs[0].shape[0]
    for place in range(NX):
        x = lax.div(place_ref[member_ref[0], place * NZ], NZ)
        outs[place][...] = acts_ref[pl.ds(pl.multiple_of(x * rows, rows), rows), :]


def open_kernel(member_ref, place_ref, tokens, mine, theirs, message, keep_tokens, keep):
    half = NX // 2
    for place in range(half):
        for out, other in ((keep_tokens, place), (message, place + half)):
            x = lax.div(place_ref[member_ref[0], other * NZ], NZ)
            out[place * QUARTER : (place + 1) * QUARTER] = tokens[x]
    both = mine[...] + theirs[...]
    count = both.shape[0] // 2
    keep[...] = both[:count]
    store_blocks(both[count:], message, half * QUARTER)


def narrow_kernel(tokens, kept, came, message, keep_tokens, keep):
    count, blocks = tokens.shape[0], kept.shape[0]
    factor = tokens[...] + came[:count]
    both = kept[...] + load_blocks(came, count, blocks)
    keep_tokens[...] = factor[: count // 2]
    keep[...] = both[: blocks // 2]
    message[: count // 2] = factor[count // 2 :]
    store_blocks(both[blocks // 2 :], message, count // 2)


def halve_kernel(tokens, kept, came, message, keep):
    blocks = kept.shape[0]
    message[:QUARTER] = tokens[:QUARTER] + came[:QUARTER]
    both = kept[...] + load_blocks(came, QUARTER, blocks)
    keep[...] = both[: blocks // 2]
    store_blocks(both[blocks // 2 :], message, QUARTER)


def piece_kernel(member_ref, core_ref, place_ref, sent, kept, came, *refs):
    acts_refs, keep, send = refs[:NX], refs[NX], refs[NX + 1]
    columns = acts_refs[0].shape[0] // LANES
    half = keep.shape[1]
    lower = core_ref[0] == 0
    errors = (kept[...] + load_blocks(came, QUARTER, 1))[0]
    factor = jnp.concatenate(
        [rows_of(sent, column, columns, FACTOR) + rows_of(came, column, columns, FACTOR) for column in range(columns)],
        axis=1,
    )
    factor = split3(factor)
    for place in range(NX):
        x = lax.div(place_ref[member_ref[0], place * NZ], NZ)
        piece = fold3(dot_nn(factor, acts_refs[place][...]))
        stays = jnp.where(lower, piece[:half], piece[half:])
        keep[x] = stays + errors if place == 0 else stays
        send[x] = jnp.where(lower, piece[half:], piece[:half])


def start_kernel(member_ref, core_ref, place_ref, mine, theirs, *refs):
    acts_refs, message = refs[:NX], refs[NX]
    lower = core_ref[0] == 0
    total = None
    for place in range(NX):
        x = lax.div(place_ref[member_ref[0], place * NZ], NZ)
        first, second = mine[x] * (1.0 / NDP), theirs[x] * (1.0 / NDP)
        panel = jnp.concatenate([jnp.where(lower, first, second), jnp.where(lower, second, first)], axis=0)
        part = dot_nt(split3(panel), acts_refs[place][...])
        total = part if total is None else total + part
    tiles_of(fold3(total), message)
    store_blocks(mine[lax.div(member_ref[0], NZ)][None] * (1.0 / NDP), message, QUARTER)


def double_kernel(sent, came, message):
    count = sent.shape[0] - QUARTER
    message[:QUARTER] = sent[:QUARTER] + came[:QUARTER]
    message[QUARTER : QUARTER + count] = sent[QUARTER:]
    message[QUARTER + count :] = came[QUARTER:]


def part_kernel(sent, came, factor, rows):
    each = sent.shape[0] // 2
    count = each - QUARTER
    for place in range(NX):
        ref = sent if place < 2 else came
        start = place % 2 * each
        factor[place * QUARTER : (place + 1) * QUARTER] = ref[start : start + QUARTER]
        rows[place * count : (place + 1) * count] = ref[start + QUARTER : start + each]


def ortho_kernel(member_ref, core_ref, place_ref, mine, theirs, tokens, gt_ref, et_hbm, split, right, panel, et_ref, factors,
                 sems):
    chunks, width = et_ref.shape[0], et_ref.shape[2]
    copies = [
        pltpu.make_async_copy(et_hbm.at[:, chunk * width : (chunk + 1) * width], et_ref.at[chunk], sems.at[chunk])
        for chunk in range(chunks)
    ]
    for copy in copies:
        copy.start()
    member = member_ref[0]
    lower = core_ref[0] == 0
    half = panel.shape[1] // 2
    for place in range(NMP):
        first = jnp.concatenate([mine[2 * place], mine[2 * place + 1]], axis=0)
        second = jnp.concatenate([theirs[2 * place], theirs[2 * place + 1]], axis=0)
        block = place_ref[member, place]
        panel[block, :half] = jnp.where(lower, first, second)
        panel[block, half:] = jnp.where(lower, second, first)
    square = panel.shape[1:]
    same = lax.broadcasted_iota(jnp.int32, square, 0) == lax.broadcasted_iota(jnp.int32, square, 1)
    panel[NMP] = jnp.where(same, 1.0, 0.0)
    columns = factors.shape[2] // LANES
    for place in range(NX):
        tiles = tokens.at[pl.ds(place * QUARTER, QUARTER)]
        factors[lax.div(place_ref[member, place * NZ], NZ)] = jnp.concatenate(
            [rows_of(tiles, column, columns, FACTOR) for column in range(columns)], axis=1
        )
    factor = jnp.concatenate([factors[x] for x in range(NX)], axis=1)
    grads = fold3(dot_nt(split3(factor), gt_ref[...]))
    for copy in copies:
        copy.wait()
    total = None
    for chunk in range(chunks):
        part = dot_nt(et_ref[chunk], split3(wide(panel, chunk, width)))
        total = part if total is None else total + part
    grads = grads + fold3(total.T)
    blocks, count = NMP, panel.shape[1]
    groups = count // 8

    def inner_of(index):
        first = index // 8
        sums = [None] * groups
        for block in range(blocks):
            row = panel[block, index : index + 1, :]
            for group in range(first, groups):
                term = panel[block, group * 8 : group * 8 + 8, :] * row
                sums[group] = term if sums[group] is None else sums[group] + term
        return [None if s is None else jnp.sum(s, axis=1, keepdims=True) for s in sums]

    order = lax.broadcasted_iota(jnp.int32, (8, 1), 0)
    for index in range(count):
        first, place = index // 8, index % 8
        inner = inner_of(index)
        scale = 1.0 / (jnp.sqrt(inner[first][place : place + 1, :]) + ortho_eps)
        weights = []
        for group in range(first, groups):
            weight = inner[group] * (scale * scale)
            if group == first:
                weight = jnp.where(order > place, weight, 0.0)
            weights.append(weight)
        for block in range(blocks + 1):
            row = panel[block, index : index + 1, :]
            for group in range(first, groups):
                if group == first and place == 7:
                    continue
                rows = slice(group * 8, group * 8 + 8)
                panel[block, rows, :] = panel[block, rows, :] - weights[group - first] * row
            panel[block, index : index + 1, :] = row * scale
    for block in range(blocks):
        split[block] = split3(panel[block])
    turned = lax.dot_general(
        panel[NMP][:, :count], grads, (((1,), (0,)), ((), ())), precision=lax.Precision.HIGHEST,
        preferred_element_type=F32,
    )
    right[...] = turned


def wide(ref, chunk, width):
    count = width // LANES
    return jnp.concatenate([ref[chunk * count + block] for block in range(count)], axis=1)


def field_kernel(start, acts_hbm, et_hbm, gt_hbm, field, acts_v, error_v, gt_v, acts_sems, error_sems, gt_sem):
    chunks, width = error_v.shape[0], error_v.shape[2]
    count = width // LANES
    gt_copy = pltpu.make_async_copy(gt_hbm, gt_v, gt_sem)
    gt_copy.start()
    for chunk in range(chunks):
        blocks = pl.ds(start + chunk * count, count)
        columns = pl.ds(start * LANES + chunk * width, width)
        place = pl.ds(chunk * count, count)
        pltpu.make_async_copy(acts_hbm.at[blocks], acts_v.at[place], acts_sems.at[chunk]).start()
        pltpu.make_async_copy(et_hbm.at[:, columns], error_v.at[chunk], error_sems.at[chunk]).start()
    gt_copy.wait()

    def body(chunk, carry):
        place = pl.ds(chunk * count, count)
        pltpu.make_async_copy(acts_v.at[place], acts_v.at[place], acts_sems.at[chunk]).wait()
        pltpu.make_async_copy(error_v.at[chunk], error_v.at[chunk], error_sems.at[chunk]).wait()
        value = dot_nn(gt_v[...], wide(acts_v, chunk, width)) + error_v[chunk].astype(F32)
        for block in range(count):
            field[chunk * count + block] = lanes(value, block)
        return carry

    lax.fori_loop(0, chunks, body, 0)


def final_kernel(dp_ref, sum_ref, basis_ref, lower, upper, weight, moment1, moment2, new_weight, new_moment1,
                 new_moment2, new_error, q_new, updated, rounded, sems):
    mean = sum_ref[...] * (1.0 / NDP)
    q_new[...] = mean
    rows, ff = mean.shape
    stack = split3(mean.T)
    hi, mid, lo = stack[:ff], stack[ff : 2 * ff], stack[2 * ff :]
    factor = jnp.concatenate([hi, hi, hi, mid, mid, lo], axis=1)
    chunks, width = rounded.shape[0], rounded.shape[2]
    count = width // LANES

    def approx_of(chunk):
        basis = wide(basis_ref, chunk, width)
        hi, mid, lo = basis[:rows], basis[rows : 2 * rows], basis[2 * rows :]
        return dot_nn(factor, jnp.concatenate([hi, mid, lo, hi, mid, hi], axis=0))

    copies = []

    def send(source, target):
        copy = pltpu.make_async_copy(source, target, sems.at[len(copies)])
        copy.start()
        copies.append(copy)

    update = approx_of(dp_ref[0])
    first = beta_one * moment1[...] + (1.0 - beta_one) * update
    second = beta_two * moment2[...] + (1.0 - beta_two) * update * update
    updated[0] = first
    updated[1] = second
    updated[2] = weight[...] - learn_rate * (first / corr_one) / (jnp.sqrt(second / corr_two) + adam_eps)
    send(updated.at[0], new_moment1)
    send(updated.at[1], new_moment2)
    send(updated.at[2], new_weight)
    for chunk in range(chunks):
        approx = approx_of(chunk)
        field = lower if chunk < chunks // 2 else upper
        first = chunk % (chunks // 2) * count
        for block in range(count):
            columns = slice(block * LANES, (block + 1) * LANES)
            rounded[chunk, :, columns] = (field[first + block] - lanes(approx, block)).astype(BF16)
        send(rounded.at[chunk], new_error.at[:, chunk * width : (chunk + 1) * width])
    for copy in copies:
        copy.wait()


def call(kernel, outs, args, specs=None, out_specs=None, scratch=(), limit=16, flops=0, moved=0):
    return pl.pallas_call(
        kernel,
        out_shape=outs,
        in_specs=specs or [VMEM] * len(args),
        out_specs=out_specs or jax.tree.map(lambda _: VMEM, outs),
        scratch_shapes=scratch,
        compiler_params=pltpu.CompilerParams(vmem_limit_bytes=int(limit * MIB)),
        cost_estimate=pl.CostEstimate(flops=flops, bytes_accessed=moved, transcendentals=0),
    )(*args)


def swap(value, axis, level):
    return lax.ppermute(value, axis, list(enumerate(level)))


def total(value, axis, levels):
    for level in levels:
        value = value + swap(value, axis, level)
    return value


def shards(acts, grad_out, error_buffer, q_prev, weight, moment1, moment2):
    member = lax.axis_index("mp").astype(jnp.int32).reshape(1)
    dp = lax.axis_index("dp").astype(jnp.int32).reshape(1)
    core = dp % 2
    gt, et = grad_out.T, error_buffer.T
    rank, ff = q_prev.shape
    tokens, model = acts.shape[0], et.shape[1]
    chunks, width = 8, model // 8
    array = jax.ShapeDtypeStruct

    gathered = lax.all_gather(acts, "mp", axis=0)

    table = jnp.asarray(met(ALONG_Z + ALONG_X, NMP))

    half = rank // 2
    blocks = array((NMP, half, LANES), F32)
    mine, send = call(
        error_kernel, [blocks, blocks], (member, core, table, q_prev, et), specs=[SMEM] * 3 + [HBM] * 2,
        scratch=[
            pltpu.VMEM((rank, ff), F32), pltpu.VMEM((chunks, ff, width), BF16), pltpu.VMEM((NMP, rank, LANES), F32),
            pltpu.SemaphoreType.DMA((chunks + 1,)),
        ],
        limit=56, flops=6 * rank * ff * model, moved=2 * ff * model,
    )
    theirs = swap(send, "dp", ALONG_DP[0])
    factor = call(
        token_kernel, array((NX, QUARTER, 8, LANES), F32), (q_prev, gt), specs=[HBM] * 2,
        scratch=[pltpu.VMEM((rank, ff), F32), pltpu.VMEM((ff, tokens), BF16), pltpu.SemaphoreType.DMA((2,))],
        limit=16, flops=6 * rank * ff * tokens, moved=2 * ff * tokens,
    )
    tiles = lambda count: array((count, 8, LANES), F32)
    kept = lambda count: array((count, half, LANES), F32)
    sent, part, keep = call(
        open_kernel, [tiles(48), tiles(2 * QUARTER), kept(16)], (member, table, factor, mine, theirs),
        specs=[SMEM, SMEM] + [VMEM] * 3, moved=MIB,
    )
    sent, late = lax.optimization_barrier((sent, acts))
    quarters = call(
        deal_kernel, [array((tokens // NX, LANES), BF16)] * NX, (member, table, late), specs=[SMEM, SMEM, VMEM], moved=MIB
    )
    across = [(x + 2) % NX * NZ + z for x in range(NX) for z in range(NZ)]
    ring = [quarters[0]] + [swap(rows, "mp", level) for rows, level in zip(quarters[1:], (*ALONG_X, across))]
    came = swap(sent, "mp", ALONG_X[1])
    sent, part, keep = call(narrow_kernel, [tiles(24), tiles(QUARTER), kept(8)], (part, keep, came), moved=MIB)
    came = swap(sent, "mp", ALONG_X[0])
    for count, level in zip((4, 2, 1), ALONG_Z[::-1]):
        sent, keep = call(halve_kernel, [tiles(QUARTER + 2 * count), kept(count)], (part, keep, came), moved=MIB)
        if count == 1:
            sent, ring = lax.optimization_barrier((sent, ring))
        part, came = sent, swap(sent, "mp", level)

    keep, send = call(
        piece_kernel, [kept(NX), kept(NX)], (member, core, table, sent, keep, came, *ring),
        specs=[SMEM] * 3 + [VMEM] * 7, moved=MIB,
    )
    keep = keep + swap(send, "dp", ALONG_DP[0])
    keep = total(total(keep, "mp", ALONG_X), "dp", ALONG_DP[1:])
    sent = call(
        start_kernel, array((QUARTER + 2, 8, LANES), F32), (member, core, table, keep, swap(keep, "dp", ALONG_DP[0]), *ring),
        specs=[SMEM] * 3 + [VMEM] * 6, moved=MIB,
    )
    for place, level in enumerate(ALONG_Z):
        came = swap(sent, "mp", level)
        sent = call(double_kernel, array((QUARTER + (4 << place), 8, LANES), F32), (sent, came), moved=MIB)
    sent = jnp.concatenate([sent, swap(sent, "mp", ALONG_X[0])])
    factor, mine = call(
        part_kernel, [array((FACTOR, 8, LANES), F32), array((2 * NMP, 8, LANES), F32)],
        (sent, swap(sent, "mp", ALONG_X[1])), moved=MIB,
    )
    basis, right = call(
        ortho_kernel, [array((NMP, 3 * rank, LANES), BF16), array((rank, ff), F32)],
        (member, core, table, mine, swap(mine, "dp", ALONG_DP[0]), factor, gt, et),
        specs=[SMEM] * 3 + [VMEM] * 4 + [HBM],
        scratch=[
            pltpu.VMEM((NMP + 1, rank, LANES), F32),
            pltpu.VMEM((chunks, ff, width), BF16),
            pltpu.VMEM((NX, rank, tokens // NX), F32),
            pltpu.SemaphoreType.DMA((chunks,)),
        ],
        limit=24, flops=8 * rank * ff * model, moved=2 * ff * model,
    )
    right, gathered = lax.optimization_barrier((right, gathered))
    halves = []
    for part, level in enumerate(ALONG_DP[1:]):
        half = call(
            functools.partial(field_kernel, part * NMP // 2), array((NMP // 2, ff, LANES), F32), (gathered, et, gt),
            specs=[HBM] * 3,
            scratch=[
                pltpu.VMEM((NMP // 2, tokens, LANES), BF16),
                pltpu.VMEM((chunks // 2, ff, width), BF16),
                pltpu.VMEM((ff, tokens), BF16),
                pltpu.SemaphoreType.DMA((chunks // 2,)),
                pltpu.SemaphoreType.DMA((chunks // 2,)),
                pltpu.SemaphoreType.DMA,
            ],
            limit=48, flops=model * ff * tokens, moved=10 * MIB,
        )
        right, half = lax.optimization_barrier((total(right, "dp", [level]), half))
        halves.append(half)
    right = total(right, "dp", ALONG_DP[:1])

    block = array((ff, width), F32)
    outs = call(
        final_kernel,
        [block] * 3 + [array((ff, model), BF16), array((rank, ff), F32)],
        (dp, right, basis, *halves, weight.T, moment1.T, moment2.T),
        specs=[SMEM] + [VMEM] * 7,
        out_specs=[HBM] * 4 + [VMEM],
        scratch=[
            pltpu.VMEM((3, ff, width), F32),
            pltpu.VMEM((chunks, ff, width), BF16),
            pltpu.SemaphoreType.DMA((3 + chunks,)),
        ],
        limit=24, flops=12 * rank * model * ff, moved=20 * MIB,
    )
    new_weight, new_moment1, new_moment2, new_error, q_new = outs
    return (new_weight.T, new_moment1.T, new_moment2.T, new_error.T, q_new)


def solution(mesh):
    placed = (
        P("dp", "mp"),
        P("dp", "mp"),
        P("dp", "mp"),
        P(None, "mp"),
        P("dp", "mp"),
        P("dp", "mp"),
        P("dp", "mp"),
    )
    return jax.shard_map(
        shards,
        mesh=mesh,
        in_specs=placed,
        out_specs=(P("dp", "mp"), P("dp", "mp"), P("dp", "mp"), P("dp", "mp"), P(None, "mp")),
        check_vma=False,
    )
```

```python
import functools

import jax
import jax.numpy as jnp
import numpy as np
from jax import lax
from jax.experimental import pallas as pl
from jax.experimental.pallas import tpu as pltpu
from jax.sharding import PartitionSpec as P

ortho_eps = 1e-08
adam_eps = 1e-08
beta_one = 0.9
beta_two = 0.95
learn_rate = 0.01
corr_one = 1.0 - 0.9**10
corr_two = 1.0 - 0.95**10

NX, NZ, NDP = 4, 8, 8
NMP = NX * NZ
FACTOR = 32
QUARTER = FACTOR // NX
LANES = 128
F32, BF16 = jnp.float32, jnp.bfloat16
MIB = 1 << 20
SMEM = pl.BlockSpec(memory_space=pltpu.SMEM)
VMEM = pl.BlockSpec(memory_space=pltpu.VMEM)
HBM = pl.BlockSpec(memory_space=pltpu.HBM)

RING4 = ([1, 0, 3, 2], [3, 2, 1, 0])
RING8 = ([3, 6, 5, 0, 7, 2, 1, 4], [7, 2, 1, 4, 3, 6, 5, 0], [1, 0, 3, 2, 5, 4, 7, 6])
ALONG_Z = [[x * NZ + to for x in range(NX) for to in level] for level in RING8]
ALONG_X = [[to * NZ + z for to in level for z in range(NZ)] for level in RING4]
ALONG_DP = [[1, 0, 3, 2, 5, 4, 7, 6]] + [[to * 2 + core for to in level for core in range(2)] for level in RING4]


def met(levels, members):
    held = [[member] for member in range(members)]
    for level in levels:
        held = [held[member] + held[level[member]] for member in range(members)]
    return np.array(held, np.int32)


def x_at(place):
    x = lax.div(lax.axis_index("mp"), NZ)
    if place & 2:
        x = NX - 1 - x
    if place & 1:
        x = x + 1 - 2 * lax.rem(x, 2)
    return x


def member_at(place):
    z = lax.rem(lax.axis_index("mp"), NZ)
    for bit, far in ((4, 1), (2, -1), (1, 3)):
        if place & bit:
            z = lax.rem(z + NZ + far * (1 - 2 * lax.rem(z, 2)), NZ)
    return x_at(place // NZ) * NZ + z


def lower_core():
    return lax.rem(lax.axis_index("dp"), 2) == 0


def split3(value):
    hi = value.astype(BF16)
    rest = value - hi.astype(F32)
    mid = rest.astype(BF16)
    lo = (rest - mid.astype(F32)).astype(BF16)
    return jnp.concatenate([hi, mid, lo], axis=0)


def fold3(stacked):
    rows = stacked.shape[0] // 3
    return stacked[:rows] + (stacked[rows : 2 * rows] + stacked[2 * rows :])


def dot_nn(a, b):
    return lax.dot_general(a, b, (((1,), (0,)), ((), ())), preferred_element_type=F32)


def dot_nt(a, b):
    return lax.dot_general(a, b, (((1,), (1,)), ((), ())), preferred_element_type=F32)


def dot_tn(a, b):
    return lax.dot_general(a, b, (((0,), (0,)), ((), ())), preferred_element_type=F32)


def add_all(values):
    while len(values) > 1:
        values = [a + b for a, b in zip(values[::2], values[1::2])] + values[len(values) // 2 * 2 :]
    return values[0]


def lanes(array, block):
    return array[:, block * LANES : (block + 1) * LANES]


def tiles_of(value, out):
    columns = value.shape[1] // LANES
    for row in range(value.shape[0] // 8):
        for column in range(columns):
            out[row * columns + column] = lanes(value[row * 8 : row * 8 + 8], column)


def rows_of(tiles, column, columns, rows):
    return jnp.concatenate([tiles[row * columns + column] for row in range(rows // 8)], axis=0)


def error_kernel(q_hbm, et_hbm, keep, send, q_ref, et_ref, parts, sems):
    count, width = et_ref.shape[0], et_ref.shape[2]
    copies = [
        pltpu.make_async_copy(et_hbm.at[:, chunk * width : (chunk + 1) * width], et_ref.at[chunk], sems.at[chunk])
        for chunk in range(count)
    ]
    first = pltpu.make_async_copy(q_hbm, q_ref, sems.at[count])
    first.start()
    for copy in copies:
        copy.start()
    first.wait()
    split = split3(q_ref[...])
    blocks = width // LANES
    half = parts.shape[1] // 2
    for chunk in range(count):
        copies[chunk].wait()
        part = fold3(dot_nn(split, et_ref[chunk]))
        for block in range(blocks):
            parts[chunk * blocks + block] = lanes(part, block)
    lower = lower_core()
    for place in range(NMP):
        block = parts[member_at(place)]
        keep[place] = jnp.where(lower, block[:half], block[half:])
        send[place] = jnp.where(lower, block[half:], block[:half])


def token_kernel(q_hbm, gt_hbm, out, q_ref, gt_ref, sems):
    copies = [pltpu.make_async_copy(q_hbm, q_ref, sems.at[0]), pltpu.make_async_copy(gt_hbm, gt_ref, sems.at[1])]
    for copy in copies:
        copy.start()
    for copy in copies:
        copy.wait()
    total = fold3(dot_nn(split3(q_ref[...]), gt_ref[...]))
    width = total.shape[1] // NX
    for x in range(NX):
        tiles_of(total[:, x * width : (x + 1) * width], out.at[x])


def store_blocks(value, out, start):
    for block in range(value.shape[0]):
        out[start + 2 * block] = value[block, :8]
        out[start + 2 * block + 1] = value[block, 8:]


def load_blocks(ref, start, count):
    return jnp.stack(
        [jnp.concatenate([ref[start + 2 * block], ref[start + 2 * block + 1]], axis=0) for block in range(count)]
    )


def deal_kernel(acts_ref, *outs):
    rows = outs[0].shape[0]
    for place in range(NX):
        x = x_at(place)
        outs[place][...] = acts_ref[pl.ds(pl.multiple_of(x * rows, rows), rows), :]


def open_kernel(tokens, mine, theirs, message, keep_tokens, keep):
    half = NX // 2
    for place in range(half):
        for out, other in ((keep_tokens, place), (message, place + half)):
            x = x_at(other)
            out[place * QUARTER : (place + 1) * QUARTER] = tokens[x]
    both = mine[...] + theirs[...]
    count = both.shape[0] // 2
    keep[...] = both[:count]
    store_blocks(both[count:], message, half * QUARTER)


def narrow_kernel(tokens, kept, came, message, keep_tokens, keep):
    count, blocks = tokens.shape[0], kept.shape[0]
    factor = tokens[...] + came[:count]
    both = kept[...] + load_blocks(came, count, blocks)
    keep_tokens[...] = factor[: count // 2]
    keep[...] = both[: blocks // 2]
    message[: count // 2] = factor[count // 2 :]
    store_blocks(both[blocks // 2 :], message, count // 2)


def halve_kernel(tokens, kept, came, message, keep):
    blocks = kept.shape[0]
    message[:QUARTER] = tokens[:QUARTER] + came[:QUARTER]
    both = kept[...] + load_blocks(came, QUARTER, blocks)
    keep[...] = both[: blocks // 2]
    store_blocks(both[blocks // 2 :], message, QUARTER)


def piece_kernel(sent, kept, came, *refs):
    acts_refs, keep, send = refs[:NX], refs[NX], refs[NX + 1]
    columns = acts_refs[0].shape[0] // LANES
    half = keep.shape[1]
    lower = lower_core()
    errors = (kept[...] + load_blocks(came, QUARTER, 1))[0]
    factor = jnp.concatenate(
        [rows_of(sent, column, columns, FACTOR) + rows_of(came, column, columns, FACTOR) for column in range(columns)],
        axis=1,
    )
    factor = split3(factor)
    for place in range(NX):
        x = x_at(place)
        piece = fold3(dot_nn(factor, acts_refs[place][...]))
        stays = jnp.where(lower, piece[:half], piece[half:])
        keep[x] = stays + errors if place == 0 else stays
        send[x] = jnp.where(lower, piece[half:], piece[:half])


def start_kernel(mine, theirs, *refs):
    acts_refs, message = refs[:NX], refs[NX]
    lower = lower_core()
    total = None
    for place in range(NX):
        x = x_at(place)
        first, second = mine[x] * (1.0 / NDP), theirs[x] * (1.0 / NDP)
        panel = jnp.concatenate([jnp.where(lower, first, second), jnp.where(lower, second, first)], axis=0)
        part = dot_nt(split3(panel), acts_refs[place][...])
        total = part if total is None else total + part
    tiles_of(fold3(total), message)
    store_blocks(mine[x_at(0)][None] * (1.0 / NDP), message, QUARTER)


def double_kernel(sent, came, message):
    count = sent.shape[0] - QUARTER
    message[:QUARTER] = sent[:QUARTER] + came[:QUARTER]
    message[QUARTER : QUARTER + count] = sent[QUARTER:]
    message[QUARTER + count :] = came[QUARTER:]


def part_kernel(sent, came, factor, rows):
    each = sent.shape[0] // 2
    count = each - QUARTER
    for place in range(NX):
        ref = sent if place < 2 else came
        start = place % 2 * each
        factor[place * QUARTER : (place + 1) * QUARTER] = ref[start : start + QUARTER]
        rows[place * count : (place + 1) * count] = ref[start + QUARTER : start + each]


def ortho_kernel(mine, theirs, tokens, gt_ref, et_hbm, split, right, panel, et_ref, factors,
                 sems):
    chunks, width = et_ref.shape[0], et_ref.shape[2]
    copies = [
        pltpu.make_async_copy(et_hbm.at[:, chunk * width : (chunk + 1) * width], et_ref.at[chunk], sems.at[chunk])
        for chunk in range(chunks)
    ]
    for copy in copies:
        copy.start()
    lower = lower_core()
    half = panel.shape[1] // 2
    for place in range(NMP):
        first = jnp.concatenate([mine[2 * place], mine[2 * place + 1]], axis=0)
        second = jnp.concatenate([theirs[2 * place], theirs[2 * place + 1]], axis=0)
        block = member_at(place)
        panel[block, :half] = jnp.where(lower, first, second)
        panel[block, half:] = jnp.where(lower, second, first)
    square = panel.shape[1:]
    same = lax.broadcasted_iota(jnp.int32, square, 0) == lax.broadcasted_iota(jnp.int32, square, 1)
    panel[NMP] = jnp.where(same, 1.0, 0.0)
    columns = factors.shape[2] // LANES
    for place in range(NX):
        tiles = tokens.at[pl.ds(place * QUARTER, QUARTER)]
        factors[x_at(place)] = jnp.concatenate(
            [rows_of(tiles, column, columns, FACTOR) for column in range(columns)], axis=1
        )
    factor = jnp.concatenate([factors[x] for x in range(NX)], axis=1)
    grads = fold3(dot_nt(split3(factor), gt_ref[...]))
    for copy in copies:
        copy.wait()
    total = None
    for chunk in range(chunks):
        part = dot_nt(et_ref[chunk], split3(wide(panel, chunk, width)))
        total = part if total is None else total + part
    grads = grads + fold3(total.T)
    blocks, count = NMP, panel.shape[1]
    groups = count // 8

    def inner_of(index):
        first = index // 8
        sums = [None] * groups
        for block in range(blocks):
            row = panel[block, index : index + 1, :]
            for group in range(first, groups):
                term = panel[block, group * 8 : group * 8 + 8, :] * row
                sums[group] = term if sums[group] is None else sums[group] + term
        return [None if s is None else jnp.sum(s, axis=1, keepdims=True) for s in sums]

    order = lax.broadcasted_iota(jnp.int32, (8, 1), 0)
    for index in range(count):
        first, place = index // 8, index % 8
        inner = inner_of(index)
        scale = 1.0 / (jnp.sqrt(inner[first][place : place + 1, :]) + ortho_eps)
        weights = []
        for group in range(first, groups):
            weight = inner[group] * (scale * scale)
            if group == first:
                weight = jnp.where(order > place, weight, 0.0)
            weights.append(weight)
        for block in range(blocks + 1):
            row = panel[block, index : index + 1, :]
            for group in range(first, groups):
                if group == first and place == 7:
                    continue
                rows = slice(group * 8, group * 8 + 8)
                panel[block, rows, :] = panel[block, rows, :] - weights[group - first] * row
            panel[block, index : index + 1, :] = row * scale
    for block in range(blocks):
        split[block] = split3(panel[block])
    turned = lax.dot_general(
        panel[NMP][:, :count], grads, (((1,), (0,)), ((), ())), precision=lax.Precision.HIGHEST,
        preferred_element_type=F32,
    )
    right[...] = turned


def wide(ref, chunk, width):
    count = width // LANES
    return jnp.concatenate([ref[chunk * count + block] for block in range(count)], axis=1)


def field_kernel(start, acts_hbm, et_hbm, gt_hbm, field, acts_v, error_v, gt_v, acts_sems, error_sems, gt_sem):
    chunks, width = error_v.shape[0], error_v.shape[2]
    count = width // LANES
    gt_copy = pltpu.make_async_copy(gt_hbm, gt_v, gt_sem)
    gt_copy.start()
    for chunk in range(chunks):
        blocks = pl.ds(start + chunk * count, count)
        columns = pl.ds(start * LANES + chunk * width, width)
        place = pl.ds(chunk * count, count)
        pltpu.make_async_copy(acts_hbm.at[blocks], acts_v.at[place], acts_sems.at[chunk]).start()
        pltpu.make_async_copy(et_hbm.at[:, columns], error_v.at[chunk], error_sems.at[chunk]).start()
    gt_copy.wait()

    def body(chunk, carry):
        place = pl.ds(chunk * count, count)
        pltpu.make_async_copy(acts_v.at[place], acts_v.at[place], acts_sems.at[chunk]).wait()
        pltpu.make_async_copy(error_v.at[chunk], error_v.at[chunk], error_sems.at[chunk]).wait()
        value = dot_nn(gt_v[...], wide(acts_v, chunk, width)) + error_v[chunk].astype(F32)
        for block in range(count):
            field[chunk * count + block] = lanes(value, block)
        return carry

    lax.fori_loop(0, chunks, body, 0)


def final_kernel(sum_ref, basis_ref, lower, upper, weight, moment1, moment2, new_weight, new_moment1,
                 new_moment2, new_error, q_new, updated, rounded, sems):
    mean = sum_ref[...] * (1.0 / NDP)
    q_new[...] = mean
    rows, ff = mean.shape
    stack = split3(mean.T)
    hi, mid, lo = stack[:ff], stack[ff : 2 * ff], stack[2 * ff :]
    factor = jnp.concatenate([hi, hi, hi, mid, mid, lo], axis=1)
    chunks, width = rounded.shape[0], rounded.shape[2]
    count = width // LANES

    def approx_of(chunk):
        basis = wide(basis_ref, chunk, width)
        hi, mid, lo = basis[:rows], basis[rows : 2 * rows], basis[2 * rows :]
        return dot_nn(factor, jnp.concatenate([hi, mid, lo, hi, mid, hi], axis=0))

    copies = []

    def send(source, target):
        copy = pltpu.make_async_copy(source, target, sems.at[len(copies)])
        copy.start()
        copies.append(copy)

    update = approx_of(lax.axis_index("dp"))
    first = beta_one * moment1[...] + (1.0 - beta_one) * update
    second = beta_two * moment2[...] + (1.0 - beta_two) * update * update
    updated[0] = first
    updated[1] = second
    updated[2] = weight[...] - learn_rate * (first / corr_one) / (jnp.sqrt(second / corr_two) + adam_eps)
    send(updated.at[0], new_moment1)
    send(updated.at[1], new_moment2)
    send(updated.at[2], new_weight)
    for chunk in range(chunks):
        approx = approx_of(chunk)
        field = lower if chunk < chunks // 2 else upper
        first = chunk % (chunks // 2) * count
        for block in range(count):
            columns = slice(block * LANES, (block + 1) * LANES)
            rounded[chunk, :, columns] = (field[first + block] - lanes(approx, block)).astype(BF16)
        send(rounded.at[chunk], new_error.at[:, chunk * width : (chunk + 1) * width])
    for copy in copies:
        copy.wait()


def call(kernel, outs, args, specs=None, out_specs=None, scratch=(), limit=16, flops=0, moved=0):
    return pl.pallas_call(
        kernel,
        out_shape=outs,
        in_specs=specs or [VMEM] * len(args),
        out_specs=out_specs or jax.tree.map(lambda _: VMEM, outs),
        scratch_shapes=scratch,
        compiler_params=pltpu.CompilerParams(vmem_limit_bytes=int(limit * MIB)),
        cost_estimate=pl.CostEstimate(flops=flops, bytes_accessed=moved, transcendentals=0),
    )(*args)


def swap(value, axis, level):
    return lax.ppermute(value, axis, list(enumerate(level)))


def total(value, axis, levels):
    for level in levels:
        value = value + swap(value, axis, level)
    return value


def shards(acts, grad_out, error_buffer, q_prev, weight, moment1, moment2):
    gt, et = grad_out.T, error_buffer.T
    rank, ff = q_prev.shape
    tokens, model = acts.shape[0], et.shape[1]
    chunks, width = 8, model // 8
    array = jax.ShapeDtypeStruct

    gathered = lax.all_gather(acts, "mp", axis=0)


    half = rank // 2
    blocks = array((NMP, half, LANES), F32)
    mine, send = call(
        error_kernel, [blocks, blocks], (q_prev, et), specs=[HBM] * 2,
        scratch=[
            pltpu.VMEM((rank, ff), F32), pltpu.VMEM((chunks, ff, width), BF16), pltpu.VMEM((NMP, rank, LANES), F32),
            pltpu.SemaphoreType.DMA((chunks + 1,)),
        ],
        limit=56, flops=6 * rank * ff * model, moved=2 * ff * model,
    )
    theirs = swap(send, "dp", ALONG_DP[0])
    factor = call(
        token_kernel, array((NX, QUARTER, 8, LANES), F32), (q_prev, gt), specs=[HBM] * 2,
        scratch=[pltpu.VMEM((rank, ff), F32), pltpu.VMEM((ff, tokens), BF16), pltpu.SemaphoreType.DMA((2,))],
        limit=16, flops=6 * rank * ff * tokens, moved=2 * ff * tokens,
    )
    tiles = lambda count: array((count, 8, LANES), F32)
    kept = lambda count: array((count, half, LANES), F32)
    sent, part, keep = call(
        open_kernel, [tiles(48), tiles(2 * QUARTER), kept(16)], (factor, mine, theirs), moved=MIB,
    )
    sent, late = lax.optimization_barrier((sent, acts))
    quarters = call(
        deal_kernel, [array((tokens // NX, LANES), BF16)] * NX, (late,), moved=MIB
    )
    across = [(x + 2) % NX * NZ + z for x in range(NX) for z in range(NZ)]
    ring = [quarters[0]] + [swap(rows, "mp", level) for rows, level in zip(quarters[1:], (*ALONG_X, across))]
    came = swap(sent, "mp", ALONG_X[1])
    sent, part, keep = call(narrow_kernel, [tiles(24), tiles(QUARTER), kept(8)], (part, keep, came), moved=MIB)
    came = swap(sent, "mp", ALONG_X[0])
    for count, level in zip((4, 2, 1), ALONG_Z[::-1]):
        sent, keep = call(halve_kernel, [tiles(QUARTER + 2 * count), kept(count)], (part, keep, came), moved=MIB)
        if count == 1:
            sent, ring = lax.optimization_barrier((sent, ring))
        part, came = sent, swap(sent, "mp", level)

    keep, send = call(
        piece_kernel, [kept(NX), kept(NX)], (sent, keep, came, *ring), moved=MIB,
    )
    keep = keep + swap(send, "dp", ALONG_DP[0])
    keep = total(total(keep, "mp", ALONG_X), "dp", ALONG_DP[1:])
    sent = call(
        start_kernel, array((QUARTER + 2, 8, LANES), F32), (keep, swap(keep, "dp", ALONG_DP[0]), *ring),
        moved=MIB,
    )
    for place, level in enumerate(ALONG_Z):
        came = swap(sent, "mp", level)
        sent = call(double_kernel, array((QUARTER + (4 << place), 8, LANES), F32), (sent, came), moved=MIB)
    sent = jnp.concatenate([sent, swap(sent, "mp", ALONG_X[0])])
    factor, mine = call(
        part_kernel, [array((FACTOR, 8, LANES), F32), array((2 * NMP, 8, LANES), F32)],
        (sent, swap(sent, "mp", ALONG_X[1])), moved=MIB,
    )
    basis, right = call(
        ortho_kernel, [array((NMP, 3 * rank, LANES), BF16), array((rank, ff), F32)],
        (mine, swap(mine, "dp", ALONG_DP[0]), factor, gt, et),
        specs=[VMEM] * 4 + [HBM],
        scratch=[
            pltpu.VMEM((NMP + 1, rank, LANES), F32),
            pltpu.VMEM((chunks, ff, width), BF16),
            pltpu.VMEM((NX, rank, tokens // NX), F32),
            pltpu.SemaphoreType.DMA((chunks,)),
        ],
        limit=24, flops=8 * rank * ff * model, moved=2 * ff * model,
    )
    right, gathered = lax.optimization_barrier((right, gathered))
    halves = []
    for part, level in enumerate(ALONG_DP[1:]):
        half = call(
            functools.partial(field_kernel, part * NMP // 2), array((NMP // 2, ff, LANES), F32), (gathered, et, gt),
            specs=[HBM] * 3,
            scratch=[
                pltpu.VMEM((NMP // 2, tokens, LANES), BF16),
                pltpu.VMEM((chunks // 2, ff, width), BF16),
                pltpu.VMEM((ff, tokens), BF16),
                pltpu.SemaphoreType.DMA((chunks // 2,)),
                pltpu.SemaphoreType.DMA((chunks // 2,)),
                pltpu.SemaphoreType.DMA,
            ],
            limit=48, flops=model * ff * tokens, moved=10 * MIB,
        )
        right, half = lax.optimization_barrier((total(right, "dp", [level]), half))
        halves.append(half)
    right = total(right, "dp", ALONG_DP[:1])

    block = array((ff, width), F32)
    outs = call(
        final_kernel,
        [block] * 3 + [array((ff, model), BF16), array((rank, ff), F32)],
        (right, basis, *halves, weight.T, moment1.T, moment2.T),
        specs=[VMEM] * 7,
        out_specs=[HBM] * 4 + [VMEM],
        scratch=[
            pltpu.VMEM((3, ff, width), F32),
            pltpu.VMEM((chunks, ff, width), BF16),
            pltpu.SemaphoreType.DMA((3 + chunks,)),
        ],
        limit=24, flops=12 * rank * model * ff, moved=20 * MIB,
    )
    new_weight, new_moment1, new_moment2, new_error, q_new = outs
    return (new_weight.T, new_moment1.T, new_moment2.T, new_error.T, q_new)


def solution(mesh):
    placed = (
        P("dp", "mp"),
        P("dp", "mp"),
        P("dp", "mp"),
        P(None, "mp"),
        P("dp", "mp"),
        P("dp", "mp"),
        P("dp", "mp"),
    )
    return jax.shard_map(
        shards,
        mesh=mesh,
        in_specs=placed,
        out_specs=(P("dp", "mp"), P("dp", "mp"), P("dp", "mp"), P("dp", "mp"), P(None, "mp")),
        check_vma=False,
    )
```
